256 devices in a mesh: frame: 4 (over y_hi, core), slab: 64 (over x, z, y_lo).
Axes of the slice: x: 4, y: 4 (y_hi: 2, y_lo: 2; y = y_hi * 2 + y_lo), z: 8, core: 2. Of those that a mesh axis runs over, the one named last changes fastest.
Arguments:
- latents: bfloat16 [4, 128, 128, 256], P('frame', 'slab'), may hold values from -6 to 6
- conv_weight: bfloat16 [2304, 256], replicated, may hold values from -0.125 to 0.125
- conv_bias: float32 [256], replicated, may hold values from -3 to 3
- out_weight: bfloat16 [3, 2304], replicated, may hold values from -0.125 to 0.125
- row_table: int32 [4, 224], P('frame'), may hold values from 0 to 255, as said below
- patch_weight: bfloat16 [588, 1280], replicated, may hold values from -0.25 to 0.25
- pos_embed: bfloat16 [256, 1280], replicated, may hold values from -3 to 3
- proj_weight: bfloat16 [1280, 1024], replicated, may hold values from -0.15625 to 0.15625
- text_embed: float32 [1024], replicated, may hold values from -6 to 6
Outputs:
- reward: float32 [4], P('frame')
- grad_conv: float32 [2304, 256], P('slab')
- grad_out: float32 [3, 2304], replicated
The draws below stay inside these ranges and needn't reach their ends.
Inputs may be any that keep to these rules, and one draw needn't show every extreme that they name: row_table[f, 0] = 0, each row of row_table never falls, row_table[f, 223] = min(255, 255), and every other row_table[f, i] is (i * 256) // 224 or one more, capped by the cummulative order.
All inputs are finite; a program needn't handle non-finite values.
Results may differ from the reference program's by a relative error of at most 0.0038.
Values may be sent and summed in bfloat16 or wider, within the bound.
A program may use at most 128 MiB of HBM per device.

```python
import jax
import jax.numpy as jnp
from jax import lax

C = 256
CW = 1280
EMB = 1024
IMG = 224
PATCH = 14
RL = 2
WL = 128
FRAMES = 4
H = 256
PATCHES = 256
N_SLAB = 64


def draw_row_table(key, part):
    key = jax.random.fold_in(key, 7)
    top = min((IMG - 1) * H // IMG + 1, H - 1)
    base = jnp.arange(IMG, dtype=jnp.int32) * H // IMG
    bits = jax.random.randint(key, (FRAMES, IMG), 0, 2).astype(jnp.int32)
    values = jnp.minimum(base[None, :] + bits, top)
    values = values.at[:, 0].set(0)
    values = values.at[:, IMG - 1].set(top)
    values = lax.cummax(values, axis=1)
    return values.astype(jnp.int32)


def level_of(key, extent, shards, low, top_value):
    def one(axis_at, blocks):
        draws = jax.random.uniform(jax.random.fold_in(jax.random.fold_in(key, 6), axis_at), (blocks,), jnp.float32, low / len(shards), top_value / len(shards))
        return jnp.repeat(jnp.exp(draws), extent[axis_at] // blocks).reshape((-1,) + (1,) * (len(extent) - axis_at - 1))

    level = one(*shards[0])
    for cut in shards[1:]:
        level = level * one(*cut)
    return level


def bell_draw(key, extent, deviation, most, pieces=(), kind=jnp.bfloat16):
    drawn = deviation * jax.random.normal(key, extent, jnp.float32)
    if pieces:
        drawn = drawn * level_of(key, extent, pieces, -0.22, 0.18)
    return jnp.clip(drawn, -most, most).astype(kind)


def setup_inputs(seed: int = 0) -> dict:
    key_list = jax.random.split(jax.random.key(seed), 10)
    latents = bell_draw(key_list[0], (FRAMES, RL * N_SLAB, WL, C), 1.0, 6.0, ((0, 4), (1, 64)))
    conv_weight = bell_draw(key_list[1], (9 * C, C), (9 * C) ** -0.5, 0.125)
    conv_bias = bell_draw(key_list[2], (C,), 0.5, 3.0, (), jnp.float32)
    out_weight = bell_draw(key_list[3], (3, 9 * C), (9 * C) ** -0.5, 0.125)
    row_table = draw_row_table(jax.random.fold_in(key_list[9], 71), 0)
    patch_weight = bell_draw(key_list[5], (3 * PATCH * PATCH, CW), (3 * PATCH * PATCH) ** -0.5, 0.25)
    pos_embed = bell_draw(key_list[6], (PATCHES, CW), 0.5, 3.0)
    proj_weight = bell_draw(key_list[7], (CW, EMB), CW ** -0.5, 0.15625)
    text_embed = bell_draw(key_list[8], (EMB,), 1.0, 6.0, (), jnp.float32)
    return dict(latents=latents, conv_weight=conv_weight, conv_bias=conv_bias, out_weight=out_weight, row_table=row_table, patch_weight=patch_weight, pos_embed=pos_embed, proj_weight=proj_weight, text_embed=text_embed)


loss_scale = 256.0
norm_eps = 1e-05

def layer_normed(values):
    centred = values - lax.optimization_barrier(jnp.mean(values, axis=-1, keepdims=True))
    return centred / jnp.sqrt(lax.optimization_barrier(jnp.mean(centred * centred, axis=-1, keepdims=True)) + norm_eps)

def clip_reward(crop_input, patch_weight, pos_embed, proj_weight, text_embed):
    grid_side = IMG // PATCH
    patches = crop_input.reshape(3, grid_side, PATCH, grid_side, PATCH).transpose(1, 3, 0, 2, 4)
    patches = patches.reshape(grid_side * grid_side, 3 * PATCH * PATCH)
    embedded = jnp.dot(patches, patch_weight.astype(jnp.float32), precision=lax.Precision.HIGHEST)
    embedded = embedded + pos_embed.astype(jnp.float32)
    pooled = lax.optimization_barrier(jnp.mean(layer_normed(embedded), axis=0))
    projected = jnp.dot(layer_normed(pooled), proj_weight.astype(jnp.float32), precision=lax.Precision.HIGHEST)
    numer = jnp.sum(projected * text_embed)
    return numer / jnp.sqrt((jnp.sum(projected * projected) + 1e-06) * (jnp.sum(text_embed * text_embed) + 1e-06))

def row_weights(table, height):
    lower = table.astype(jnp.int32)
    following = jnp.concatenate([lower[1:], jnp.full((1,), height, jnp.int32)])
    upper = jnp.maximum(following, lower + 1)
    rows = jnp.arange(height, dtype=jnp.int32)
    inside = (rows[None, :] >= lower[:, None]) & (rows[None, :] < upper[:, None])
    counts = (upper - lower).astype(jnp.float32)
    return jnp.where(inside, 1.0, 0.0).astype(jnp.float32) / counts[:, None]

def upsample(values):
    return jnp.repeat(jnp.repeat(values, 2, axis=0), 2, axis=1)

def pad_grid(values):
    return jnp.pad(values, ((1, 1), (1, 1), (0, 0)))

def conv_hidden(padded, weight, row_count, col_count):
    channels = padded.shape[-1]
    summed = jnp.zeros((row_count * col_count, weight.shape[1]), jnp.float32)
    for tap_index in range(9):
        row_shift, col_shift = (tap_index // 3, tap_index % 3)
        window = padded[row_shift:row_shift + row_count, col_shift:col_shift + col_count].reshape(row_count * col_count, channels)
        summed = summed + jnp.dot(window, weight[tap_index * channels:(tap_index + 1) * channels], preferred_element_type=jnp.float32)
    return summed

def conv_image(padded, weight, row_count, col_count):
    channels = padded.shape[-1]
    summed = jnp.zeros((3, row_count * col_count), jnp.float32)
    for tap_index in range(9):
        row_shift, col_shift = (tap_index // 3, tap_index % 3)
        window = padded[row_shift:row_shift + row_count, col_shift:col_shift + col_count].reshape(row_count * col_count, channels)
        summed = summed + lax.dot_general(weight[:, tap_index * channels:(tap_index + 1) * channels], window, (((1,), (1,)), ((), ())), preferred_element_type=jnp.float32)
    return summed

def image_grad_to_hidden(grad_pad, weight, row_count, col_count):
    channels = weight.shape[1] // 9
    summed = jnp.zeros((row_count * col_count, channels), jnp.float32)
    for tap_index in range(9):
        row_shift, col_shift = (tap_index // 3, tap_index % 3)
        window = grad_pad[:, 2 - row_shift:2 - row_shift + row_count, 2 - col_shift:2 - col_shift + col_count].reshape(3, row_count * col_count)
        summed = summed + lax.dot_general(window, weight[:, tap_index * channels:(tap_index + 1) * channels], (((0,), (0,)), ((), ())), preferred_element_type=jnp.float32)
    return summed

def kernel_grad(padded, conv_grad, row_count, col_count):
    channels = padded.shape[-1]
    blocks = []
    for tap_index in range(9):
        row_shift, col_shift = (tap_index // 3, tap_index % 3)
        window = padded[row_shift:row_shift + row_count, col_shift:col_shift + col_count].reshape(row_count * col_count, channels)
        blocks.append(lax.dot_general(window, conv_grad, (((0,), (0,)), ((), ())), preferred_element_type=jnp.float32))
    return jnp.concatenate(blocks, axis=0)

def out_kernel_grad(grad_flat, hidden_pad, row_count, col_count):
    channels = hidden_pad.shape[-1]
    blocks = []
    for tap_index in range(9):
        row_shift, col_shift = (tap_index // 3, tap_index % 3)
        window = hidden_pad[row_shift:row_shift + row_count, col_shift:col_shift + col_count].reshape(row_count * col_count, channels)
        blocks.append(jnp.dot(grad_flat, window, preferred_element_type=jnp.float32))
    return jnp.concatenate(blocks, axis=1)

def reference(latents, conv_weight, conv_bias, out_weight, row_table, patch_weight, pos_embed, proj_weight, text_embed):
    channels = latents.shape[-1]
    height = 2 * latents.shape[1]
    width_px = 2 * latents.shape[2]
    column_pick = (jnp.arange(IMG) * width_px // IMG).astype(jnp.int32)
    rewards = []
    kernel_total = jnp.zeros((9 * channels, channels), jnp.float32)
    out_total = jnp.zeros((3, 9 * channels), jnp.float32)
    for frame_index in range(latents.shape[0]):
        padded = pad_grid(upsample(latents[frame_index]))
        conv_sum = conv_hidden(padded, conv_weight, height, width_px) + conv_bias
        hidden = jax.nn.silu(conv_sum).astype(jnp.bfloat16).reshape(height, width_px, channels)
        hidden_pad = pad_grid(hidden)
        decoded = conv_image(hidden_pad, out_weight, height, width_px).astype(jnp.bfloat16).reshape(3, height, width_px)
        weights = row_weights(row_table[frame_index], height)
        picked = decoded[:, :, column_pick].astype(jnp.float32)
        crop = jnp.einsum('ih,chj->cij', weights, picked, precision=lax.Precision.HIGHEST)
        reward, pullback = jax.vjp(lambda crop_input: clip_reward(crop_input, patch_weight, pos_embed, proj_weight, text_embed), crop)
        crop_grad = pullback(jnp.float32(-loss_scale))[0]
        rows_grad = jnp.einsum('ih,cij->chj', weights, crop_grad, precision=lax.Precision.HIGHEST)
        image_grad = jnp.zeros((3, height, width_px), jnp.float32).at[:, :, column_pick].add(rows_grad)
        grad_rounded = image_grad.astype(jnp.bfloat16)
        grad_pad = jnp.pad(grad_rounded, ((0, 0), (1, 1), (1, 1)))
        hidden_grad = image_grad_to_hidden(grad_pad, out_weight, height, width_px)
        gate_value = jax.nn.sigmoid(conv_sum)
        conv_grad = (hidden_grad * gate_value * (1.0 + conv_sum * (1.0 - gate_value))).astype(jnp.bfloat16)
        kernel_total = kernel_total + kernel_grad(padded, conv_grad, height, width_px)
        out_total = out_total + out_kernel_grad(grad_rounded.reshape(3, height * width_px), hidden_pad, height, width_px)
        rewards.append(reward)
    return (jnp.stack(rewards).astype(jnp.float32), kernel_total, out_total)
```

```python
import jax
import jax.numpy as jnp
from jax import lax
from jax.experimental import pallas as pl
from jax.experimental.pallas import tpu as pltpu
from jax.sharding import PartitionSpec as P

MESH = pl.DeviceIdType.MESH
F32 = jnp.float32
BF16 = jnp.bfloat16

C = 256
CW = 1280
EMB = 1024
IMG = 224
PATCH = 14
WL = 128
N_SLAB = 64
GROUPS = 16
KP = 14 * 64
LOSS_SCALE = 256.0
EPS = 1e-05


def dot_nn(a, b):
    return lax.dot_general(a, b, (((1,), (0,)), ((), ())), preferred_element_type=F32)


def dot_nt(a, b):
    return lax.dot_general(a, b, (((1,), (1,)), ((), ())), preferred_element_type=F32)


def dot_tn(a, b):
    return lax.dot_general(a, b, (((0,), (0,)), ((), ())), preferred_element_type=F32)


def iota(shape, dim):
    return lax.broadcasted_iota(jnp.int32, shape, dim)


def split2(v):
    hi = v.astype(BF16)
    lo = (v - hi.astype(F32)).astype(BF16)
    return hi, lo


def lat_row(r6, a):
    return (r6 - 1 + a - 1) // 2 + 1


def patch_column(c14):
    c16 = c14 * 8 // 7
    return c16 % 2, c16 // 2


def kernel(
    lat_hbm, cw_hbm, bias_ref, ow_ref, table_ref, pw_hbm, pos_hbm, proj_hbm, text_ref,
    reward_ref, gconv_ref, gout_ref,
    lat4, wb, lcat, zbuf, hbuf, gate, wd32, wo32, pw, pwp, pos, proj,
    dec, dall, ct, gt, ybuf, psend, precv, igs, latt,
    g32, gbf, gcr, xbf, x32, xr, zbf, z32, zr, yb, yr,
    go2, gocr, goz, gozr, gox, goxr,
    loc_sem, halo_ss, halo_rs, gat_ss, gat_rs, pool_ss, pool_rs,
    c_ss, c_rs, x_ss, x_rs, z_ss, z_rs, y_ss, y_rs,
):
    f = lax.axis_index("frame")
    s = lax.axis_index("slab")
    y_hi, core = f // 2, f % 2
    x, z, y_lo = s // 16, (s % 16) // 2, s % 2
    p, q = s // 4, s % 4
    low_half = q < 2
    base = jnp.where(low_half, 4 * p - 4, 4 * p)
    p2 = jnp.where(low_half, p - 1, p + 1)
    p2c = jnp.clip(p2, 0, GROUPS - 1)

    loads = []

    def load(src, dst):
        copy = pltpu.make_async_copy(src, dst, loc_sem.at[len(loads)])
        copy.start()
        loads.append(copy)
        return copy

    lat_load = load(lat_hbm.at[0], lat4.at[pl.ds(1, 2)])
    w_loads = []
    for a in range(3):
        for b in range(3):
            t = 3 * a + b
            w_loads.append(
                load(cw_hbm.at[pl.ds(t * C, C)], wb.at[b, pl.ds(a * C, C)])
            )
    pw_load = load(pw_hbm, pw)
    pos_loads = [
        load(pos_hbm.at[pl.ds(pl.multiple_of(16 * p, 16), 16)], pos.at[pl.ds(0, 16)]),
        load(pos_hbm.at[pl.ds(pl.multiple_of(16 * p2c, 16), 16)], pos.at[pl.ds(16, 16)]),
    ]
    proj_load = load(proj_hbm, proj)

    dall[...] = jnp.zeros_like(dall)
    lat4[0] = jnp.zeros((WL, C), BF16)
    lat4[3] = jnp.zeros((WL, C), BF16)

    barrier = pltpu.get_barrier_semaphore()

    def greet(cond, fd, sd):
        def go():
            pl.semaphore_signal(barrier, inc=1, device_id=(fd, sd), device_id_type=MESH)

        if cond is None:
            go()
        else:
            pl.when(cond)(go)

    greet(s > 0, f, s - 1)
    greet(s < N_SLAB - 1, f, s + 1)
    for d in range(1, 4):
        greet(None, f, 4 * p + (q + d) % 4)
    for v in range(4):
        greet((q == 0) & (p > 0), f, 4 * p - 4 + v)
        greet((q == 3) & (p < GROUPS - 1), f, 4 * p + 4 + v)
    greet((q < 3) & (p < GROUPS - 1), f, 4 * p + 4)
    greet((q == 3) & (p < GROUPS - 2), f, 4 * p + 8)
    for d in range(1, GROUPS):
        greet(None, f, 4 * ((p + d) % GROUPS) + q)
    for d in range(1, 4):
        greet(None, f, ((x + d) % 4) * 16 + z * 2 + y_lo)
    for d in range(1, 8):
        greet(None, f, x * 16 + ((z + d) % 8) * 2 + y_lo)
    yc = y_hi * 4 + y_lo * 2 + core

    def yc_device(idx):
        return (idx // 4) * 2 + idx % 2, x * 16 + z * 2 + (idx // 2) % 2

    for d in range(1, 8):
        greet(None, *yc_device((yc + d) % 8))

    def one(cond):
        return jnp.where(cond, 1, 0)

    expected = (
        one(s > 0) + one(s < N_SLAB - 1)
        + 3 + one(p < GROUPS - 1) + one(p > 0)
        + one((q == 0) & (p > 0)) * 3 + one((q == 0) & (p > 1))
        + 15 + 3 + 7 + 7
    )

    wd32[...] = jnp.zeros_like(wd32)
    wo32[...] = jnp.zeros_like(wo32)
    for a in range(3):
        for b in range(3):
            t = 3 * a + b
            tap = ow_ref[:, t * C:(t + 1) * C].astype(F32)
            wo32[b * 16 + (2 - a) * 4:b * 16 + (2 - a) * 4 + 3, :] = tap
            for r in range(4):
                wd32[b * 16 + r * 4:b * 16 + r * 4 + 3, (r + a) * C:(r + a + 1) * C] = tap

    pl.semaphore_wait(barrier, expected)

    sends = []

    def remote(src, dst, ssem, rsem, fd, sd):
        return pltpu.make_async_remote_copy(
            src_ref=src, dst_ref=dst, send_sem=ssem, recv_sem=rsem,
            device_id=(fd, sd), device_id_type=MESH,
        )

    def guard(cond, action):
        if cond is None:
            action()
        else:
            pl.when(cond)(action)

    def send(cond, *what):
        copy = remote(*what)
        guard(cond, copy.start)
        sends.append((cond, copy))
        return copy

    up = send(s > 0, lat_hbm.at[0, 0], lat4.at[3], halo_ss.at[0], halo_rs.at[1], f, s - 1)
    down = send(
        s < N_SLAB - 1, lat_hbm.at[0, 1], lat4.at[0], halo_ss.at[1], halo_rs.at[0], f, s + 1
    )

    bias = bias_ref[...]
    first = iota((WL, C), 0) == 0
    last = iota((WL, C), 0) == WL - 1

    def conv_rows(rows):
        count = len(rows)
        for n, r6 in enumerate(rows):
            for a in range(3):
                lcat[n * WL:(n + 1) * WL, a * C:(a + 1) * C] = lat4[lat_row(r6, a)]
        for b in range(3):
            zbuf[b, 0:count * WL] = dot_nn(lcat[0:count * WL, :], wb[b])
        for n, r6 in enumerate(rows):
            here = slice(n * WL, (n + 1) * WL)
            z0, z1, z2 = zbuf[0, here], zbuf[1, here], zbuf[2, here]
            before = jnp.where(first, 0.0, pltpu.roll(z0, 1, 0))
            after = jnp.where(last, 0.0, pltpu.roll(z2, WL - 1, 0))
            for pc, total in ((0, before + z1 + z2), (1, z0 + z1 + after)):
                total = total + bias
                hidden = total / (1.0 + jnp.exp(-total))
                if r6 == 0:
                    hidden = jnp.where(s > 0, hidden, 0.0)
                elif r6 == 5:
                    hidden = jnp.where(s < N_SLAB - 1, hidden, 0.0)
                else:
                    gate[pc * WL:(pc + 1) * WL, (r6 - 1) * C:r6 * C] = total
                hbuf[pc * WL:(pc + 1) * WL, r6 * C:(r6 + 1) * C] = hidden.astype(BF16)

    lat_load.wait()
    for copy in w_loads:
        copy.wait()
    conv_rows([2, 3])

    guard(s < N_SLAB - 1, up.wait_recv)
    guard(s > 0, down.wait_recv)
    conv_rows([0, 1, 4, 5])

    res = dot_nt(wd32[...].astype(BF16), hbuf[...])
    even, odd = res[:, 0:WL], res[:, WL:2 * WL]
    left = iota((16, WL), 1) == 0
    right = iota((16, WL), 1) == WL - 1
    dec_even = jnp.where(left, 0.0, pltpu.roll(odd[0:16], 1, 1)) + even[16:32] + odd[32:48]
    dec_odd = even[0:16] + odd[16:32] + jnp.where(right, 0.0, pltpu.roll(even[32:48], WL - 1, 1))
    decoded = jnp.concatenate([dec_even, dec_odd], axis=1).astype(BF16)
    dec[...] = decoded
    dall[jnp.where(low_half, q + 4, q)] = decoded

    def gather_send(n, cond, target, slot):
        send(cond, dec, dall.at[slot], gat_ss.at[n], gat_rs.at[slot], f, target)

    for d in range(1, 4):
        qd = (q + d) % 4
        gather_send(d - 1, None, 4 * p + qd, jnp.where(qd < 2, q + 4, q))
    gather_send(3, p < GROUPS - 1, 4 * p + 4, q)
    gather_send(4, p > 0, 4 * p - 1, q + 4)
    gather_send(5, (q == 0) & (p > 0), 4 * p - 4, 8)
    gather_send(6, (q == 0) & (p > 0), 4 * p - 3, 8)
    gather_send(7, (q == 0) & (p > 0), 4 * p - 2, 4)
    gather_send(8, (q == 0) & (p > 1), 4 * p - 5, 8)

    rk = iota((128, 1), 0)
    g = rk & 63
    colour = one(g >= 14) + one(g >= 28)
    ig = jnp.where(rk < 64, p, p2) * PATCH + g - 14 * colour
    valid = (g < 42) & (ig >= 0) & (ig < IMG)
    table = table_ref[...].astype(F32)
    cols = iota((128, IMG), 1)
    lo = jnp.sum(jnp.where(cols == ig, table, 0.0), axis=1, keepdims=True)
    nxt = jnp.sum(jnp.where(cols == ig + 1, table, 0.0), axis=1, keepdims=True)
    nxt = nxt + jnp.where(ig == IMG - 1, 256.0, 0.0)
    hi = jnp.maximum(nxt, lo + 1.0)
    inv = 1.0 / (hi - lo)
    lane = iota((128, 144), 1)
    row = (4 * base + (lane >> 2)).astype(F32)
    inside = valid & ((lane & 3) == colour) & (row >= lo) & (row < hi)
    pick = jnp.where(inside, 1.0, 0.0).astype(BF16)
    lane = iota((128, 128), 1)
    row = (4 * s - 1 + (lane >> 2)).astype(F32)
    inside = valid & ((lane & 3) == colour) & (row >= lo) & (row < hi) & (lane < 24)
    both = jnp.where(lane == 32, inv, jnp.where(inside, 1.0, 0.0)).T
    back = both[0:32].astype(BF16)
    back = jnp.concatenate([back, back], axis=1)
    inv_row = both[32:33]

    pw_load.wait()
    prow = iota((KP, 588), 0)
    pg = prow & 63
    order = jnp.where(
        (pg < 42) & (iota((KP, 588), 1) == 14 * pg + 2 * (prow >> 7) + ((prow >> 6) & 1)), 1.0, 0.0
    ).astype(BF16)
    for n in range(CW // 256):
        cut = slice(n * 256, (n + 1) * 256)
        pwp[:, cut] = dot_nn(order, pw[:, cut]).astype(BF16)

    def gather_wait(slot, cond, source):
        copy = remote(dec, dall.at[slot], gat_ss.at[0], gat_rs.at[slot], f, source)
        pl.when(cond)(copy.wait_recv)

    more = p < GROUPS - 1
    for v in range(4):
        gather_wait(
            v, (low_half & (q == 0) & (p > 0)) | ((q >= 2) & (q != v)),
            jnp.where(low_half, 4 * p - 4 + v, 4 * p + v),
        )
        if v == 0:
            cond = (low_half & (q != v)) | ((q >= 2) & more)
        else:
            cond = (low_half & (q != v)) | ((q == 3) & more)
        gather_wait(v + 4, cond, jnp.where(low_half, 4 * p + v, 4 * p + 4 + v))
    gather_wait(
        8, (low_half & more) | ((q == 3) & (p < GROUPS - 2)),
        jnp.where(low_half, 4 * p + 4, 4 * p + 8),
    )

    crop = dot_nn(pick, dall[...].reshape(144, 256)) * inv
    ct[...] = crop.T
    lane16 = iota((16, 128), 1) < 64
    parts0, parts1 = [], []
    for n in range(7):
        pair = []
        for c14 in (2 * n, 2 * n + 1):
            pc, pj = patch_column(c14)
            pair.append(ct[pl.ds(pc * WL + pj, 16, stride=8), :])
        parts0.append(jnp.where(lane16, pair[0], pltpu.roll(pair[1], 64, 1)))
        parts1.append(jnp.where(lane16, pltpu.roll(pair[0], 64, 1), pair[1]))
    patches = jnp.concatenate(
        [jnp.concatenate(parts0, axis=1), jnp.concatenate(parts1, axis=1)], axis=0
    )
    for copy in pos_loads:
        copy.wait()
    emb = dot_nn(jnp.concatenate(split2(patches), axis=0), pwp[...])
    emb = emb[0:32] + emb[32:64] + pos[...].astype(F32)
    centred = emb - jnp.mean(emb, axis=1, keepdims=True)
    sigma = jnp.sqrt(jnp.mean(centred * centred, axis=1, keepdims=True) + EPS)
    normed = centred / sigma
    ybuf[...] = normed
    gsum = jnp.sum(normed[0:16], axis=0, keepdims=True)
    psend[...] = gsum
    precv[p] = gsum

    for d in range(1, GROUPS):
        send(
            None, psend, precv.at[p], pool_ss.at[d], pool_rs.at[p],
            f, 4 * ((p + d) % GROUPS) + q,
        )

    for n in range(4):
        cut = slice(n * C, (n + 1) * C)
        total = gate[:, cut]
        sig = 1.0 / (1.0 + jnp.exp(-total))
        gate[:, cut] = sig * (1.0 + total * (1.0 - sig))
    for n in range(4):
        latt[:, n * WL:(n + 1) * WL] = lat4[n].astype(F32).T.astype(BF16)
    text = text_ref[...]
    text2 = jnp.sum(text * text, axis=1, keepdims=True) + 1e-06
    gt[...] = jnp.zeros_like(gt)

    for d in range(1, GROUPS):
        pd = (p + d) % GROUPS
        remote(
            psend, precv.at[pd], pool_ss.at[d], pool_rs.at[pd], f, 4 * pd + q
        ).wait_recv()
    pooled = precv[0]
    for n in range(1, GROUPS):
        pooled = pooled + precv[n]
    pooled = pooled * (1.0 / 256.0)

    proj_load.wait()

    def two_rows(v):
        top = iota((16, v.shape[1]), 0)
        hi_part = v.astype(BF16).astype(F32)
        return jnp.where(top == 0, hi_part, jnp.where(top == 1, v - hi_part, 0.0)).astype(BF16)

    pc_ = pooled - jnp.mean(pooled, axis=1, keepdims=True)
    psigma = jnp.sqrt(jnp.mean(pc_ * pc_, axis=1, keepdims=True) + EPS)
    unit = pc_ / psigma
    projected = jnp.sum(dot_nn(two_rows(unit), proj[...]), axis=0, keepdims=True)
    numer = jnp.sum(projected * text, axis=1, keepdims=True)
    norm2 = jnp.sum(projected * projected, axis=1, keepdims=True) + 1e-06
    scale = 1.0 / jnp.sqrt(norm2 * text2)
    reward = numer * scale
    reward_ref[0] = reward[0, 0]
    dproj = -LOSS_SCALE * (text * scale - projected * (reward / norm2))
    dunit = jnp.sum(dot_nt(two_rows(dproj), proj[...]), axis=0, keepdims=True)

    def norm_back(dy, y, sg):
        m1 = jnp.mean(dy, axis=1, keepdims=True)
        m2 = jnp.mean(dy * y, axis=1, keepdims=True)
        return (dy - m1 - y * m2) / sg

    dpooled = norm_back(dunit, unit, psigma) * (1.0 / 256.0)
    demb = norm_back(dpooled, ybuf[...], sigma)
    dpat = dot_nt(jnp.concatenate(split2(demb), axis=0), pwp[...])
    dpat = dpat[0:32] + dpat[32:64]
    for n in range(7):
        d0 = dpat[0:16, n * 128:(n + 1) * 128]
        d1 = dpat[16:32, n * 128:(n + 1) * 128]
        pair = (
            jnp.where(lane16, d0, pltpu.roll(d1, 64, 1)),
            jnp.where(lane16, pltpu.roll(d0, 64, 1), d1),
        )
        for half in range(2):
            pc, pj = patch_column(2 * n + half)
            gt[pl.ds(pc * WL + pj, 16, stride=8), :] = pair[half]

    grows = jnp.concatenate(split2(gt[...] * inv_row), axis=1)
    image = dot_nt(back, grows).astype(BF16).astype(F32)
    even, odd = image[:, 0:WL], image[:, WL:2 * WL]
    left = iota((32, WL), 1) == 0
    right = iota((32, WL), 1) == WL - 1
    odd_before = jnp.where(left, 0.0, pltpu.roll(odd, 1, 1))
    even_after = jnp.where(right, 0.0, pltpu.roll(even, WL - 1, 1))
    igs[0] = jnp.concatenate([odd, even_after], axis=1)
    igs[1] = image
    igs[2] = jnp.concatenate([odd_before, even], axis=1)

    wout = wo32[...].astype(BF16)
    go = jnp.zeros((48, C), F32)
    cols_of = []
    for r in range(4):
        im = jnp.concatenate([igs[b, 4 * r:4 * r + 16, :] for b in range(3)], axis=0).astype(BF16)
        go = go + dot_nn(im, hbuf[:, (r + 1) * C:(r + 2) * C])
        cg = dot_tn(im, wout) * gate[:, r * C:(r + 1) * C]
        ev, od = cg[0:WL], cg[WL:2 * WL]
        od_before = jnp.where(first, 0.0, pltpu.roll(od, 1, 0))
        ev_after = jnp.where(last, 0.0, pltpu.roll(ev, WL - 1, 0))
        cols_of.append((od + ev_after, ev + od, od_before + ev))

    for b in range(3):
        for half in range(2):
            go2[half, b * 12:(b + 1) * 12, :] = go[b * 16:b * 16 + 12, half * 128:(half + 1) * 128]
    for half in range(2):
        go2[half, 36:40, :] = jnp.zeros((4, 128), F32)

    def put_grad(a, b, value):
        at = (3 * a + b) * C
        for half in range(2):
            part = value[:, half * 128:(half + 1) * 128]
            g32[half, at:at + C, :] = part
            gbf[half, at:at + C, :] = part.astype(BF16)

    for b in range(3):
        u0, u1, u2, u3 = (cols_of[r][b] for r in range(4))
        outer = jnp.concatenate([u0, u1 + u2, u3], axis=0).astype(BF16)
        inner = jnp.concatenate([u0 + u1, u2 + u3], axis=0).astype(BF16)
        put_grad(0, b, dot_nn(latt[:, 0:3 * WL], outer))
        put_grad(1, b, dot_nn(latt[:, WL:3 * WL], inner))
        put_grad(2, b, dot_nn(latt[:, WL:4 * WL], outer))

    fc = y_hi * 2 + 1 - core
    main = send(None, gbf.at[1 - core], gcr, c_ss.at[0], c_rs.at[0], fc, s)
    outk = send(None, go2.at[1 - core], gocr, c_ss.at[1], c_rs.at[1], fc, s)
    outk.wait_recv()
    gsum_z = go2[core] + gocr[...]
    goz[...] = gsum_z
    for d in range(1, 8):
        zd = (z + d) % 8
        send(
            None, goz, gozr.at[z], z_ss.at[0, d], z_rs.at[0, z], f, x * 16 + zd * 2 + y_lo
        )
    main.wait_recv()
    for n in range(4):
        cut = slice(n * 576, (n + 1) * 576)
        total = g32[core, cut, :] + gcr[cut, :].astype(F32)
        x32[n] = total
        xbf[n] = total.astype(BF16)

    for d in range(1, 4):
        xd = (x + d) % 4
        send(
            None, xbf.at[xd], xr.at[x], x_ss.at[0, d], x_rs.at[0, x], f, xd * 16 + z * 2 + y_lo
        )
    gozr[z] = gsum_z
    for d in range(1, 8):
        zd = (z + d) % 8
        remote(
            goz, gozr.at[zd], z_ss.at[0, d], z_rs.at[0, zd], f, x * 16 + zd * 2 + y_lo
        ).wait_recv()
    gsum_x = jnp.sum(gozr[...], axis=0)
    gox[...] = gsum_x
    xr[x] = jnp.zeros((576, 128), BF16)
    for d in range(1, 4):
        xd = (x + d) % 4
        remote(
            xbf.at[xd], xr.at[xd], x_ss.at[0, d], x_rs.at[0, xd], f, xd * 16 + z * 2 + y_lo
        ).wait_recv()
    for n in range(8):
        cut = slice(n * 72, (n + 1) * 72)
        total = x32[x, cut, :]
        for k in range(4):
            total = total + xr[k, cut, :].astype(F32)
        z32[n] = total
        zbf[n] = jnp.concatenate([total, jnp.zeros((8, 128), F32)], axis=0).astype(BF16)

    for d in range(1, 8):
        zd = (z + d) % 8
        send(
            None, zbf.at[zd], zr.at[z], z_ss.at[1, d], z_rs.at[1, z], f, x * 16 + zd * 2 + y_lo
        )
    for d in range(1, 4):
        xd = (x + d) % 4
        send(
            None, gox, goxr.at[x], x_ss.at[1, d], x_rs.at[1, x], f, xd * 16 + z * 2 + y_lo
        )
    goxr[x] = gsum_x
    zr[z] = jnp.zeros((80, 128), BF16)
    for d in range(1, 4):
        xd = (x + d) % 4
        remote(
            gox, goxr.at[xd], x_ss.at[1, d], x_rs.at[1, xd], f, xd * 16 + z * 2 + y_lo
        ).wait_recv()
    gsum_y = jnp.sum(goxr[...], axis=0)
    for d in range(1, 8):
        zd = (z + d) % 8
        remote(
            zbf.at[zd], zr.at[zd], z_ss.at[1, d], z_rs.at[1, zd], f, x * 16 + zd * 2 + y_lo
        ).wait_recv()
    total = z32[z]
    for n in range(8):
        total = total + zr[n, 0:72, :].astype(F32)

    for n in range(2):
        yb[n, 0:36, :] = total[36 * n:36 * n + 36]
        yb[n, 36:40, :] = jnp.zeros((4, 128), F32)
        yb[n, 40:80, :] = gsum_y
    for d in range(1, 8):
        yd = (yc + d) % 8
        send(
            None, yb.at[(yd // 2) % 2], yr.at[yc], y_ss.at[d], y_rs.at[yc], *yc_device(yd)
        )
    yr[yc] = yb[y_lo]
    for d in range(1, 8):
        yd = (yc + d) % 8
        remote(
            yb.at[0], yr.at[yd], y_ss.at[d], y_rs.at[yd], *yc_device(yd)
        ).wait_recv()
    for half in range(2):
        total = (yr[half] + yr[2 + half]) + (yr[4 + half] + yr[6 + half])
        cut = slice(half * 128, (half + 1) * 128)
        gconv_ref[:, cut] = total[0:36]
        for a in range(3):
            for b in range(3):
                at = 40 + b * 12 + (2 - a) * 4
                t = (3 * a + b) * C + half * 128
                gout_ref[:, t:t + 128] = total[at:at + 3]

    for cond, copy in sends:
        guard(cond, copy.wait_send)


def per_device(latents, conv_weight, conv_bias, out_weight, row_table, patch_weight, pos_embed,
               proj_weight, text_embed):
    vmem = pl.BlockSpec(memory_space=pltpu.VMEM)
    hbm = pl.BlockSpec(memory_space=pl.ANY)
    V = pltpu.VMEM
    dma = pltpu.SemaphoreType.DMA
    reward, gconv, gout = pl.pallas_call(
        kernel,
        out_shape=(
            jax.ShapeDtypeStruct((1,), F32),
            jax.ShapeDtypeStruct((36, C), F32),
            jax.ShapeDtypeStruct((3, 9 * C), F32),
        ),
        in_specs=[hbm, hbm, vmem, vmem, vmem, hbm, hbm, hbm, vmem],
        out_specs=(pl.BlockSpec(memory_space=pltpu.SMEM), vmem, vmem),
        scratch_shapes=[
            V((4, WL, C), BF16),
            V((3, 3 * C, C), BF16),
            V((4 * WL, 3 * C), BF16),
            V((3, 4 * WL, C), F32),
            V((2 * WL, 6 * C), BF16),
            V((2 * WL, 4 * C), F32),
            V((48, 6 * C), F32),
            V((48, C), F32),
            V((588, CW), BF16),
            V((KP, CW), BF16),
            V((32, CW), BF16),
            V((CW, EMB), BF16),
            V((16, 256), BF16),
            V((9, 16, 256), BF16),
            V((256, 128), F32),
            V((256, 128), F32),
            V((32, CW), F32),
            V((1, CW), F32),
            V((GROUPS, 1, CW), F32),
            V((3, 32, 256), F32),
            V((C, 4 * WL), BF16),
            V((2, 9 * C, 128), F32),
            V((2, 9 * C, 128), BF16),
            V((9 * C, 128), BF16),
            V((4, 576, 128), BF16),
            V((4, 576, 128), F32),
            V((4, 576, 128), BF16),
            V((8, 80, 128), BF16),
            V((8, 72, 128), F32),
            V((8, 80, 128), BF16),
            V((2, 80, 128), F32),
            V((8, 80, 128), F32),
            V((2, 40, 128), F32),
            V((40, 128), F32),
            V((40, 128), F32),
            V((8, 40, 128), F32),
            V((40, 128), F32),
            V((4, 40, 128), F32),
            dma((14,)), dma((2,)), dma((2,)), dma((9,)), dma((9,)), dma((16,)), dma((16,)),
            dma((2,)), dma((2,)), dma((2, 4)), dma((2, 4)), dma((2, 8)), dma((2, 8)),
            dma((8,)), dma((8,)),
        ],
        compiler_params=pltpu.CompilerParams(
            collective_id=0, has_side_effects=True, vmem_limit_bytes=50 * 1024 * 1024
        ),
    )(
        latents, conv_weight, conv_bias.reshape(1, C), out_weight, row_table, patch_weight,
        pos_embed, proj_weight, text_embed.reshape(1, EMB),
    )
    return reward, gconv, gout


def solution(mesh):
    return jax.shard_map(
        per_device,
        mesh=mesh,
        in_specs=(
            P("frame", "slab", None, None), P(), P(), P(), P("frame", None), P(), P(), P(), P(),
        ),
        out_specs=(P("frame"), P("slab", None), P()),
        check_vma=False,
    )
```

```python
import jax
import jax.numpy as jnp
from jax import lax
from jax.experimental import pallas as pl
from jax.experimental.pallas import tpu as pltpu
from jax.sharding import PartitionSpec as P

MESH = pl.DeviceIdType.MESH
F32 = jnp.float32
BF16 = jnp.bfloat16

C = 256
CW = 1280
EMB = 1024
IMG = 224
PATCH = 14
WL = 128
N_SLAB = 64
GROUPS = 16
KP = 14 * 64
LOSS_SCALE = 256.0
EPS = 1e-05


def dot_nn(a, b):
    return lax.dot_general(a, b, (((1,), (0,)), ((), ())), preferred_element_type=F32)


def dot_nt(a, b):
    return lax.dot_general(a, b, (((1,), (1,)), ((), ())), preferred_element_type=F32)


def dot_tn(a, b):
    return lax.dot_general(a, b, (((0,), (0,)), ((), ())), preferred_element_type=F32)


def iota(shape, dim):
    return lax.broadcasted_iota(jnp.int32, shape, dim)


def split2(v):
    hi = v.astype(BF16)
    lo = (v - hi.astype(F32)).astype(BF16)
    return hi, lo


def lat_row(r6, a):
    return (r6 - 1 + a - 1) // 2 + 1


def patch_column(c14):
    c16 = c14 * 8 // 7
    return c16 % 2, c16 // 2


def kernel(
    lat_hbm, cw_hbm, bias_hbm, ow_hbm, table_hbm, pw_hbm, pos_hbm, proj_hbm, text_hbm,
    reward_ref, gconv_ref, gout_ref,
    bias_ref, ow_ref, table_ref, text_ref,
    lat4, wb, lcat, zbuf, hbuf, gate, wd32, wo32, pw, pwp, pos, proj,
    dec, dall, ct, gt, ybuf, psend, precv, igs, latt,
    g32, gbf, gcr, xbf, x32, xr, zbf, z32, zr, yb, yr,
    go2, gocr, goz, gozr, gox, goxr, goy, goyr,
    loc_sem, halo_ss, halo_rs, gat_ss, gat_rs, pool_ss, pool_rs,
    c_ss, c_rs, x_ss, x_rs, z_ss, z_rs, y_ss, y_rs,
):
    f = lax.axis_index("frame")
    s = lax.axis_index("slab")
    y_hi, core = f // 2, f % 2
    x, z, y_lo = s // 16, (s % 16) // 2, s % 2
    p, q = s // 4, s % 4
    low_half = q < 2
    base = jnp.where(low_half, 4 * p - 4, 4 * p)
    p2 = jnp.where(low_half, p - 1, p + 1)
    p2c = jnp.clip(p2, 0, GROUPS - 1)

    dall[...] = jnp.zeros_like(dall)
    lat4[0] = jnp.zeros((WL, C), BF16)
    lat4[3] = jnp.zeros((WL, C), BF16)

    barrier = pltpu.get_barrier_semaphore()

    def greet(cond, fd, sd):
        def go():
            pl.semaphore_signal(barrier, inc=1, device_id=(fd, sd), device_id_type=MESH)

        if cond is None:
            go()
        else:
            pl.when(cond)(go)

    greet(s > 0, f, s - 1)
    greet(s < N_SLAB - 1, f, s + 1)
    for d in range(1, 4):
        greet(None, f, 4 * p + (q + d) % 4)
    for v in range(4):
        greet((q == 0) & (p > 0), f, 4 * p - 4 + v)
        greet((q == 3) & (p < GROUPS - 1), f, 4 * p + 4 + v)
    greet((q < 3) & (p < GROUPS - 1), f, 4 * p + 4)
    greet((q == 3) & (p < GROUPS - 2), f, 4 * p + 8)
    for d in range(1, GROUPS):
        greet(None, f, 4 * ((p + d) % GROUPS) + q)
    for d in range(1, 4):
        greet(None, f, ((x + d) % 4) * 16 + z * 2 + y_lo)
    for d in range(1, 8):
        greet(None, f, x * 16 + ((z + d) % 8) * 2 + y_lo)
    yc = y_hi * 4 + y_lo * 2 + core

    def yc_device(idx):
        return (idx // 4) * 2 + idx % 2, x * 16 + z * 2 + (idx // 2) % 2

    for d in range(1, 8):
        greet(None, *yc_device((yc + d) % 8))
    y = y_hi * 2 + y_lo
    own_pair = x // 2 == y_hi

    def last_source(slot):
        if slot < 4:
            return (slot // 2) * 2, x * 16 + z * 2 + slot % 2
        return (x // 2) * 2 + 1, (slot - 4) * 16 + z * 2 + y_lo

    for slot in range(4, 8):
        greet((core == 0) | (y_hi != x // 2) | (x != slot - 4), *last_source(slot))

    def one(cond):
        return jnp.where(cond, 1, 0)

    expected = (
        one(s > 0) + one(s < N_SLAB - 1)
        + 3 + one(p < GROUPS - 1) + one(p > 0)
        + one((q == 0) & (p > 0)) * 3 + one((q == 0) & (p > 1))
        + 15 + 3 + 7 + 7 + jnp.where(core == 0, 0, jnp.where(own_pair, 7, 8))
    )

    loads = []

    def load(src, dst):
        copy = pltpu.make_async_copy(src, dst, loc_sem.at[len(loads)])
        copy.start()
        loads.append(copy)
        return copy

    lat_load = load(lat_hbm.at[0], lat4.at[pl.ds(1, 2)])
    ow_load = load(ow_hbm, ow_ref)
    bias_load = load(bias_hbm, bias_ref)
    table_load = load(table_hbm, table_ref)
    text_load = load(text_hbm, text_ref)
    w_loads = []
    for a in range(3):
        for b in range(3):
            t = 3 * a + b
            w_loads.append(
                load(cw_hbm.at[pl.ds(t * C, C)], wb.at[b, pl.ds(a * C, C)])
            )
    pw_load = load(pw_hbm, pw)
    pos_loads = [
        load(pos_hbm.at[pl.ds(pl.multiple_of(16 * p, 16), 16)], pos.at[pl.ds(0, 16)]),
        load(pos_hbm.at[pl.ds(pl.multiple_of(16 * p2c, 16), 16)], pos.at[pl.ds(16, 16)]),
    ]
    proj_load = load(proj_hbm, proj)

    pl.semaphore_wait(barrier, expected)

    sends = []

    def remote(src, dst, ssem, rsem, fd, sd):
        return pltpu.make_async_remote_copy(
            src_ref=src, dst_ref=dst, send_sem=ssem, recv_sem=rsem,
            device_id=(fd, sd), device_id_type=MESH,
        )

    def guard(cond, action):
        if cond is None:
            action()
        else:
            pl.when(cond)(action)

    def send(cond, *what):
        copy = remote(*what)
        guard(cond, copy.start)
        sends.append((cond, copy))
        return copy

    up = send(s > 0, lat_hbm.at[0, 0], lat4.at[3], halo_ss.at[0], halo_rs.at[1], f, s - 1)
    down = send(
        s < N_SLAB - 1, lat_hbm.at[0, 1], lat4.at[0], halo_ss.at[1], halo_rs.at[0], f, s + 1
    )

    wd32[...] = jnp.zeros_like(wd32)
    wo32[...] = jnp.zeros_like(wo32)
    ow_load.wait()
    for a in range(3):
        for b in range(3):
            t = 3 * a + b
            tap = ow_ref[:, t * C:(t + 1) * C].astype(F32)
            wo32[b * 16 + (2 - a) * 4:b * 16 + (2 - a) * 4 + 3, :] = tap
            for r in range(4):
                wd32[b * 16 + r * 4:b * 16 + r * 4 + 3, (r + a) * C:(r + a + 1) * C] = tap

    bias_load.wait()
    bias = bias_ref[...]
    first = iota((WL, C), 0) == 0
    last = iota((WL, C), 0) == WL - 1

    def conv_rows(rows):
        count = len(rows)
        for n, r6 in enumerate(rows):
            for a in range(3):
                lcat[n * WL:(n + 1) * WL, a * C:(a + 1) * C] = lat4[lat_row(r6, a)]
        for b in range(3):
            zbuf[b, 0:count * WL] = dot_nn(lcat[0:count * WL, :], wb[b])
        for n, r6 in enumerate(rows):
            here = slice(n * WL, (n + 1) * WL)
            z0, z1, z2 = zbuf[0, here], zbuf[1, here], zbuf[2, here]
            before = jnp.where(first, 0.0, pltpu.roll(z0, 1, 0))
            after = jnp.where(last, 0.0, pltpu.roll(z2, WL - 1, 0))
            for pc, total in ((0, before + z1 + z2), (1, z0 + z1 + after)):
                total = total + bias
                hidden = total / (1.0 + jnp.exp(-total))
                if r6 == 0:
                    hidden = jnp.where(s > 0, hidden, 0.0)
                elif r6 == 5:
                    hidden = jnp.where(s < N_SLAB - 1, hidden, 0.0)
                else:
                    gate[pc * WL:(pc + 1) * WL, (r6 - 1) * C:r6 * C] = total
                hbuf[pc * WL:(pc + 1) * WL, r6 * C:(r6 + 1) * C] = hidden.astype(BF16)

    lat_load.wait()
    for copy in w_loads:
        copy.wait()
    conv_rows([2, 3])

    guard(s < N_SLAB - 1, up.wait_recv)
    guard(s > 0, down.wait_recv)
    conv_rows([0, 1, 4, 5])

    res = dot_nt(wd32[...].astype(BF16), hbuf[...])
    even, odd = res[:, 0:WL], res[:, WL:2 * WL]
    left = iota((16, WL), 1) == 0
    right = iota((16, WL), 1) == WL - 1
    dec_even = jnp.where(left, 0.0, pltpu.roll(odd[0:16], 1, 1)) + even[16:32] + odd[32:48]
    dec_odd = even[0:16] + odd[16:32] + jnp.where(right, 0.0, pltpu.roll(even[32:48], WL - 1, 1))
    decoded = jnp.concatenate([dec_even, dec_odd], axis=1).astype(BF16)
    dec[...] = decoded
    dall[jnp.where(low_half, q + 4, q)] = decoded

    def gather_send(n, cond, target, slot):
        send(cond, dec, dall.at[slot], gat_ss.at[n], gat_rs.at[slot], f, target)

    for d in range(1, 4):
        qd = (q + d) % 4
        gather_send(d - 1, None, 4 * p + qd, jnp.where(qd < 2, q + 4, q))
    gather_send(3, p < GROUPS - 1, 4 * p + 4, q)
    gather_send(4, p > 0, 4 * p - 1, q + 4)
    gather_send(5, (q == 0) & (p > 0), 4 * p - 4, 8)
    gather_send(6, (q == 0) & (p > 0), 4 * p - 3, 8)
    gather_send(7, (q == 0) & (p > 0), 4 * p - 2, 4)
    gather_send(8, (q == 0) & (p > 1), 4 * p - 5, 8)

    rk = iota((128, 1), 0)
    g = rk & 63
    colour = one(g >= 14) + one(g >= 28)
    ig = jnp.where(rk < 64, p, p2) * PATCH + g - 14 * colour
    valid = (g < 42) & (ig >= 0) & (ig < IMG)
    table_load.wait()
    table = table_ref[...].astype(F32)
    cols = iota((128, IMG), 1)
    lo = jnp.sum(jnp.where(cols == ig, table, 0.0), axis=1, keepdims=True)
    nxt = jnp.sum(jnp.where(cols == ig + 1, table, 0.0), axis=1, keepdims=True)
    nxt = nxt + jnp.where(ig == IMG - 1, 256.0, 0.0)
    hi = jnp.maximum(nxt, lo + 1.0)
    inv = 1.0 / (hi - lo)
    lane = iota((128, 144), 1)
    row = (4 * base + (lane >> 2)).astype(F32)
    inside = valid & ((lane & 3) == colour) & (row >= lo) & (row < hi)
    pick = jnp.where(inside, 1.0, 0.0).astype(BF16)
    lane = iota((128, 128), 1)
    row = (4 * s - 1 + (lane >> 2)).astype(F32)
    inside = valid & ((lane & 3) == colour) & (row >= lo) & (row < hi) & (lane < 24)
    both = jnp.where(lane == 32, inv, jnp.where(inside, 1.0, 0.0)).T
    back = both[0:32].astype(BF16)
    back = jnp.concatenate([back, back], axis=1)
    inv_row = both[32:33]

    pw_load.wait()
    prow = iota((KP, 588), 0)
    pg = prow & 63
    order = jnp.where(
        (pg < 42) & (iota((KP, 588), 1) == 14 * pg + 2 * (prow >> 7) + ((prow >> 6) & 1)), 1.0, 0.0
    ).astype(BF16)
    for n in range(CW // 256):
        cut = slice(n * 256, (n + 1) * 256)
        pwp[:, cut] = dot_nn(order, pw[:, cut]).astype(BF16)

    def gather_wait(slot, cond, source):
        copy = remote(dec, dall.at[slot], gat_ss.at[0], gat_rs.at[slot], f, source)
        pl.when(cond)(copy.wait_recv)

    more = p < GROUPS - 1
    for v in range(4):
        gather_wait(
            v, (low_half & (q == 0) & (p > 0)) | ((q >= 2) & (q != v)),
            jnp.where(low_half, 4 * p - 4 + v, 4 * p + v),
        )
        if v == 0:
            cond = (low_half & (q != v)) | ((q >= 2) & more)
        else:
            cond = (low_half & (q != v)) | ((q == 3) & more)
        gather_wait(v + 4, cond, jnp.where(low_half, 4 * p + v, 4 * p + 4 + v))
    gather_wait(
        8, (low_half & more) | ((q == 3) & (p < GROUPS - 2)),
        jnp.where(low_half, 4 * p + 4, 4 * p + 8),
    )

    crop = dot_nn(pick, dall[...].reshape(144, 256)) * inv
    ct[...] = crop.T
    lane16 = iota((16, 128), 1) < 64
    parts0, parts1 = [], []
    for n in range(7):
        pair = []
        for c14 in (2 * n, 2 * n + 1):
            pc, pj = patch_column(c14)
            pair.append(ct[pl.ds(pc * WL + pj, 16, stride=8), :])
        parts0.append(jnp.where(lane16, pair[0], pltpu.roll(pair[1], 64, 1)))
        parts1.append(jnp.where(lane16, pltpu.roll(pair[0], 64, 1), pair[1]))
    patches = jnp.concatenate(
        [jnp.concatenate(parts0, axis=1), jnp.concatenate(parts1, axis=1)], axis=0
    )
    for copy in pos_loads:
        copy.wait()
    emb = dot_nn(jnp.concatenate(split2(patches), axis=0), pwp[...])
    emb = emb[0:32] + emb[32:64] + pos[...].astype(F32)
    centred = emb - jnp.mean(emb, axis=1, keepdims=True)
    sigma = jnp.sqrt(jnp.mean(centred * centred, axis=1, keepdims=True) + EPS)
    normed = centred / sigma
    ybuf[...] = normed
    gsum = jnp.sum(normed[0:16], axis=0, keepdims=True)
    psend[...] = gsum
    precv[p] = gsum

    for d in range(1, GROUPS):
        send(
            None, psend, precv.at[p], pool_ss.at[d], pool_rs.at[p],
            f, 4 * ((p + d) % GROUPS) + q,
        )

    for n in range(4):
        cut = slice(n * C, (n + 1) * C)
        total = gate[:, cut]
        sig = 1.0 / (1.0 + jnp.exp(-total))
        gate[:, cut] = sig * (1.0 + total * (1.0 - sig))
    for n in range(4):
        latt[:, n * WL:(n + 1) * WL] = lat4[n].astype(F32).T.astype(BF16)
    text_load.wait()
    text = text_ref[...]
    text2 = jnp.sum(text * text, axis=1, keepdims=True) + 1e-06
    gt[...] = jnp.zeros_like(gt)

    for d in range(1, GROUPS):
        pd = (p + d) % GROUPS
        remote(
            psend, precv.at[pd], pool_ss.at[d], pool_rs.at[pd], f, 4 * pd + q
        ).wait_recv()
    pooled = precv[0]
    for n in range(1, GROUPS):
        pooled = pooled + precv[n]
    pooled = pooled * (1.0 / 256.0)

    proj_load.wait()

    def two_rows(v):
        top = iota((16, v.shape[1]), 0)
        hi_part = v.astype(BF16).astype(F32)
        return jnp.where(top == 0, hi_part, jnp.where(top == 1, v - hi_part, 0.0)).astype(BF16)

    pc_ = pooled - jnp.mean(pooled, axis=1, keepdims=True)
    psigma = jnp.sqrt(jnp.mean(pc_ * pc_, axis=1, keepdims=True) + EPS)
    unit = pc_ / psigma
    projected = jnp.sum(dot_nn(two_rows(unit), proj[...]), axis=0, keepdims=True)
    numer = jnp.sum(projected * text, axis=1, keepdims=True)
    norm2 = jnp.sum(projected * projected, axis=1, keepdims=True) + 1e-06
    scale = 1.0 / jnp.sqrt(norm2 * text2)
    reward = numer * scale
    reward_ref[0] = reward[0, 0]
    dproj = -LOSS_SCALE * (text * scale - projected * (reward / norm2))
    dunit = jnp.sum(dot_nt(two_rows(dproj), proj[...]), axis=0, keepdims=True)

    def norm_back(dy, y, sg):
        m1 = jnp.mean(dy, axis=1, keepdims=True)
        m2 = jnp.mean(dy * y, axis=1, keepdims=True)
        return (dy - m1 - y * m2) / sg

    dpooled = norm_back(dunit, unit, psigma) * (1.0 / 256.0)
    demb = norm_back(dpooled, ybuf[...], sigma)
    dpat = dot_nt(jnp.concatenate(split2(demb), axis=0), pwp[...])
    dpat = dpat[0:32] + dpat[32:64]
    for n in range(7):
        d0 = dpat[0:16, n * 128:(n + 1) * 128]
        d1 = dpat[16:32, n * 128:(n + 1) * 128]
        pair = (
            jnp.where(lane16, d0, pltpu.roll(d1, 64, 1)),
            jnp.where(lane16, pltpu.roll(d0, 64, 1), d1),
        )
        for half in range(2):
            pc, pj = patch_column(2 * n + half)
            gt[pl.ds(pc * WL + pj, 16, stride=8), :] = pair[half]

    grows = jnp.concatenate(split2(gt[...] * inv_row), axis=1)
    image = dot_nt(back, grows).astype(BF16).astype(F32)
    even, odd = image[:, 0:WL], image[:, WL:2 * WL]
    left = iota((32, WL), 1) == 0
    right = iota((32, WL), 1) == WL - 1
    odd_before = jnp.where(left, 0.0, pltpu.roll(odd, 1, 1))
    even_after = jnp.where(right, 0.0, pltpu.roll(even, WL - 1, 1))
    igs[0] = jnp.concatenate([odd, even_after], axis=1)
    igs[1] = image
    igs[2] = jnp.concatenate([odd_before, even], axis=1)

    ims = []
    go = jnp.zeros((48, C), F32)
    for r in range(4):
        im = jnp.concatenate([igs[b, 4 * r:4 * r + 16, :] for b in range(3)], axis=0).astype(BF16)
        ims.append(im)
        go = go + dot_nn(im, hbuf[:, (r + 1) * C:(r + 2) * C])
    for b in range(3):
        for half in range(2):
            go2[half, b * 12:(b + 1) * 12, :] = go[b * 16:b * 16 + 12, half * 128:(half + 1) * 128]
    for half in range(2):
        go2[half, 36:40, :] = jnp.zeros((4, 128), F32)
    fc = y_hi * 2 + 1 - core
    outk = send(None, go2.at[1 - core], gocr, c_ss.at[3], c_rs.at[3], fc, s)

    wout = wo32[...].astype(BF16)
    cols_of = []
    for r in range(4):
        cg = dot_tn(ims[r], wout) * gate[:, r * C:(r + 1) * C]
        ev, od = cg[0:WL], cg[WL:2 * WL]
        od_before = jnp.where(first, 0.0, pltpu.roll(od, 1, 0))
        ev_after = jnp.where(last, 0.0, pltpu.roll(ev, WL - 1, 0))
        cols_of.append((od + ev_after, ev + od, od_before + ev))

    def put_grad(a, b, value):
        at = (3 * a + b) * C
        for half in range(2):
            part = value[:, half * 128:(half + 1) * 128]
            g32[half, at:at + C, :] = part
            gbf[half, at:at + C, :] = part.astype(BF16)

    outer = [
        jnp.concatenate([cols_of[0][b], cols_of[1][b] + cols_of[2][b], cols_of[3][b]], axis=0)
        .astype(BF16) for b in range(3)
    ]
    inner = [
        jnp.concatenate([cols_of[0][b] + cols_of[1][b], cols_of[2][b] + cols_of[3][b]], axis=0)
        .astype(BF16) for b in range(3)
    ]
    main = []
    for a, start, stop, terms in ((0, 0, 3, outer), (1, 1, 3, inner), (2, 1, 4, outer)):
        for b in range(3):
            put_grad(a, b, dot_nn(latt[:, start * WL:stop * WL], terms[b]))
        rows = pl.ds(a * 768, 768)
        main.append(
            send(None, gbf.at[1 - core, rows], gcr.at[rows], c_ss.at[a], c_rs.at[a], fc, s)
        )
    outk.wait_recv()
    gsum_z = go2[core] + gocr[...]
    goz[...] = gsum_z
    for d in range(1, 8):
        zd = (z + d) % 8
        send(
            None, goz, gozr.at[z], z_ss.at[0, d], z_rs.at[0, z], f, x * 16 + zd * 2 + y_lo
        )

    mine = jnp.where(core == 0, x, y)

    def quarter_device(n):
        fd = jnp.where(core == 0, f, (n // 2) * 2 + 1)
        sd = jnp.where(core == 0, n * 16 + z * 2 + y_lo, x * 16 + z * 2 + n % 2)
        return fd, sd

    def halves_sum(half, start, count):
        return g32[half, start:start + count, :] + gcr[start:start + count, :].astype(F32)

    for part in range(2):
        if part == 0:
            main[0].wait_recv()
            main[1].wait_recv()
        else:
            main[2].wait_recv()

        @pl.when(core == 0)
        def along_x():
            for n in (2 * part, 2 * part + 1):
                total = halves_sum(0, n * 576, 576)
                x32[n] = total
                xbf[n] = total.astype(BF16)

        @pl.when(core == 1)
        def along_y():
            for two in range(4):
                units = [
                    halves_sum(1, (2 * part + h) * 576 + (2 * two + k) * 72, 72)
                    for k in range(2) for h in range(2)
                ]
                for n in range(2):
                    total = jnp.concatenate([u[36 * n:36 * n + 36] for u in units], axis=0)
                    x32[2 * part + n, two * 144:(two + 1) * 144, :] = total
                    xbf[2 * part + n, two * 144:(two + 1) * 144, :] = total.astype(BF16)

        for n in (2 * part, 2 * part + 1):
            send(
                mine != n, xbf.at[n], xr.at[mine], x_ss.at[0, n], x_rs.at[0, mine],
                *quarter_device(n),
            )

    xr[mine] = jnp.zeros((576, 128), BF16)
    gozr[z] = gsum_z
    for d in range(1, 8):
        zd = (z + d) % 8
        remote(
            goz, gozr.at[zd], z_ss.at[0, d], z_rs.at[0, zd], f, x * 16 + zd * 2 + y_lo
        ).wait_recv()
    gsum_x = jnp.sum(gozr[...], axis=0)
    gox[...] = gsum_x
    for d in range(1, 4):
        xd = (x + d) % 4
        send(
            None, gox, goxr.at[x], x_ss.at[1, d], x_rs.at[1, x], f, xd * 16 + z * 2 + y_lo
        )
    for n in range(4):
        copy = remote(xbf.at[n], xr.at[n], x_ss.at[0, n], x_rs.at[0, n], *quarter_device(n))
        guard(mine != n, copy.wait_recv)
    for n in range(8):
        cut = slice(n * 72, (n + 1) * 72)
        total = x32[mine, cut, :]
        for k in range(4):
            total = total + xr[k, cut, :].astype(F32)
        z32[n] = total
        zbf[n] = jnp.concatenate([total, jnp.zeros((8, 128), F32)], axis=0).astype(BF16)

    for d in range(1, 8):
        zd = (z + d) % 8
        send(
            None, zbf.at[zd], zr.at[z], z_ss.at[1, d], z_rs.at[1, z], f, x * 16 + zd * 2 + y_lo
        )
    goxr[x] = gsum_x
    zr[z] = jnp.zeros((80, 128), BF16)
    for d in range(1, 4):
        xd = (x + d) % 4
        remote(
            gox, goxr.at[xd], x_ss.at[1, d], x_rs.at[1, xd], f, xd * 16 + z * 2 + y_lo
        ).wait_recv()
    gsum_y = jnp.sum(goxr[...], axis=0)
    goy[...] = gsum_y
    for d in range(1, 8):
        yd = (yc + d) % 8
        send(None, goy, goyr.at[yc], y_ss.at[0, d], y_rs.at[0, yc], *yc_device(yd))
    goyr[yc] = gsum_y
    for d in range(1, 8):
        zd = (z + d) % 8
        remote(
            zbf.at[zd], zr.at[zd], z_ss.at[1, d], z_rs.at[1, zd], f, x * 16 + zd * 2 + y_lo
        ).wait_recv()
    total = z32[z]
    for n in range(8):
        total = total + zr[n, 0:72, :].astype(F32)

    for n in range(2):
        yb[n, 0:36, :] = total[36 * n:36 * n + 36]
        yb[n, 36:40, :] = jnp.zeros((4, 128), F32)
    slot = jnp.where(core == 0, y, 4 + x)
    for n in range(2):
        sd = jnp.where(core == 0, x * 16 + z * 2 + n, (2 * y_hi + n) * 16 + z * 2 + y_lo)
        here = sd == s

        @pl.when(here)
        def keep():
            yr[slot] = yb[n]

        for j in range(4):
            send(
                jnp.logical_not(here & (f == j)), yb.at[n], yr.at[slot],
                y_ss.at[1, 4 * n + j], y_rs.at[1, slot], j, sd,
            )

    for d in range(1, 8):
        yd = (yc + d) % 8
        remote(
            goy, goyr.at[yd], y_ss.at[0, d], y_rs.at[0, yd], *yc_device(yd)
        ).wait_recv()
    for half in range(2):
        total = (goyr[half] + goyr[2 + half]) + (goyr[4 + half] + goyr[6 + half])
        for a in range(3):
            for b in range(3):
                at = b * 12 + (2 - a) * 4
                t = (3 * a + b) * C + half * 128
                gout_ref[:, t:t + 128] = total[at:at + 3]
    for half in range(2):
        for n in range(4):
            fd, sd = last_source(4 * half + n)
            copy = remote(
                yb.at[0], yr.at[4 * half + n], y_ss.at[1, 0], y_rs.at[1, 4 * half + n], fd, sd
            )
            guard((fd != f) | (sd != s), copy.wait_recv)
        total = (yr[4 * half] + yr[4 * half + 1]) + (yr[4 * half + 2] + yr[4 * half + 3])
        gconv_ref[:, half * 128:(half + 1) * 128] = total[0:36]

    for cond, copy in sends:
        guard(cond, copy.wait_send)


def per_device(latents, conv_weight, conv_bias, out_weight, row_table, patch_weight, pos_embed,
               proj_weight, text_embed):
    vmem = pl.BlockSpec(memory_space=pltpu.VMEM)
    hbm = pl.BlockSpec(memory_space=pltpu.HBM)
    V = pltpu.VMEM
    dma = pltpu.SemaphoreType.DMA
    reward, gconv, gout = pl.pallas_call(
        kernel,
        out_shape=(
            jax.ShapeDtypeStruct((1,), F32),
            jax.ShapeDtypeStruct((36, C), F32),
            jax.ShapeDtypeStruct((3, 9 * C), F32),
        ),
        in_specs=[hbm] * 9,
        out_specs=(pl.BlockSpec(memory_space=pltpu.SMEM), vmem, vmem),
        scratch_shapes=[
            V((1, C), F32), V((3, 9 * C), BF16), V((1, IMG), jnp.int32), V((1, EMB), F32),
            V((4, WL, C), BF16),
            V((3, 3 * C, C), BF16),
            V((4 * WL, 3 * C), BF16),
            V((3, 4 * WL, C), F32),
            V((2 * WL, 6 * C), BF16),
            V((2 * WL, 4 * C), F32),
            V((48, 6 * C), F32),
            V((48, C), F32),
            V((588, CW), BF16),
            V((KP, CW), BF16),
            V((32, CW), BF16),
            V((CW, EMB), BF16),
            V((16, 256), BF16),
            V((9, 16, 256), BF16),
            V((256, 128), F32),
            V((256, 128), F32),
            V((32, CW), F32),
            V((1, CW), F32),
            V((GROUPS, 1, CW), F32),
            V((3, 32, 256), F32),
            V((C, 4 * WL), BF16),
            V((2, 9 * C, 128), F32),
            V((2, 9 * C, 128), BF16),
            V((9 * C, 128), BF16),
            V((4, 576, 128), BF16),
            V((4, 576, 128), F32),
            V((4, 576, 128), BF16),
            V((8, 80, 128), BF16),
            V((8, 72, 128), F32),
            V((8, 80, 128), BF16),
            V((2, 40, 128), F32),
            V((8, 40, 128), F32),
            V((2, 40, 128), F32),
            V((40, 128), F32),
            V((40, 128), F32),
            V((8, 40, 128), F32),
            V((40, 128), F32),
            V((4, 40, 128), F32),
            V((40, 128), F32),
            V((8, 40, 128), F32),
            dma((18,)), dma((2,)), dma((2,)), dma((9,)), dma((9,)), dma((16,)), dma((16,)),
            dma((4,)), dma((4,)), dma((2, 4)), dma((2, 4)), dma((2, 8)), dma((2, 8)),
            dma((2, 8)), dma((2, 8)),
        ],
        compiler_params=pltpu.CompilerParams(
            collective_id=0, has_side_effects=True, vmem_limit_bytes=60 * 1024 * 1024
        ),
    )(
        latents, conv_weight, conv_bias.reshape(1, C), out_weight, row_table, patch_weight,
        pos_embed, proj_weight, text_embed.reshape(1, EMB),
    )
    return reward, gconv, gout


def solution(mesh):
    return jax.shard_map(
        per_device,
        mesh=mesh,
        in_specs=(
            P("frame", "slab", None, None), P(), P(), P(), P("frame", None), P(), P(), P(), P(),
        ),
        out_specs=(P("frame"), P("slab", None), P()),
        check_vma=False,
    )
```

```python
import jax
import jax.numpy as jnp
from jax import lax
from jax.experimental import pallas as pl
from jax.experimental.pallas import tpu as pltpu
from jax.sharding import PartitionSpec as P

MESH = pl.DeviceIdType.MESH
F32 = jnp.float32
BF16 = jnp.bfloat16

C = 256
CW = 1280
EMB = 1024
IMG = 224
PATCH = 14
WL = 128
N_SLAB = 64
GROUPS = 16
KP = 14 * 64
LOSS_SCALE = 256.0
EPS = 1e-05


def dot_nn(a, b):
    return lax.dot_general(a, b, (((1,), (0,)), ((), ())), preferred_element_type=F32)


def dot_nt(a, b):
    return lax.dot_general(a, b, (((1,), (1,)), ((), ())), preferred_element_type=F32)


def dot_tn(a, b):
    return lax.dot_general(a, b, (((0,), (0,)), ((), ())), preferred_element_type=F32)


def iota(shape, dim):
    return lax.broadcasted_iota(jnp.int32, shape, dim)


def split2(v):
    hi = v.astype(BF16)
    lo = (v - hi.astype(F32)).astype(BF16)
    return hi, lo


def lat_row(r6, a):
    return (r6 - 1 + a - 1) // 2 + 1


def patch_column(c14):
    c16 = c14 * 8 // 7
    return c16 % 2, c16 // 2


def kernel(
    lat_hbm, cw_hbm, bias_hbm, ow_hbm, table_hbm, pw_hbm, pos_hbm, proj_hbm, text_hbm,
    reward_ref, gconv_ref, gout_ref,
    bias_ref, ow_ref, table_ref, text_ref,
    lat4, wb, lcat, zbuf, hbuf, gate, wd32, wo32, pw, pwp, pos, proj,
    dec, dall, ct, gt, ybuf, psend, precv, igs, latt,
    g32, gbf, gcr, xbf, x32, xr, zbf, z32, zr, yb, yr,
    go2, gocr, goz, gozr, gox, goxr, goy, goyr,
    loc_sem, halo_ss, halo_rs, gat_ss, gat_rs, pool_ss, pool_rs,
    c_ss, c_rs, u_ss, u_rs, x_ss, x_rs, z_ss, z_rs, y_ss, y_rs, flood_sem,
):
    f = lax.axis_index("frame")
    s = lax.axis_index("slab")
    y_hi, core = f // 2, f % 2
    x, z, y_lo = s // 16, (s % 16) // 2, s % 2
    p, q = s // 4, s % 4
    low_half = q < 2
    base = jnp.where(low_half, 4 * p - 4, 4 * p)
    p2 = jnp.where(low_half, p - 1, p + 1)
    p2c = jnp.clip(p2, 0, GROUPS - 1)

    dall[...] = jnp.zeros_like(dall)
    lat4[0] = jnp.zeros((WL, C), BF16)
    lat4[3] = jnp.zeros((WL, C), BF16)

    barrier = pltpu.get_barrier_semaphore()

    def greet(cond, fd, sd):
        def go():
            pl.semaphore_signal(barrier, inc=1, device_id=(fd, sd), device_id_type=MESH)

        if cond is None:
            go()
        else:
            pl.when(cond)(go)

    greet(s > 0, f, s - 1)
    greet(s < N_SLAB - 1, f, s + 1)
    for d in range(1, 4):
        greet(None, f, 4 * p + (q + d) % 4)
    for v in range(4):
        greet((q == 0) & (p > 0), f, 4 * p - 4 + v)
        greet((q == 3) & (p < GROUPS - 1), f, 4 * p + 4 + v)
    greet((q < 3) & (p < GROUPS - 1), f, 4 * p + 4)
    greet((q == 3) & (p < GROUPS - 2), f, 4 * p + 8)
    for d in range(1, 4):
        greet(None, f, ((x + d) % 4) * 16 + z * 2 + y_lo)
    for d in (2, 6):
        greet(None, f, x * 16 + ((z + d) % 8) * 2 + y_lo)
    yc = y_hi * 4 + y_lo * 2 + core

    def yc_device(idx):
        return (idx // 4) * 2 + idx % 2, x * 16 + z * 2 + (idx // 2) % 2

    for d in range(1, 8):
        greet(None, *yc_device((yc + d) % 8))
    y = y_hi * 2 + y_lo

    def last_source(slot):
        if slot < 4:
            return (slot // 2) * 2, x * 16 + z * 2 + slot % 2
        return (x // 2) * 2 + 1, (slot - 4) * 16 + z * 2 + y_lo

    def one(cond):
        return jnp.where(cond, 1, 0)

    expected = (
        one(s > 0) + one(s < N_SLAB - 1)
        + 3 + one(p < GROUPS - 1) + one(p > 0)
        + one((q == 0) & (p > 0)) * 3 + one((q == 0) & (p > 1))
        + 3 + 2 + 7
    )

    loads = []

    def load(src, dst):
        copy = pltpu.make_async_copy(src, dst, loc_sem.at[len(loads)])
        copy.start()
        loads.append(copy)
        return copy

    lat_load = load(lat_hbm.at[0], lat4.at[pl.ds(1, 2)])
    ow_load = load(ow_hbm, ow_ref)
    bias_load = load(bias_hbm, bias_ref)
    table_load = load(table_hbm, table_ref)
    text_load = load(text_hbm, text_ref)
    w_loads = []
    for a in range(3):
        for b in range(3):
            t = 3 * a + b
            w_loads.append(
                load(cw_hbm.at[pl.ds(t * C, C)], wb.at[b, pl.ds(a * C, C)])
            )
    pw_load = load(pw_hbm, pw)
    pos_loads = [
        load(pos_hbm.at[pl.ds(pl.multiple_of(16 * p, 16), 16)], pos.at[pl.ds(0, 16)]),
        load(pos_hbm.at[pl.ds(pl.multiple_of(16 * p2c, 16), 16)], pos.at[pl.ds(16, 16)]),
    ]
    proj_load = load(proj_hbm, proj)

    pl.semaphore_wait(barrier, expected)

    def flood(stage):
        for n, d in enumerate((2, 6)):
            pl.semaphore_signal(
                flood_sem.at[2 * stage + n], inc=1,
                device_id=(f, x * 16 + ((z + d) % 8) * 2 + y_lo), device_id_type=MESH,
            )

    def flood_wait(stage):
        for n in range(2):
            pl.semaphore_wait(flood_sem.at[2 * stage + n], 1)

    flood(0)

    sends = []

    def remote(src, dst, ssem, rsem, fd, sd):
        return pltpu.make_async_remote_copy(
            src_ref=src, dst_ref=dst, send_sem=ssem, recv_sem=rsem,
            device_id=(fd, sd), device_id_type=MESH,
        )

    def guard(cond, action):
        if cond is None:
            action()
        else:
            pl.when(cond)(action)

    def send(cond, *what):
        copy = remote(*what)
        guard(cond, copy.start)
        sends.append((cond, copy))
        return copy

    up = send(s > 0, lat_hbm.at[0, 0], lat4.at[3], halo_ss.at[0], halo_rs.at[1], f, s - 1)
    down = send(
        s < N_SLAB - 1, lat_hbm.at[0, 1], lat4.at[0], halo_ss.at[1], halo_rs.at[0], f, s + 1
    )

    wd32[...] = jnp.zeros_like(wd32)
    wo32[...] = jnp.zeros_like(wo32)
    ow_load.wait()
    for a in range(3):
        for b in range(3):
            t = 3 * a + b
            tap = ow_ref[:, t * C:(t + 1) * C].astype(F32)
            wo32[b * 16 + (2 - a) * 4:b * 16 + (2 - a) * 4 + 3, :] = tap
            for r in range(4):
                wd32[b * 16 + r * 4:b * 16 + r * 4 + 3, (r + a) * C:(r + a + 1) * C] = tap

    bias_load.wait()
    bias = bias_ref[...]
    first = iota((WL, C), 0) == 0
    last = iota((WL, C), 0) == WL - 1

    def activate(r6, z0, z1, z2):
        before = jnp.where(first, 0.0, pltpu.roll(z0, 1, 0))
        after = jnp.where(last, 0.0, pltpu.roll(z2, WL - 1, 0))
        for pc, total in ((0, before + z1 + z2), (1, z0 + z1 + after)):
            total = total + bias
            hidden = total * (0.5 + 0.5 * jnp.tanh(0.5 * total))
            if r6 == 0:
                hidden = jnp.where(s > 0, hidden, 0.0)
            elif r6 == 5:
                hidden = jnp.where(s < N_SLAB - 1, hidden, 0.0)
            else:
                gate[pc * WL:(pc + 1) * WL, (r6 - 1) * C:r6 * C] = total
            hbuf[pc * WL:(pc + 1) * WL, r6 * C:(r6 + 1) * C] = hidden.astype(BF16)

    lat_load.wait()
    for copy in w_loads:
        copy.wait()

    for n, r6 in enumerate((2, 3)):
        for a in range(3):
            lcat[n * WL:(n + 1) * WL, a * C:(a + 1) * C] = lat4[lat_row(r6, a)]
    for b in range(3):
        zbuf[b, 0:2 * WL] = dot_nn(lcat[0:2 * WL, :], wb[b])
    for n, r6 in enumerate((2, 3)):
        here = slice(n * WL, (n + 1) * WL)
        activate(r6, zbuf[0, here], zbuf[1, here], zbuf[2, here])
    for b in range(3):
        top, low = lat4[1], lat4[2]
        zbuf[b, 0:WL] = dot_nn(top, wb[b, 2 * C:3 * C])
        zbuf[b, WL:2 * WL] = dot_nn(jnp.concatenate([top, top], axis=1), wb[b, C:3 * C])
        zbuf[b, 2 * WL:3 * WL] = dot_nn(jnp.concatenate([low, low], axis=1), wb[b, 0:2 * C])
        zbuf[b, 3 * WL:4 * WL] = dot_nn(low, wb[b, 0:C])

    guard(s < N_SLAB - 1, up.wait_recv)
    guard(s > 0, down.wait_recv)
    flood_wait(0)
    flood(1)
    for near, far, edge, inner_tap, outer_tap in ((1, 0, 0, 0, 1), (4, 5, 3, 2, 1)):
        halo_row = lat4[edge]
        near_z, far_z = [], []
        for b in range(3):
            one_tap = dot_nn(halo_row, wb[b, inner_tap * C:(inner_tap + 1) * C])
            two_taps = one_tap + dot_nn(halo_row, wb[b, outer_tap * C:(outer_tap + 1) * C])
            n = 0 if near == 1 else 3
            far_z.append(zbuf[b, n * WL:(n + 1) * WL] + two_taps)
            n = 1 if near == 1 else 2
            near_z.append(zbuf[b, n * WL:(n + 1) * WL] + one_tap)
        activate(far, *far_z)
        activate(near, *near_z)

    res = dot_nt(wd32[...].astype(BF16), hbuf[...])
    even, odd = res[:, 0:WL], res[:, WL:2 * WL]
    left = iota((16, WL), 1) == 0
    right = iota((16, WL), 1) == WL - 1
    dec_even = jnp.where(left, 0.0, pltpu.roll(odd[0:16], 1, 1)) + even[16:32] + odd[32:48]
    dec_odd = even[0:16] + odd[16:32] + jnp.where(right, 0.0, pltpu.roll(even[32:48], WL - 1, 1))
    decoded = jnp.concatenate([dec_even, dec_odd], axis=1).astype(BF16)
    dec[...] = decoded
    dall[jnp.where(low_half, q + 4, q)] = decoded

    def gather_send(n, cond, target, slot):
        send(cond, dec, dall.at[slot], gat_ss.at[n], gat_rs.at[slot], f, target)

    for d in range(1, 4):
        qd = (q + d) % 4
        gather_send(d - 1, None, 4 * p + qd, jnp.where(qd < 2, q + 4, q))
    gather_send(3, p < GROUPS - 1, 4 * p + 4, q)
    gather_send(4, p > 0, 4 * p - 1, q + 4)
    gather_send(5, (q == 0) & (p > 0), 4 * p - 4, 8)
    gather_send(6, (q == 0) & (p > 0), 4 * p - 3, 8)
    gather_send(7, (q == 0) & (p > 0), 4 * p - 2, 4)
    gather_send(8, (q == 0) & (p > 1), 4 * p - 5, 8)

    rk = iota((128, 1), 0)
    g = rk & 63
    colour = one(g >= 14) + one(g >= 28)
    ig = jnp.where(rk < 64, p, p2) * PATCH + g - 14 * colour
    valid = (g < 42) & (ig >= 0) & (ig < IMG)
    table_load.wait()
    table = table_ref[...].astype(F32)
    cols = iota((128, IMG), 1)
    lo = jnp.sum(jnp.where(cols == ig, table, 0.0), axis=1, keepdims=True)
    nxt = jnp.sum(jnp.where(cols == ig + 1, table, 0.0), axis=1, keepdims=True)
    nxt = nxt + jnp.where(ig == IMG - 1, 256.0, 0.0)
    hi = jnp.maximum(nxt, lo + 1.0)
    inv = 1.0 / (hi - lo)
    lane = iota((128, 144), 1)
    row = (4 * base + (lane >> 2)).astype(F32)
    inside = valid & ((lane & 3) == colour) & (row >= lo) & (row < hi)
    pick = jnp.where(inside, 1.0, 0.0).astype(BF16)
    lane = iota((128, 128), 1)
    row = (4 * s - 1 + (lane >> 2)).astype(F32)
    inside = valid & ((lane & 3) == colour) & (row >= lo) & (row < hi) & (lane < 24)
    both = jnp.where(lane == 32, inv, jnp.where(inside, 1.0, 0.0)).T
    back = both[0:32].astype(BF16)
    back = jnp.concatenate([back, back], axis=1)
    inv_row = both[32:33]

    pw_load.wait()
    prow = iota((KP, 588), 0)
    pg = prow & 63
    order = jnp.where(
        (pg < 42) & (iota((KP, 588), 1) == 14 * pg + 2 * (prow >> 7) + ((prow >> 6) & 1)), 1.0, 0.0
    ).astype(BF16)
    for n in range(CW // 256):
        cut = slice(n * 256, (n + 1) * 256)
        pwp[:, cut] = dot_nn(order, pw[:, cut]).astype(BF16)

    def gather_wait(slot, cond, source):
        copy = remote(dec, dall.at[slot], gat_ss.at[0], gat_rs.at[slot], f, source)
        pl.when(cond)(copy.wait_recv)

    more = p < GROUPS - 1
    for v in range(4):
        gather_wait(
            v, (low_half & (q == 0) & (p > 0)) | ((q >= 2) & (q != v)),
            jnp.where(low_half, 4 * p - 4 + v, 4 * p + v),
        )
        if v == 0:
            cond = (low_half & (q != v)) | ((q >= 2) & more)
        else:
            cond = (low_half & (q != v)) | ((q == 3) & more)
        gather_wait(v + 4, cond, jnp.where(low_half, 4 * p + v, 4 * p + 4 + v))
    gather_wait(
        8, (low_half & more) | ((q == 3) & (p < GROUPS - 2)),
        jnp.where(low_half, 4 * p + 4, 4 * p + 8),
    )

    flood_wait(1)
    crop = dot_nn(pick, dall[...].reshape(144, 256)) * inv
    ct[...] = crop.T
    lane16 = iota((16, 128), 1) < 64
    parts0, parts1 = [], []
    for n in range(7):
        pair = []
        for c14 in (2 * n, 2 * n + 1):
            pc, pj = patch_column(c14)
            pair.append(ct[pl.ds(pc * WL + pj, 16, stride=8), :])
        parts0.append(jnp.where(lane16, pair[0], pltpu.roll(pair[1], 64, 1)))
        parts1.append(jnp.where(lane16, pltpu.roll(pair[0], 64, 1), pair[1]))
    patches = jnp.concatenate(
        [jnp.concatenate(parts0, axis=1), jnp.concatenate(parts1, axis=1)], axis=0
    )
    for copy in pos_loads:
        copy.wait()
    emb = dot_nn(jnp.concatenate(split2(patches), axis=0), pwp[...])
    emb = emb[0:32] + emb[32:64] + pos[...].astype(F32)
    centred = emb - jnp.mean(emb, axis=1, keepdims=True)
    sigma = jnp.sqrt(jnp.mean(centred * centred, axis=1, keepdims=True) + EPS)
    normed = centred / sigma
    ybuf[...] = normed
    gsum = jnp.sum(normed[0:16], axis=0, keepdims=True)
    psend[...] = gsum
    precv[p] = gsum

    for d in range(1, GROUPS):
        send(
            None, psend, precv.at[p], pool_ss.at[d], pool_rs.at[p],
            f, 4 * ((p + d) % GROUPS) + q,
        )

    for n in range(4):
        cut = slice(n * C, (n + 1) * C)
        total = gate[:, cut]
        sig = 0.5 + 0.5 * jnp.tanh(0.5 * total)
        gate[:, cut] = sig * (1.0 + total * (1.0 - sig))
    for n in range(4):
        latt[:, n * WL:(n + 1) * WL] = lat4[n].astype(F32).T.astype(BF16)
    text_load.wait()
    text = text_ref[...]
    text2 = jnp.sum(text * text, axis=1, keepdims=True) + 1e-06
    gt[...] = jnp.zeros_like(gt)

    for d in range(1, GROUPS):
        pd = (p + d) % GROUPS
        remote(
            psend, precv.at[pd], pool_ss.at[d], pool_rs.at[pd], f, 4 * pd + q
        ).wait_recv()
    pooled = precv[0]
    for n in range(1, GROUPS):
        pooled = pooled + precv[n]
    pooled = pooled * (1.0 / 256.0)

    proj_load.wait()

    def two_rows(v):
        top = iota((16, v.shape[1]), 0)
        hi_part = v.astype(BF16).astype(F32)
        return jnp.where(top == 0, hi_part, jnp.where(top == 1, v - hi_part, 0.0)).astype(BF16)

    pc_ = pooled - jnp.mean(pooled, axis=1, keepdims=True)
    psigma = jnp.sqrt(jnp.mean(pc_ * pc_, axis=1, keepdims=True) + EPS)
    unit = pc_ / psigma
    projected = jnp.sum(dot_nn(two_rows(unit), proj[...]), axis=0, keepdims=True)
    numer = jnp.sum(projected * text, axis=1, keepdims=True)
    norm2 = jnp.sum(projected * projected, axis=1, keepdims=True) + 1e-06
    scale = 1.0 / jnp.sqrt(norm2 * text2)
    reward = numer * scale
    reward_ref[0] = reward[0, 0]
    dproj = -LOSS_SCALE * (text * scale - projected * (reward / norm2))
    dunit = jnp.sum(dot_nt(two_rows(dproj), proj[...]), axis=0, keepdims=True)

    def norm_back(dy, y, sg):
        m1 = jnp.mean(dy, axis=1, keepdims=True)
        m2 = jnp.mean(dy * y, axis=1, keepdims=True)
        return (dy - m1 - y * m2) / sg

    dpooled = norm_back(dunit, unit, psigma) * (1.0 / 256.0)
    demb = norm_back(dpooled, ybuf[...], sigma)
    dpat = dot_nt(jnp.concatenate(split2(demb), axis=0), pwp[...])
    dpat = dpat[0:32] + dpat[32:64]
    for n in range(7):
        d0 = dpat[0:16, n * 128:(n + 1) * 128]
        d1 = dpat[16:32, n * 128:(n + 1) * 128]
        pair = (
            jnp.where(lane16, d0, pltpu.roll(d1, 64, 1)),
            jnp.where(lane16, pltpu.roll(d0, 64, 1), d1),
        )
        for half in range(2):
            pc, pj = patch_column(2 * n + half)
            gt[pl.ds(pc * WL + pj, 16, stride=8), :] = pair[half]

    grows = jnp.concatenate(split2(gt[...] * inv_row), axis=1)
    image = dot_nt(back, grows).astype(BF16).astype(F32)
    even, odd = image[:, 0:WL], image[:, WL:2 * WL]
    left = iota((32, WL), 1) == 0
    right = iota((32, WL), 1) == WL - 1
    odd_before = jnp.where(left, 0.0, pltpu.roll(odd, 1, 1))
    even_after = jnp.where(right, 0.0, pltpu.roll(even, WL - 1, 1))
    igs[0] = jnp.concatenate([odd, even_after], axis=1)
    igs[1] = image
    igs[2] = jnp.concatenate([odd_before, even], axis=1)

    ims = []
    go = jnp.zeros((48, C), F32)
    for r in range(4):
        im = jnp.concatenate([igs[b, 4 * r:4 * r + 16, :] for b in range(3)], axis=0).astype(BF16)
        ims.append(im)
        go = go + dot_nn(im, hbuf[:, (r + 1) * C:(r + 2) * C])
    for half in range(2):
        go2[half, 27:32, :] = jnp.zeros((5, 128), F32)
        for t in range(9):
            at = (t % 3) * 16 + (2 - t // 3) * 4
            go2[half, 3 * t:3 * t + 3, :] = go[at:at + 3, half * 128:(half + 1) * 128]
    fc = y_hi * 2 + 1 - core
    outk = send(None, go2.at[1 - core], gocr, c_ss.at[3], c_rs.at[3], fc, s)

    wout = wo32[...].astype(BF16)
    cols_of = []
    for r in range(4):
        cg = dot_tn(ims[r], wout) * gate[:, r * C:(r + 1) * C]
        ev, od = cg[0:WL], cg[WL:2 * WL]
        od_before = jnp.where(first, 0.0, pltpu.roll(od, 1, 0))
        ev_after = jnp.where(last, 0.0, pltpu.roll(ev, WL - 1, 0))
        cols_of.append((od + ev_after, ev + od, od_before + ev))

    def put_grad(a, b, value):
        at = (3 * a + b) * C
        for half in range(2):
            part = value[:, half * 128:(half + 1) * 128]
            g32[half, at:at + C, :] = part
            gbf[half, at:at + C, :] = part.astype(BF16)

    outer = [
        jnp.concatenate([cols_of[0][b], cols_of[1][b] + cols_of[2][b], cols_of[3][b]], axis=0)
        .astype(BF16) for b in range(3)
    ]
    inner = [
        jnp.concatenate([cols_of[0][b] + cols_of[1][b], cols_of[2][b] + cols_of[3][b]], axis=0)
        .astype(BF16) for b in range(3)
    ]
    outk.wait_recv()
    gsum_z = go2[core] + gocr[...]
    goz[...] = gsum_z
    for d in range(1, 8):
        zd = (z + d) % 8
        send(
            None, goz, gozr.at[z], z_ss.at[0, d], z_rs.at[0, z], f, x * 16 + zd * 2 + y_lo
        )

    main = []
    for a, start, stop, terms in ((0, 0, 3, outer), (1, 1, 3, inner), (2, 1, 4, outer)):
        for b in range(3):
            put_grad(a, b, dot_nn(latt[:, start * WL:stop * WL], terms[b]))
        rows = pl.ds(a * 768, 768)
        main.append(
            send(None, gbf.at[1 - core, rows], gcr.at[rows], c_ss.at[a], c_rs.at[a], fc, s)
        )

    mine = jnp.where(core == 0, x, y)

    def quarter_device(n):
        fd = jnp.where(core == 0, f, (n // 2) * 2 + 1)
        sd = jnp.where(core == 0, n * 16 + z * 2 + y_lo, x * 16 + z * 2 + n % 2)
        return fd, sd

    def halves_sum(half, start, count):
        return g32[half, start:start + count, :] + gcr[start:start + count, :].astype(F32)

    for w in range(4):
        for part in range(2):
            if w == 0 and part == 0:
                main[0].wait_recv()
                main[1].wait_recv()
            elif w == 0:
                main[2].wait_recv()

            @pl.when(core == 0)
            def along_x():
                for n in (2 * part, 2 * part + 1):
                    total = jnp.concatenate(
                        [halves_sum(0, n * 576 + zd * 72, 72) for zd in (w, w + 4)], axis=0
                    )
                    x32[n, w] = total
                    xbf[n, w] = total.astype(BF16)

            @pl.when(core == 1)
            def along_y():
                units = [
                    halves_sum(1, (2 * part + h) * 576 + zd * 72, 72)
                    for zd in (w, w + 4) for h in range(2)
                ]
                for n in range(2):
                    total = jnp.concatenate([u[36 * n:36 * n + 36] for u in units], axis=0)
                    x32[2 * part + n, w] = total
                    xbf[2 * part + n, w] = total.astype(BF16)

            for n in (2 * part, 2 * part + 1):
                send(
                    mine != n, xbf.at[n, w], xr.at[w, mine], u_ss.at[w, n], u_rs.at[w, mine],
                    *quarter_device(n),
                )

    for w in range(4):
        xr[w, mine] = jnp.zeros((144, 128), BF16)
    zr[z] = jnp.zeros((80, 128), BF16)
    for w in range(4):
        for n in range(4):
            copy = remote(
                xbf.at[n, w], xr.at[w, n], u_ss.at[w, n], u_rs.at[w, n], *quarter_device(n)
            )
            guard(mine != n, copy.wait_recv)
        for k in range(2):
            zd = w + 4 * k
            cut = slice(k * 72, (k + 1) * 72)
            total = x32[mine, w, cut, :]
            for n in range(4):
                total = total + xr[w, n, cut, :].astype(F32)
            z32[zd] = total
            zbf[zd] = jnp.concatenate([total, jnp.zeros((8, 128), F32)], axis=0).astype(BF16)
            send(
                z != zd, zbf.at[zd], zr.at[z], z_ss.at[1, zd], z_rs.at[1, z],
                f, x * 16 + zd * 2 + y_lo,
            )

    gozr[z] = gsum_z
    for d in range(1, 8):
        zd = (z + d) % 8
        remote(
            goz, gozr.at[zd], z_ss.at[0, d], z_rs.at[0, zd], f, x * 16 + zd * 2 + y_lo
        ).wait_recv()
    gsum_x = jnp.sum(gozr[...], axis=0)
    gox[...] = gsum_x
    for d in range(1, 4):
        xd = (x + d) % 4
        send(None, gox, goxr.at[x], x_ss.at[d], x_rs.at[x], f, xd * 16 + z * 2 + y_lo)
    goxr[x] = gsum_x
    for d in range(1, 4):
        xd = (x + d) % 4
        remote(
            gox, goxr.at[xd], x_ss.at[d], x_rs.at[xd], f, xd * 16 + z * 2 + y_lo
        ).wait_recv()
    gsum_y = jnp.sum(goxr[...], axis=0)
    goy[...] = gsum_y
    for d in range(1, 8):
        yd = (yc + d) % 8
        send(None, goy, goyr.at[yc], y_ss.at[0, d], y_rs.at[0, yc], *yc_device(yd))
    goyr[yc] = gsum_y

    for d in range(1, 8):
        zd = (z + d) % 8
        remote(
            zbf.at[zd], zr.at[zd], z_ss.at[1, d], z_rs.at[1, zd], f, x * 16 + zd * 2 + y_lo
        ).wait_recv()
    total = z32[z]
    for n in range(8):
        total = total + zr[n, 0:72, :].astype(F32)

    for n in range(2):
        yb[n, 0:36, :] = total[36 * n:36 * n + 36]
        yb[n, 36:40, :] = jnp.zeros((4, 128), F32)
    slot = jnp.where(core == 0, y, 4 + x)
    for n in range(2):
        sd = jnp.where(core == 0, x * 16 + z * 2 + n, (2 * y_hi + n) * 16 + z * 2 + y_lo)
        here = sd == s

        @pl.when(here)
        def keep():
            yr[slot] = yb[n]

        for j in range(4):
            send(
                jnp.logical_not(here & (f == j)), yb.at[n], yr.at[slot],
                y_ss.at[1, 4 * n + j], y_rs.at[1, slot], j, sd,
            )

    for d in range(1, 8):
        yd = (yc + d) % 8
        remote(
            goy, goyr.at[yd], y_ss.at[0, d], y_rs.at[0, yd], *yc_device(yd)
        ).wait_recv()
    for half in range(2):
        total = (goyr[half] + goyr[2 + half]) + (goyr[4 + half] + goyr[6 + half])
        for t in range(9):
            gout_ref[:, t * C + half * 128:t * C + (half + 1) * 128] = total[3 * t:3 * t + 3]
    for half in range(2):
        for n in range(4):
            fd, sd = last_source(4 * half + n)
            copy = remote(
                yb.at[0], yr.at[4 * half + n], y_ss.at[1, 0], y_rs.at[1, 4 * half + n], fd, sd
            )
            guard((fd != f) | (sd != s), copy.wait_recv)
        total = (yr[4 * half] + yr[4 * half + 1]) + (yr[4 * half + 2] + yr[4 * half + 3])
        gconv_ref[:, half * 128:(half + 1) * 128] = total[0:36]

    for cond, copy in sends:
        guard(cond, copy.wait_send)


def per_device(latents, conv_weight, conv_bias, out_weight, row_table, patch_weight, pos_embed,
               proj_weight, text_embed):
    vmem = pl.BlockSpec(memory_space=pltpu.VMEM)
    hbm = pl.BlockSpec(memory_space=pltpu.HBM)
    V = pltpu.VMEM
    dma = pltpu.SemaphoreType.DMA
    reward, gconv, gout = pl.pallas_call(
        kernel,
        out_shape=(
            jax.ShapeDtypeStruct((1,), F32),
            jax.ShapeDtypeStruct((36, C), F32),
            jax.ShapeDtypeStruct((3, 9 * C), F32),
        ),
        in_specs=[hbm] * 9,
        out_specs=(pl.BlockSpec(memory_space=pltpu.SMEM), vmem, vmem),
        scratch_shapes=[
            V((1, C), F32), V((3, 9 * C), BF16), V((1, IMG), jnp.int32), V((1, EMB), F32),
            V((4, WL, C), BF16),
            V((3, 3 * C, C), BF16),
            V((2 * WL, 3 * C), BF16),
            V((3, 4 * WL, C), F32),
            V((2 * WL, 6 * C), BF16),
            V((2 * WL, 4 * C), F32),
            V((48, 6 * C), F32),
            V((48, C), F32),
            V((588, CW), BF16),
            V((KP, CW), BF16),
            V((32, CW), BF16),
            V((CW, EMB), BF16),
            V((16, 256), BF16),
            V((9, 16, 256), BF16),
            V((256, 128), F32),
            V((256, 128), F32),
            V((32, CW), F32),
            V((1, CW), F32),
            V((GROUPS, 1, CW), F32),
            V((3, 32, 256), F32),
            V((C, 4 * WL), BF16),
            V((2, 9 * C, 128), F32),
            V((2, 9 * C, 128), BF16),
            V((9 * C, 128), BF16),
            V((4, 4, 144, 128), BF16),
            V((4, 4, 144, 128), F32),
            V((4, 4, 144, 128), BF16),
            V((8, 80, 128), BF16),
            V((8, 72, 128), F32),
            V((8, 80, 128), BF16),
            V((2, 40, 128), F32),
            V((8, 40, 128), F32),
            V((2, 32, 128), F32),
            V((32, 128), F32),
            V((32, 128), F32),
            V((8, 32, 128), F32),
            V((32, 128), F32),
            V((4, 32, 128), F32),
            V((32, 128), F32),
            V((8, 32, 128), F32),
            dma((18,)), dma((2,)), dma((2,)), dma((9,)), dma((9,)), dma((16,)), dma((16,)),
            dma((4,)), dma((4,)), dma((4, 4)), dma((4, 4)), dma((4,)), dma((4,)),
            dma((2, 8)), dma((2, 8)),
            dma((2, 8)), dma((2, 8)), pltpu.SemaphoreType.REGULAR((4,)),
        ],
        compiler_params=pltpu.CompilerParams(
            collective_id=0, has_side_effects=True, vmem_limit_bytes=60 * 1024 * 1024
        ),
    )(
        latents, conv_weight, conv_bias.reshape(1, C), out_weight, row_table, patch_weight,
        pos_embed, proj_weight, text_embed.reshape(1, EMB),
    )
    return reward, gconv, gout


def solution(mesh):
    return jax.shard_map(
        per_device,
        mesh=mesh,
        in_specs=(
            P("frame", "slab", None, None), P(), P(), P(), P("frame", None), P(), P(), P(), P(),
        ),
        out_specs=(P("frame"), P("slab", None), P()),
        check_vma=False,
    )
```

```python
import jax
import jax.numpy as jnp
from jax import lax
from jax.experimental import pallas as pl
from jax.experimental.pallas import tpu as pltpu
from jax.sharding import PartitionSpec as P

MESH = pl.DeviceIdType.MESH
F32 = jnp.float32
BF16 = jnp.bfloat16

C = 256
CW = 1280
EMB = 1024
IMG = 224
PATCH = 14
WL = 128
N_SLAB = 64
GROUPS = 16
KP = 14 * 64
LOSS_SCALE = 256.0
EPS = 1e-05


def dot_nn(a, b):
    return lax.dot_general(a, b, (((1,), (0,)), ((), ())), preferred_element_type=F32)


def dot_nt(a, b):
    return lax.dot_general(a, b, (((1,), (1,)), ((), ())), preferred_element_type=F32)


def dot_tn(a, b):
    return lax.dot_general(a, b, (((0,), (0,)), ((), ())), preferred_element_type=F32)


def iota(shape, dim):
    return lax.broadcasted_iota(jnp.int32, shape, dim)


def split2(v):
    hi = v.astype(BF16)
    lo = (v - hi.astype(F32)).astype(BF16)
    return hi, lo


def lat_row(r6, a):
    return (r6 - 1 + a - 1) // 2 + 1


def patch_column(c14):
    c16 = c14 * 8 // 7
    return c16 % 2, c16 // 2


def kernel(
    lat_hbm, cw_hbm, bias_hbm, ow_hbm, table_hbm, pw_hbm, pos_hbm, proj_hbm, text_hbm,
    reward_ref, gconv_ref, gout_ref,
    bias_ref, ow_ref, table_ref, text_ref,
    lat4, wb, lcat, zbuf, hbuf, gate, wd32, wo32, pw, pwp, pos, proj,
    dec, dall, ct, gt, ybuf, psend, precv, igs, latt,
    g32, gbf, gcr, xbf, x32, xr, zbf, z32, zr, yb, yr,
    go2, gocr, goz, gozr, gox, goxr, goy, goyr,
    loc_sem, halo_ss, halo_rs, gat_ss, gat_rs, pool_ss, pool_rs,
    c_ss, c_rs, u_ss, u_rs, x_ss, x_rs, z_ss, z_rs, y_ss, y_rs, flood_sem,
):
    f = lax.axis_index("frame")
    s = lax.axis_index("slab")
    y_hi, core = f // 2, f % 2
    x, z, y_lo = s // 16, (s % 16) // 2, s % 2
    p, q = s // 4, s % 4
    low_half = q < 2
    base = jnp.where(low_half, 4 * p - 4, 4 * p)
    p2 = jnp.where(low_half, p - 1, p + 1)
    p2c = jnp.clip(p2, 0, GROUPS - 1)

    dall[...] = jnp.zeros_like(dall)
    lat4[0] = jnp.zeros((WL, C), BF16)
    lat4[3] = jnp.zeros((WL, C), BF16)

    barrier = pltpu.get_barrier_semaphore()

    def greet(cond, fd, sd):
        def go():
            pl.semaphore_signal(barrier, inc=1, device_id=(fd, sd), device_id_type=MESH)

        if cond is None:
            go()
        else:
            pl.when(cond)(go)

    greet(s > 0, f, s - 1)
    greet(s < N_SLAB - 1, f, s + 1)
    for d in range(1, 4):
        greet(None, f, 4 * p + (q + d) % 4)
    for v in range(4):
        greet((q == 0) & (p > 0), f, 4 * p - 4 + v)
        greet((q == 3) & (p < GROUPS - 1), f, 4 * p + 4 + v)
    greet((q < 3) & (p < GROUPS - 1), f, 4 * p + 4)
    for d in range(1, 4):
        greet(None, f, ((x + d) % 4) * 16 + z * 2 + y_lo)
    for d in (2, 6):
        greet(None, f, x * 16 + ((z + d) % 8) * 2 + y_lo)
    yc = y_hi * 4 + y_lo * 2 + core

    def yc_device(idx):
        return (idx // 4) * 2 + idx % 2, x * 16 + z * 2 + (idx // 2) % 2

    for d in range(1, 8):
        greet(None, *yc_device((yc + d) % 8))
    y = y_hi * 2 + y_lo

    def last_source(slot):
        if slot < 4:
            return (slot // 2) * 2, x * 16 + z * 2 + slot % 2
        return (x // 2) * 2 + 1, (slot - 4) * 16 + z * 2 + y_lo

    def one(cond):
        return jnp.where(cond, 1, 0)

    expected = (
        one(s > 0) + one(s < N_SLAB - 1)
        + 3 + one(p < GROUPS - 1) + one(p > 0)
        + one((q == 0) & (p > 0)) * 3
        + 3 + 2 + 7
    )

    loads = []

    def load(src, dst):
        copy = pltpu.make_async_copy(src, dst, loc_sem.at[len(loads)])
        copy.start()
        loads.append(copy)
        return copy

    lat_load = load(lat_hbm.at[0], lat4.at[pl.ds(1, 2)])
    ow_load = load(ow_hbm, ow_ref)
    bias_load = load(bias_hbm, bias_ref)
    table_load = load(table_hbm, table_ref)
    text_load = load(text_hbm, text_ref)
    w_loads = []
    for a in range(3):
        for b in range(3):
            t = 3 * a + b
            w_loads.append(
                load(cw_hbm.at[pl.ds(t * C, C)], wb.at[b, pl.ds(a * C, C)])
            )
    pw_load = load(pw_hbm, pw)
    pos_loads = [
        load(pos_hbm.at[pl.ds(pl.multiple_of(16 * p, 16), 16)], pos.at[pl.ds(0, 16)]),
        load(pos_hbm.at[pl.ds(pl.multiple_of(16 * p2c, 16), 16)], pos.at[pl.ds(16, 16)]),
    ]
    proj_load = load(proj_hbm, proj)

    pl.semaphore_wait(barrier, expected)

    def flood(stage):
        for n, d in enumerate((2, 6)):
            pl.semaphore_signal(
                flood_sem.at[2 * stage + n], inc=1,
                device_id=(f, x * 16 + ((z + d) % 8) * 2 + y_lo), device_id_type=MESH,
            )

    def flood_wait(stage):
        for n in range(2):
            pl.semaphore_wait(flood_sem.at[2 * stage + n], 1)

    flood(0)

    @pl.when((q == 0) & (p < GROUPS - 1))
    def tell():
        pl.semaphore_signal(
            flood_sem.at[4], inc=1, device_id=(f, s + 4), device_id_type=MESH
        )

    sends = []

    def remote(src, dst, ssem, rsem, fd, sd):
        return pltpu.make_async_remote_copy(
            src_ref=src, dst_ref=dst, send_sem=ssem, recv_sem=rsem,
            device_id=(fd, sd), device_id_type=MESH,
        )

    def guard(cond, action):
        if cond is None:
            action()
        else:
            pl.when(cond)(action)

    def send(cond, *what):
        copy = remote(*what)
        guard(cond, copy.start)
        sends.append((cond, copy))
        return copy

    up = send(s > 0, lat_hbm.at[0, 0], lat4.at[3], halo_ss.at[0], halo_rs.at[1], f, s - 1)
    down = send(
        s < N_SLAB - 1, lat_hbm.at[0, 1], lat4.at[0], halo_ss.at[1], halo_rs.at[0], f, s + 1
    )

    wd32[...] = jnp.zeros_like(wd32)
    wo32[...] = jnp.zeros_like(wo32)
    ow_load.wait()
    for a in range(3):
        for b in range(3):
            t = 3 * a + b
            tap = ow_ref[:, t * C:(t + 1) * C].astype(F32)
            wo32[b * 16 + (2 - a) * 4:b * 16 + (2 - a) * 4 + 3, :] = tap
            for r in range(4):
                wd32[b * 16 + r * 4:b * 16 + r * 4 + 3, (r + a) * C:(r + a + 1) * C] = tap

    bias_load.wait()
    bias = bias_ref[...]
    first = iota((WL, C), 0) == 0
    last = iota((WL, C), 0) == WL - 1

    def activate(r6, z0, z1, z2):
        before = jnp.where(first, 0.0, pltpu.roll(z0, 1, 0))
        after = jnp.where(last, 0.0, pltpu.roll(z2, WL - 1, 0))
        for pc, total in ((0, before + z1 + z2), (1, z0 + z1 + after)):
            total = total + bias
            hidden = total * (0.5 + 0.5 * jnp.tanh(0.5 * total))
            if r6 == 0:
                hidden = jnp.where(s > 0, hidden, 0.0)
            elif r6 == 5:
                hidden = jnp.where(s < N_SLAB - 1, hidden, 0.0)
            else:
                gate[pc * WL:(pc + 1) * WL, (r6 - 1) * C:r6 * C] = total
            hbuf[pc * WL:(pc + 1) * WL, r6 * C:(r6 + 1) * C] = hidden.astype(BF16)

    lat_load.wait()
    for copy in w_loads:
        copy.wait()

    for n, r6 in enumerate((2, 3)):
        for a in range(3):
            lcat[n * WL:(n + 1) * WL, a * C:(a + 1) * C] = lat4[lat_row(r6, a)]
    for b in range(3):
        zbuf[b, 0:2 * WL] = dot_nn(lcat[0:2 * WL, :], wb[b])
    for n, r6 in enumerate((2, 3)):
        here = slice(n * WL, (n + 1) * WL)
        activate(r6, zbuf[0, here], zbuf[1, here], zbuf[2, here])
    for b in range(3):
        top, low = lat4[1], lat4[2]
        zbuf[b, 0:WL] = dot_nn(top, wb[b, 2 * C:3 * C])
        zbuf[b, WL:2 * WL] = dot_nn(jnp.concatenate([top, top], axis=1), wb[b, C:3 * C])
        zbuf[b, 2 * WL:3 * WL] = dot_nn(jnp.concatenate([low, low], axis=1), wb[b, 0:2 * C])
        zbuf[b, 3 * WL:4 * WL] = dot_nn(low, wb[b, 0:C])

    guard(s < N_SLAB - 1, up.wait_recv)
    guard(s > 0, down.wait_recv)
    flood_wait(0)
    flood(1)
    for near, far, edge, inner_tap, outer_tap in ((1, 0, 0, 0, 1), (4, 5, 3, 2, 1)):
        halo_row = lat4[edge]
        near_z, far_z = [], []
        for b in range(3):
            one_tap = dot_nn(halo_row, wb[b, inner_tap * C:(inner_tap + 1) * C])
            two_taps = one_tap + dot_nn(halo_row, wb[b, outer_tap * C:(outer_tap + 1) * C])
            n = 0 if near == 1 else 3
            far_z.append(zbuf[b, n * WL:(n + 1) * WL] + two_taps)
            n = 1 if near == 1 else 2
            near_z.append(zbuf[b, n * WL:(n + 1) * WL] + one_tap)
        activate(far, *far_z)
        activate(near, *near_z)

    res = dot_nt(wd32[...].astype(BF16), hbuf[...])
    even, odd = res[:, 0:WL], res[:, WL:2 * WL]
    left = iota((16, WL), 1) == 0
    right = iota((16, WL), 1) == WL - 1
    dec_even = jnp.where(left, 0.0, pltpu.roll(odd[0:16], 1, 1)) + even[16:32] + odd[32:48]
    dec_odd = even[0:16] + odd[16:32] + jnp.where(right, 0.0, pltpu.roll(even[32:48], WL - 1, 1))
    decoded = jnp.concatenate([dec_even, dec_odd], axis=1).astype(BF16)
    dec[...] = decoded
    dall[jnp.where(low_half, q + 4, q)] = decoded

    @pl.when((q == 0) & (p > 0))
    def told():
        pl.semaphore_wait(flood_sem.at[4], 1)

    def gather_send(n, cond, target, slot):
        send(cond, dec, dall.at[slot], gat_ss.at[n], gat_rs.at[slot], f, target)

    for d in range(1, 4):
        qd = (q + d) % 4
        gather_send(d - 1, None, 4 * p + qd, jnp.where(qd < 2, q + 4, q))
    gather_send(3, p < GROUPS - 1, 4 * p + 4, q)
    gather_send(4, p > 0, 4 * p - 1, q + 4)
    gather_send(5, (q == 0) & (p > 0), 4 * p - 4, 8)
    gather_send(6, (q == 0) & (p > 0), 4 * p - 3, 8)
    gather_send(7, (q == 0) & (p > 0), 4 * p - 2, 4)
    gather_send(8, (q == 0) & (p > 1), 4 * p - 5, 8)

    rk = iota((128, 1), 0)
    g = rk & 63
    colour = one(g >= 14) + one(g >= 28)
    ig = jnp.where(rk < 64, p, p2) * PATCH + g - 14 * colour
    valid = (g < 42) & (ig >= 0) & (ig < IMG)
    table_load.wait()
    table = table_ref[...].astype(F32)
    cols = iota((128, IMG), 1)
    lo = jnp.sum(jnp.where(cols == ig, table, 0.0), axis=1, keepdims=True)
    nxt = jnp.sum(jnp.where(cols == ig + 1, table, 0.0), axis=1, keepdims=True)
    nxt = nxt + jnp.where(ig == IMG - 1, 256.0, 0.0)
    hi = jnp.maximum(nxt, lo + 1.0)
    inv = 1.0 / (hi - lo)
    lane = iota((128, 144), 1)
    row = (4 * base + (lane >> 2)).astype(F32)
    inside = valid & ((lane & 3) == colour) & (row >= lo) & (row < hi)
    pick = jnp.where(inside, 1.0, 0.0).astype(BF16)
    lane = iota((128, 128), 1)
    row = (4 * s - 1 + (lane >> 2)).astype(F32)
    inside = valid & ((lane & 3) == colour) & (row >= lo) & (row < hi) & (lane < 24)
    both = jnp.where(lane == 32, inv, jnp.where(inside, 1.0, 0.0)).T
    back = both[0:32].astype(BF16)
    back = jnp.concatenate([back, back], axis=1)
    inv_row = both[32:33]

    pw_load.wait()
    prow = iota((KP, 588), 0)
    pg = prow & 63
    order = jnp.where(
        (pg < 42) & (iota((KP, 588), 1) == 14 * pg + 2 * (prow >> 7) + ((prow >> 6) & 1)), 1.0, 0.0
    ).astype(BF16)
    for n in range(CW // 256):
        cut = slice(n * 256, (n + 1) * 256)
        pwp[:, cut] = dot_nn(order, pw[:, cut]).astype(BF16)

    def gather_wait(slot, cond, source):
        copy = remote(dec, dall.at[slot], gat_ss.at[0], gat_rs.at[slot], f, source)
        pl.when(cond)(copy.wait_recv)

    more = p < GROUPS - 1
    for v in range(4):
        gather_wait(
            v, (low_half & (q == 0) & (p > 0)) | ((q >= 2) & (q != v)),
            jnp.where(low_half, 4 * p - 4 + v, 4 * p + v),
        )
        if v == 0:
            cond = (low_half & (q != v)) | ((q >= 2) & more)
        else:
            cond = (low_half & (q != v)) | ((q == 3) & more)
        gather_wait(v + 4, cond, jnp.where(low_half, 4 * p + v, 4 * p + 4 + v))
    gather_wait(
        8, (low_half & more) | ((q == 3) & (p < GROUPS - 2)),
        jnp.where(low_half, 4 * p + 4, 4 * p + 8),
    )

    flood_wait(1)
    crop = dot_nn(pick, dall[...].reshape(144, 256)) * inv
    ct[...] = crop.T
    lane16 = iota((16, 128), 1) < 64
    pairs = []
    for n in range(7):
        pair = []
        for c14 in (2 * n, 2 * n + 1):
            pc, pj = patch_column(c14)
            pair.append(ct[pl.ds(pc * WL + pj, 16, stride=8), :])
        pairs.append(pair)
    for copy in pos_loads:
        copy.wait()

    def embed(parts, rows):
        patches = jnp.concatenate(parts, axis=1)
        emb = dot_nn(jnp.concatenate(split2(patches), axis=0), pwp[...])
        emb = emb[0:16] + emb[16:32] + pos[rows, :].astype(F32)
        centred = emb - jnp.mean(emb, axis=1, keepdims=True)
        sigma = jnp.sqrt(jnp.mean(centred * centred, axis=1, keepdims=True) + EPS)
        normed = centred / sigma
        ybuf[rows, :] = normed
        return normed, sigma

    normed, sigma0 = embed(
        [jnp.where(lane16, one_, pltpu.roll(two, 64, 1)) for one_, two in pairs], slice(0, 16)
    )
    gsum = jnp.sum(normed, axis=0, keepdims=True)
    psend[...] = gsum
    precv[p] = gsum

    for d in range(1, GROUPS):
        send(
            None, psend, precv.at[p], pool_ss.at[d], pool_rs.at[p],
            f, 4 * ((p + d) % GROUPS) + q,
        )

    sigma1 = embed(
        [jnp.where(lane16, pltpu.roll(one_, 64, 1), two) for one_, two in pairs], slice(16, 32)
    )[1]
    sigma = jnp.concatenate([sigma0, sigma1], axis=0)

    for n in range(4):
        cut = slice(n * C, (n + 1) * C)
        total = gate[:, cut]
        sig = 0.5 + 0.5 * jnp.tanh(0.5 * total)
        gate[:, cut] = sig * (1.0 + total * (1.0 - sig))
    for n in range(4):
        latt[:, n * WL:(n + 1) * WL] = lat4[n].astype(F32).T.astype(BF16)
    text_load.wait()
    text = text_ref[...]
    text2 = jnp.sum(text * text, axis=1, keepdims=True) + 1e-06
    gt[...] = jnp.zeros_like(gt)

    for d in range(1, GROUPS):
        pd = (p + d) % GROUPS
        remote(
            psend, precv.at[pd], pool_ss.at[d], pool_rs.at[pd], f, 4 * pd + q
        ).wait_recv()
    pooled = precv[0]
    for n in range(1, GROUPS):
        pooled = pooled + precv[n]
    pooled = pooled * (1.0 / 256.0)

    proj_load.wait()

    def two_rows(v):
        top = iota((16, v.shape[1]), 0)
        hi_part = v.astype(BF16).astype(F32)
        return jnp.where(top == 0, hi_part, jnp.where(top == 1, v - hi_part, 0.0)).astype(BF16)

    pc_ = pooled - jnp.mean(pooled, axis=1, keepdims=True)
    psigma = jnp.sqrt(jnp.mean(pc_ * pc_, axis=1, keepdims=True) + EPS)
    unit = pc_ / psigma
    projected = jnp.sum(dot_nn(two_rows(unit), proj[...]), axis=0, keepdims=True)
    numer = jnp.sum(projected * text, axis=1, keepdims=True)
    norm2 = jnp.sum(projected * projected, axis=1, keepdims=True) + 1e-06
    scale = 1.0 / jnp.sqrt(norm2 * text2)
    reward = numer * scale
    reward_ref[0] = reward[0, 0]
    dproj = -LOSS_SCALE * (text * scale - projected * (reward / norm2))
    dunit = jnp.sum(dot_nt(two_rows(dproj), proj[...]), axis=0, keepdims=True)

    def norm_back(dy, y, sg):
        m1 = jnp.mean(dy, axis=1, keepdims=True)
        m2 = jnp.mean(dy * y, axis=1, keepdims=True)
        return (dy - m1 - y * m2) / sg

    dpooled = norm_back(dunit, unit, psigma) * (1.0 / 256.0)
    demb = norm_back(dpooled, ybuf[...], sigma)
    dpat = dot_nt(jnp.concatenate(split2(demb), axis=0), pwp[...])
    dpat = dpat[0:32] + dpat[32:64]
    for n in range(7):
        d0 = dpat[0:16, n * 128:(n + 1) * 128]
        d1 = dpat[16:32, n * 128:(n + 1) * 128]
        pair = (
            jnp.where(lane16, d0, pltpu.roll(d1, 64, 1)),
            jnp.where(lane16, pltpu.roll(d0, 64, 1), d1),
        )
        for half in range(2):
            pc, pj = patch_column(2 * n + half)
            gt[pl.ds(pc * WL + pj, 16, stride=8), :] = pair[half]

    grows = jnp.concatenate(split2(gt[...] * inv_row), axis=1)
    image = dot_nt(back, grows).astype(BF16).astype(F32)
    even, odd = image[:, 0:WL], image[:, WL:2 * WL]
    left = iota((32, WL), 1) == 0
    right = iota((32, WL), 1) == WL - 1
    odd_before = jnp.where(left, 0.0, pltpu.roll(odd, 1, 1))
    even_after = jnp.where(right, 0.0, pltpu.roll(even, WL - 1, 1))
    igs[0] = jnp.concatenate([odd, even_after], axis=1)
    igs[1] = image
    igs[2] = jnp.concatenate([odd_before, even], axis=1)

    ims = []
    go = jnp.zeros((48, C), F32)
    for r in range(4):
        im = jnp.concatenate([igs[b, 4 * r:4 * r + 16, :] for b in range(3)], axis=0).astype(BF16)
        ims.append(im)
        go = go + dot_nn(im, hbuf[:, (r + 1) * C:(r + 2) * C])
    for half in range(2):
        go2[half, 27:32, :] = jnp.zeros((5, 128), F32)
        for t in range(9):
            at = (t % 3) * 16 + (2 - t // 3) * 4
            go2[half, 3 * t:3 * t + 3, :] = go[at:at + 3, half * 128:(half + 1) * 128]
    fc = y_hi * 2 + 1 - core
    outk = send(None, go2.at[1 - core], gocr, c_ss.at[3], c_rs.at[3], fc, s)

    wout = wo32[...].astype(BF16)
    cols_of = []
    for r in range(4):
        cg = dot_tn(ims[r], wout) * gate[:, r * C:(r + 1) * C]
        ev, od = cg[0:WL], cg[WL:2 * WL]
        od_before = jnp.where(first, 0.0, pltpu.roll(od, 1, 0))
        ev_after = jnp.where(last, 0.0, pltpu.roll(ev, WL - 1, 0))
        cols_of.append((od + ev_after, ev + od, od_before + ev))

    def put_grad(a, b, value):
        at = (3 * a + b) * C
        for half in range(2):
            part = value[:, half * 128:(half + 1) * 128]
            g32[half, at:at + C, :] = part
            gbf[half, at:at + C, :] = part.astype(BF16)

    outer = [
        jnp.concatenate([cols_of[0][b], cols_of[1][b] + cols_of[2][b], cols_of[3][b]], axis=0)
        .astype(BF16) for b in range(3)
    ]
    inner = [
        jnp.concatenate([cols_of[0][b] + cols_of[1][b], cols_of[2][b] + cols_of[3][b]], axis=0)
        .astype(BF16) for b in range(3)
    ]
    outk.wait_recv()
    gsum_z = go2[core] + gocr[...]
    goz[...] = gsum_z.astype(BF16)
    for d in range(1, 8):
        zd = (z + d) % 8
        send(
            None, goz, gozr.at[z], z_ss.at[0, d], z_rs.at[0, z], f, x * 16 + zd * 2 + y_lo
        )

    main = []
    for a, start, stop, terms in ((0, 0, 3, outer), (1, 1, 3, inner), (2, 1, 4, outer)):
        for b in range(3):
            put_grad(a, b, dot_nn(latt[:, start * WL:stop * WL], terms[b]))
        rows = pl.ds(a * 768, 768)
        main.append(
            send(None, gbf.at[1 - core, rows], gcr.at[rows], c_ss.at[a], c_rs.at[a], fc, s)
        )

    mine = jnp.where(core == 0, x, y)

    def quarter_device(n):
        fd = jnp.where(core == 0, f, (n // 2) * 2 + 1)
        sd = jnp.where(core == 0, n * 16 + z * 2 + y_lo, x * 16 + z * 2 + n % 2)
        return fd, sd

    def halves_sum(half, start, count):
        return g32[half, start:start + count, :] + gcr[start:start + count, :].astype(F32)

    for w in range(4):
        for part in range(2):
            if w == 0 and part == 0:
                main[0].wait_recv()
                main[1].wait_recv()
            elif w == 0:
                main[2].wait_recv()

            @pl.when(core == 0)
            def along_x():
                for n in (2 * part, 2 * part + 1):
                    total = jnp.concatenate(
                        [halves_sum(0, n * 576 + zd * 72, 72) for zd in (w, w + 4)], axis=0
                    )
                    x32[n, w] = total
                    xbf[n, w] = total.astype(BF16)

            @pl.when(core == 1)
            def along_y():
                units = [
                    halves_sum(1, (2 * part + h) * 576 + zd * 72, 72)
                    for zd in (w, w + 4) for h in range(2)
                ]
                for n in range(2):
                    total = jnp.concatenate([u[36 * n:36 * n + 36] for u in units], axis=0)
                    x32[2 * part + n, w] = total
                    xbf[2 * part + n, w] = total.astype(BF16)

            for n in (2 * part, 2 * part + 1):
                send(
                    mine != n, xbf.at[n, w], xr.at[w, mine], u_ss.at[w, n], u_rs.at[w, mine],
                    *quarter_device(n),
                )

    for w in range(4):
        xr[w, mine] = jnp.zeros((144, 128), BF16)
    zr[z] = jnp.zeros((80, 128), BF16)
    for w in range(4):
        for n in range(4):
            copy = remote(
                xbf.at[n, w], xr.at[w, n], u_ss.at[w, n], u_rs.at[w, n], *quarter_device(n)
            )
            guard(mine != n, copy.wait_recv)
        for k in range(2):
            zd = w + 4 * k
            cut = slice(k * 72, (k + 1) * 72)
            total = x32[mine, w, cut, :]
            for n in range(4):
                total = total + xr[w, n, cut, :].astype(F32)
            z32[zd] = total
            zbf[zd] = jnp.concatenate([total, jnp.zeros((8, 128), F32)], axis=0).astype(BF16)
            send(
                z != zd, zbf.at[zd], zr.at[z], z_ss.at[1, zd], z_rs.at[1, z],
                f, x * 16 + zd * 2 + y_lo,
            )
        if w == 1:
            gozr[z] = jnp.zeros((32, 128), BF16)
            for d in range(1, 8):
                zd = (z + d) % 8
                remote(
                    goz, gozr.at[zd], z_ss.at[0, d], z_rs.at[0, zd], f, x * 16 + zd * 2 + y_lo
                ).wait_recv()
            gsum_x = gsum_z + jnp.sum(gozr[...].astype(F32), axis=0)
            gox[...] = gsum_x
            for d in range(1, 4):
                xd = (x + d) % 4
                send(None, gox, goxr.at[x], x_ss.at[d], x_rs.at[x], f, xd * 16 + z * 2 + y_lo)

    goxr[x] = gsum_x
    for d in range(1, 4):
        xd = (x + d) % 4
        remote(
            gox, goxr.at[xd], x_ss.at[d], x_rs.at[xd], f, xd * 16 + z * 2 + y_lo
        ).wait_recv()
    gsum_y = jnp.sum(goxr[...], axis=0)
    goy[...] = gsum_y
    for d in range(1, 8):
        yd = (yc + d) % 8
        send(None, goy, goyr.at[yc], y_ss.at[0, d], y_rs.at[0, yc], *yc_device(yd))
    goyr[yc] = gsum_y

    for d in range(1, 8):
        zd = (z + d) % 8
        remote(
            zbf.at[zd], zr.at[zd], z_ss.at[1, d], z_rs.at[1, zd], f, x * 16 + zd * 2 + y_lo
        ).wait_recv()
    total = z32[z]
    for n in range(8):
        total = total + zr[n, 0:72, :].astype(F32)

    for n in range(2):
        yb[n, 0:36, :] = total[36 * n:36 * n + 36]
        yb[n, 36:40, :] = jnp.zeros((4, 128), F32)
    slot = jnp.where(core == 0, y, 4 + x)
    for n in range(2):
        sd = jnp.where(core == 0, x * 16 + z * 2 + n, (2 * y_hi + n) * 16 + z * 2 + y_lo)
        here = sd == s

        @pl.when(here)
        def keep():
            yr[slot] = yb[n]

        for j in range(4):
            send(
                jnp.logical_not(here & (f == j)), yb.at[n], yr.at[slot],
                y_ss.at[1, 4 * n + j], y_rs.at[1, slot], j, sd,
            )

    for d in range(1, 8):
        yd = (yc + d) % 8
        remote(
            goy, goyr.at[yd], y_ss.at[0, d], y_rs.at[0, yd], *yc_device(yd)
        ).wait_recv()
    for half in range(2):
        total = (goyr[half] + goyr[2 + half]) + (goyr[4 + half] + goyr[6 + half])
        for t in range(9):
            gout_ref[:, t * C + half * 128:t * C + (half + 1) * 128] = total[3 * t:3 * t + 3]
    for half in range(2):
        for n in range(4):
            fd, sd = last_source(4 * half + n)
            copy = remote(
                yb.at[0], yr.at[4 * half + n], y_ss.at[1, 0], y_rs.at[1, 4 * half + n], fd, sd
            )
            guard((fd != f) | (sd != s), copy.wait_recv)
        total = (yr[4 * half] + yr[4 * half + 1]) + (yr[4 * half + 2] + yr[4 * half + 3])
        gconv_ref[:, half * 128:(half + 1) * 128] = total[0:36]

    for cond, copy in sends:
        guard(cond, copy.wait_send)


def per_device(latents, conv_weight, conv_bias, out_weight, row_table, patch_weight, pos_embed,
               proj_weight, text_embed):
    vmem = pl.BlockSpec(memory_space=pltpu.VMEM)
    hbm = pl.BlockSpec(memory_space=pltpu.HBM)
    V = pltpu.VMEM
    dma = pltpu.SemaphoreType.DMA
    reward, gconv, gout = pl.pallas_call(
        kernel,
        out_shape=(
            jax.ShapeDtypeStruct((1,), F32),
            jax.ShapeDtypeStruct((36, C), F32),
            jax.ShapeDtypeStruct((3, 9 * C), F32),
        ),
        in_specs=[hbm] * 9,
        out_specs=(pl.BlockSpec(memory_space=pltpu.SMEM), vmem, vmem),
        scratch_shapes=[
            V((1, C), F32), V((3, 9 * C), BF16), V((1, IMG), jnp.int32), V((1, EMB), F32),
            V((4, WL, C), BF16),
            V((3, 3 * C, C), BF16),
            V((2 * WL, 3 * C), BF16),
            V((3, 4 * WL, C), F32),
            V((2 * WL, 6 * C), BF16),
            V((2 * WL, 4 * C), F32),
            V((48, 6 * C), F32),
            V((48, C), F32),
            V((588, CW), BF16),
            V((KP, CW), BF16),
            V((32, CW), BF16),
            V((CW, EMB), BF16),
            V((16, 256), BF16),
            V((9, 16, 256), BF16),
            V((256, 128), F32),
            V((256, 128), F32),
            V((32, CW), F32),
            V((1, CW), F32),
            V((GROUPS, 1, CW), F32),
            V((3, 32, 256), F32),
            V((C, 4 * WL), BF16),
            V((2, 9 * C, 128), F32),
            V((2, 9 * C, 128), BF16),
            V((9 * C, 128), BF16),
            V((4, 4, 144, 128), BF16),
            V((4, 4, 144, 128), F32),
            V((4, 4, 144, 128), BF16),
            V((8, 80, 128), BF16),
            V((8, 72, 128), F32),
            V((8, 80, 128), BF16),
            V((2, 40, 128), F32),
            V((8, 40, 128), F32),
            V((2, 32, 128), F32),
            V((32, 128), F32),
            V((32, 128), BF16),
            V((8, 32, 128), BF16),
            V((32, 128), F32),
            V((4, 32, 128), F32),
            V((32, 128), F32),
            V((8, 32, 128), F32),
            dma((18,)), dma((2,)), dma((2,)), dma((9,)), dma((9,)), dma((16,)), dma((16,)),
            dma((4,)), dma((4,)), dma((4, 4)), dma((4, 4)), dma((4,)), dma((4,)),
            dma((2, 8)), dma((2, 8)),
            dma((2, 8)), dma((2, 8)), pltpu.SemaphoreType.REGULAR((5,)),
        ],
        compiler_params=pltpu.CompilerParams(
            collective_id=0, has_side_effects=True, vmem_limit_bytes=60 * 1024 * 1024
        ),
    )(
        latents, conv_weight, conv_bias.reshape(1, C), out_weight, row_table, patch_weight,
        pos_embed, proj_weight, text_embed.reshape(1, EMB),
    )
    return reward, gconv, gout


def solution(mesh):
    return jax.shard_map(
        per_device,
        mesh=mesh,
        in_specs=(
            P("frame", "slab", None, None), P(), P(), P(), P("frame", None), P(), P(), P(), P(),
        ),
        out_specs=(P("frame"), P("slab", None), P()),
        check_vma=False,
    )
```

```python
import jax
import jax.numpy as jnp
from jax import lax
from jax.experimental import pallas as pl
from jax.experimental.pallas import tpu as pltpu
from jax.sharding import PartitionSpec as P

MESH = pl.DeviceIdType.MESH
F32 = jnp.float32
BF16 = jnp.bfloat16

C = 256
CW = 1280
EMB = 1024
IMG = 224
PATCH = 14
WL = 128
N_SLAB = 64
GROUPS = 16
KP = 14 * 64
LOSS_SCALE = 256.0
EPS = 1e-05


def dot_nn(a, b):
    return lax.dot_general(a, b, (((1,), (0,)), ((), ())), preferred_element_type=F32)


def dot_nt(a, b):
    return lax.dot_general(a, b, (((1,), (1,)), ((), ())), preferred_element_type=F32)


def dot_tn(a, b):
    return lax.dot_general(a, b, (((0,), (0,)), ((), ())), preferred_element_type=F32)


def iota(shape, dim):
    return lax.broadcasted_iota(jnp.int32, shape, dim)


def split2(v):
    hi = v.astype(BF16)
    lo = (v - hi.astype(F32)).astype(BF16)
    return hi, lo


def lat_row(r6, a):
    return (r6 - 1 + a - 1) // 2 + 1


def patch_column(c14):
    c16 = c14 * 8 // 7
    return c16 % 2, c16 // 2


def kernel(
    lat_hbm, cw_hbm, bias_hbm, ow_hbm, table_hbm, pw_hbm, pos_hbm, proj_hbm, text_hbm,
    reward_ref, gconv_ref, gout_ref,
    bias_ref, ow_ref, table_ref, text_ref,
    lat4, wl, taps, hbuf, gate, wd32, wo32, pw, pwp, pos, proj,
    dec, dall, ct, gt, ybuf, psend, precv, igs, latt,
    g32, gbf, gcr, xbf, x32, xr, zbf, z32, zr, yb, yr,
    go2, gocr, goz, gozr, gox, goxr, goy, goyr,
    loc_sem, halo_ss, halo_rs, gat_ss, gat_rs, pool_ss, pool_rs,
    c_ss, c_rs, u_ss, u_rs, x_ss, x_rs, z_ss, z_rs, y_ss, y_rs, flood_sem,
):
    f = lax.axis_index("frame")
    s = lax.axis_index("slab")
    y_hi, core = f // 2, f % 2
    x, z, y_lo = s // 16, (s % 16) // 2, s % 2
    p, q = s // 4, s % 4
    low_half = q < 2
    base = jnp.where(low_half, 4 * p - 4, 4 * p)
    p2 = jnp.where(low_half, p - 1, p + 1)
    p2c = jnp.clip(p2, 0, GROUPS - 1)

    dall[...] = jnp.zeros_like(dall)
    lat4[0] = jnp.zeros((WL, C), BF16)
    lat4[3] = jnp.zeros((WL, C), BF16)

    barrier = pltpu.get_barrier_semaphore()

    def greet(cond, fd, sd):
        def go():
            pl.semaphore_signal(barrier, inc=1, device_id=(fd, sd), device_id_type=MESH)

        if cond is None:
            go()
        else:
            pl.when(cond)(go)

    greet(s > 0, f, s - 1)
    greet(s < N_SLAB - 1, f, s + 1)
    for d in range(1, 4):
        greet(None, f, 4 * p + (q + d) % 4)
    for v in range(4):
        greet((q == 0) & (p > 0), f, 4 * p - 4 + v)
        greet((q == 3) & (p < GROUPS - 1), f, 4 * p + 4 + v)
    greet((q < 3) & (p < GROUPS - 1), f, 4 * p + 4)
    for d in range(1, 4):
        greet(None, f, ((x + d) % 4) * 16 + z * 2 + y_lo)
    for d in (2, 6):
        greet(None, f, x * 16 + ((z + d) % 8) * 2 + y_lo)
    yc = y_hi * 4 + y_lo * 2 + core

    def yc_device(idx):
        return (idx // 4) * 2 + idx % 2, x * 16 + z * 2 + (idx // 2) % 2

    for d in range(1, 8):
        greet(None, *yc_device((yc + d) % 8))
    y = y_hi * 2 + y_lo

    def one(cond):
        return jnp.where(cond, 1, 0)

    expected = (
        one(s > 0) + one(s < N_SLAB - 1)
        + 3 + one(p < GROUPS - 1) + one(p > 0)
        + one((q == 0) & (p > 0)) * 3
        + 3 + 2 + 7
    )

    loads = []

    def load(src, dst):
        copy = pltpu.make_async_copy(src, dst, loc_sem.at[len(loads)])
        copy.start()
        loads.append(copy)
        return copy

    def load_parts(pairs, whole):
        sem = loc_sem.at[len(loads)]
        for src, dst in pairs:
            pltpu.make_async_copy(src, dst, sem).start()
        copy = pltpu.make_async_copy(whole, whole, sem)
        loads.append(copy)
        return copy

    lat_load = load(lat_hbm.at[0], lat4.at[pl.ds(1, 2)])
    w_load = load_parts(
        [
            (cw_hbm.at[pl.ds(t * C, C)], wl.at[:, pl.ds(t * C, C)])
            for t in range(9)
        ],
        wl,
    )

    pl.semaphore_wait(barrier, expected)

    def flood(stage):
        for n, d in enumerate((2, 6)):
            pl.semaphore_signal(
                flood_sem.at[2 * stage + n], inc=1,
                device_id=(f, x * 16 + ((z + d) % 8) * 2 + y_lo), device_id_type=MESH,
            )

    def flood_wait(stage):
        for n in range(2):
            pl.semaphore_wait(flood_sem.at[2 * stage + n], 1)

    flood(0)

    @pl.when((q == 0) & (p < GROUPS - 1))
    def tell():
        pl.semaphore_signal(
            flood_sem.at[4], inc=1, device_id=(f, s + 4), device_id_type=MESH
        )

    sends = []

    def remote(src, dst, ssem, rsem, fd, sd):
        return pltpu.make_async_remote_copy(
            src_ref=src, dst_ref=dst, send_sem=ssem, recv_sem=rsem,
            device_id=(fd, sd), device_id_type=MESH,
        )

    def guard(cond, action):
        if cond is None:
            action()
        else:
            pl.when(cond)(action)

    def send(cond, *what):
        copy = remote(*what)
        guard(cond, copy.start)
        sends.append((cond, copy))
        return copy

    def send_part(cond, *what):
        guard(cond, remote(*what).start)

    def all_of(whole, ssem, rsem, cond=None):
        copy = remote(whole, whole, ssem, rsem, y_hi * 2 + 1 - core, s)
        sends.append((cond, copy))
        guard(cond, copy.wait_recv)

    up = send(s > 0, lat_hbm.at[0, 0], lat4.at[3], halo_ss.at[0], halo_rs.at[1], f, s - 1)
    down = send(
        s < N_SLAB - 1, lat_hbm.at[0, 1], lat4.at[0], halo_ss.at[1], halo_rs.at[0], f, s + 1
    )

    ow_load = load(ow_hbm, ow_ref)
    bias_load = load(bias_hbm, bias_ref)
    table_load = load(table_hbm, table_ref)
    text_load = load(text_hbm, text_ref)
    pw_load = load(pw_hbm, pw)
    pos_load = load_parts(
        [
            (pos_hbm.at[pl.ds(pl.multiple_of(16 * p, 16), 16)], pos.at[pl.ds(0, 16)]),
            (pos_hbm.at[pl.ds(pl.multiple_of(16 * p2c, 16), 16)], pos.at[pl.ds(16, 16)]),
        ],
        pos,
    )
    proj_load = load(proj_hbm, proj)

    wd32[...] = jnp.zeros_like(wd32)
    wo32[...] = jnp.zeros_like(wo32)
    ow_load.wait()
    for a in range(3):
        for b in range(3):
            t = 3 * a + b
            tap = ow_ref[:, t * C:(t + 1) * C].astype(F32)
            wo32[b * 16 + (2 - a) * 4:b * 16 + (2 - a) * 4 + 3, :] = tap
            for r in range(4):
                wd32[b * 16 + r * 4:b * 16 + r * 4 + 3, (r + a) * C:(r + a + 1) * C] = tap

    bias_load.wait()
    bias = bias_ref[...]
    first = iota((WL, C), 0) == 0
    last = iota((WL, C), 0) == WL - 1

    def activate(r6, z0, z1, z2):
        before = jnp.where(first, 0.0, pltpu.roll(z0, 1, 0))
        after = jnp.where(last, 0.0, pltpu.roll(z2, WL - 1, 0))
        for pc, total in ((0, before + z1 + z2), (1, z0 + z1 + after)):
            total = total + bias
            hidden = total * (0.5 + 0.5 * jnp.tanh(0.5 * total))
            if r6 == 0:
                hidden = jnp.where(s > 0, hidden, 0.0)
            elif r6 == 5:
                hidden = jnp.where(s < N_SLAB - 1, hidden, 0.0)
            else:
                gate[pc * WL:(pc + 1) * WL, (r6 - 1) * C:r6 * C] = total
            hbuf[pc * WL:(pc + 1) * WL, r6 * C:(r6 + 1) * C] = hidden.astype(BF16)

    lat_load.wait()
    w_load.wait()

    taps[...] = dot_nn(lat4[1:3].reshape(2 * WL, C), wl[...])

    def part(row, a, b):
        t = 3 * a + b
        return taps[(row - 1) * WL:row * WL, t * C:(t + 1) * C]

    def own_terms(r6, b):
        rows = [(lat_row(r6, a), a) for a in range(3)]
        return sum(part(row, a, b) for row, a in rows if row in (1, 2))

    for r6 in (2, 3):
        activate(r6, *[own_terms(r6, b) for b in range(3)])

    guard(s < N_SLAB - 1, up.wait_recv)
    guard(s > 0, down.wait_recv)
    flood_wait(0)
    flood(1)
    for near, far, edge, start in ((1, 0, 0, 0), (4, 5, 3, 3)):
        halo_z = dot_nn(lat4[edge], wl[:, start * C:(start + 6) * C])
        inner = [halo_z[:, (b if near == 1 else b + 3) * C:][:, 0:C] for b in range(3)]
        outer = [halo_z[:, (b + 3 if near == 1 else b) * C:][:, 0:C] for b in range(3)]
        activate(near, *[own_terms(near, b) + inner[b] for b in range(3)])
        activate(far, *[own_terms(far, b) + (inner[b] + outer[b]) for b in range(3)])

    res = dot_nt(wd32[...].astype(BF16), hbuf[...])
    even, odd = res[:, 0:WL], res[:, WL:2 * WL]
    left = iota((16, WL), 1) == 0
    right = iota((16, WL), 1) == WL - 1
    dec_even = jnp.where(left, 0.0, pltpu.roll(odd[0:16], 1, 1)) + even[16:32] + odd[32:48]
    dec_odd = even[0:16] + odd[16:32] + jnp.where(right, 0.0, pltpu.roll(even[32:48], WL - 1, 1))
    decoded = jnp.concatenate([dec_even, dec_odd], axis=1).astype(BF16)
    dec[...] = decoded
    dall[jnp.where(low_half, q + 4, q)] = decoded

    @pl.when((q == 0) & (p > 0))
    def told():
        pl.semaphore_wait(flood_sem.at[4], 1)

    def gather_send(n, cond, target, slot):
        send(cond, dec, dall.at[slot], gat_ss.at[n], gat_rs.at[slot], f, target)

    for d in range(1, 4):
        qd = (q + d) % 4
        gather_send(d - 1, None, 4 * p + qd, jnp.where(qd < 2, q + 4, q))
    gather_send(3, p < GROUPS - 1, 4 * p + 4, q)
    gather_send(4, p > 0, 4 * p - 1, q + 4)
    gather_send(5, (q == 0) & (p > 0), 4 * p - 4, 8)
    gather_send(6, (q == 0) & (p > 0), 4 * p - 3, 8)
    gather_send(7, (q == 0) & (p > 0), 4 * p - 2, 4)
    gather_send(8, (q == 0) & (p > 1), 4 * p - 5, 8)

    rk = iota((128, 1), 0)
    g = rk & 63
    colour = one(g >= 14) + one(g >= 28)
    ig = jnp.where(rk < 64, p, p2) * PATCH + g - 14 * colour
    valid = (g < 42) & (ig >= 0) & (ig < IMG)
    table_load.wait()
    table = table_ref[...].astype(F32)
    cols = iota((128, IMG), 1)
    lo = jnp.sum(jnp.where(cols == ig, table, 0.0), axis=1, keepdims=True)
    nxt = jnp.sum(jnp.where(cols == ig + 1, table, 0.0), axis=1, keepdims=True)
    nxt = nxt + jnp.where(ig == IMG - 1, 256.0, 0.0)
    hi = jnp.maximum(nxt, lo + 1.0)
    inv = 1.0 / (hi - lo)
    lane = iota((128, 144), 1)
    row = (4 * base + (lane >> 2)).astype(F32)
    inside = valid & ((lane & 3) == colour) & (row >= lo) & (row < hi)
    pick = jnp.where(inside, 1.0, 0.0).astype(BF16)
    lane = iota((128, 128), 1)
    row = (4 * s - 1 + (lane >> 2)).astype(F32)
    inside = valid & ((lane & 3) == colour) & (row >= lo) & (row < hi) & (lane < 24)
    both = jnp.where(lane == 32, inv, jnp.where(inside, 1.0, 0.0)).T
    back = both[0:32].astype(BF16)
    back = jnp.concatenate([back, back], axis=1)
    inv_row = both[32:33]

    pw_load.wait()
    prow = iota((KP, 588), 0)
    pg = prow & 63
    order = jnp.where(
        (pg < 42) & (iota((KP, 588), 1) == 14 * pg + 2 * (prow >> 7) + ((prow >> 6) & 1)), 1.0, 0.0
    ).astype(BF16)
    for n in range(CW // 256):
        cut = slice(n * 256, (n + 1) * 256)
        pwp[:, cut] = dot_nn(order, pw[:, cut]).astype(BF16)

    def gather_wait(slot, cond, source):
        copy = remote(dec, dall.at[slot], gat_ss.at[0], gat_rs.at[slot], f, source)
        pl.when(cond)(copy.wait_recv)

    more = p < GROUPS - 1
    for v in range(4):
        gather_wait(
            v, (low_half & (q == 0) & (p > 0)) | ((q >= 2) & (q != v)),
            jnp.where(low_half, 4 * p - 4 + v, 4 * p + v),
        )
        if v == 0:
            cond = (low_half & (q != v)) | ((q >= 2) & more)
        else:
            cond = (low_half & (q != v)) | ((q == 3) & more)
        gather_wait(v + 4, cond, jnp.where(low_half, 4 * p + v, 4 * p + 4 + v))
    gather_wait(
        8, (low_half & more) | ((q == 3) & (p < GROUPS - 2)),
        jnp.where(low_half, 4 * p + 4, 4 * p + 8),
    )

    flood_wait(1)
    crop = dot_nn(pick, dall[...].reshape(144, 256)) * inv
    ct[...] = crop.T
    lane16 = iota((16, 128), 1) < 64
    pairs = []
    for n in range(7):
        pair = []
        for c14 in (2 * n, 2 * n + 1):
            pc, pj = patch_column(c14)
            pair.append(ct[pl.ds(pc * WL + pj, 16, stride=8), :])
        pairs.append(pair)
    pos_load.wait()

    def embed(parts, rows):
        patches = jnp.concatenate(parts, axis=1)
        emb = dot_nn(jnp.concatenate(split2(patches), axis=0), pwp[...])
        emb = emb[0:16] + emb[16:32] + pos[rows, :].astype(F32)
        centred = emb - jnp.mean(emb, axis=1, keepdims=True)
        sigma = jnp.sqrt(jnp.mean(centred * centred, axis=1, keepdims=True) + EPS)
        normed = centred / sigma
        ybuf[rows, :] = normed
        return normed, sigma

    normed, sigma0 = embed(
        [jnp.where(lane16, one_, pltpu.roll(two, 64, 1)) for one_, two in pairs], slice(0, 16)
    )
    gsum = jnp.sum(normed, axis=0, keepdims=True)
    psend[...] = gsum
    precv[p] = gsum

    for d in range(1, GROUPS):
        send_part(
            None, psend, precv.at[p], pool_ss.at[0], pool_rs.at[0], f, 4 * ((p + d) % GROUPS) + q
        )

    sigma1 = embed(
        [jnp.where(lane16, pltpu.roll(one_, 64, 1), two) for one_, two in pairs], slice(16, 32)
    )[1]
    sigma = jnp.concatenate([sigma0, sigma1], axis=0)

    for n in range(4):
        cut = slice(n * C, (n + 1) * C)
        total = gate[:, cut]
        sig = 0.5 + 0.5 * jnp.tanh(0.5 * total)
        gate[:, cut] = sig * (1.0 + total * (1.0 - sig))
    for n in range(4):
        latt[:, n * WL:(n + 1) * WL] = lat4[n].astype(F32).T.astype(BF16)
    text_load.wait()
    text = text_ref[...]
    text2 = jnp.sum(text * text, axis=1, keepdims=True) + 1e-06
    gt[...] = jnp.zeros_like(gt)

    all_of(precv.at[pl.ds(0, GROUPS - 1)], pool_ss.at[0], pool_rs.at[0])
    pooled = precv[0]
    for n in range(1, GROUPS):
        pooled = pooled + precv[n]
    pooled = pooled * (1.0 / 256.0)

    proj_load.wait()

    def two_rows(v):
        top = iota((16, v.shape[1]), 0)
        hi_part = v.astype(BF16).astype(F32)
        return jnp.where(top == 0, hi_part, jnp.where(top == 1, v - hi_part, 0.0)).astype(BF16)

    pc_ = pooled - jnp.mean(pooled, axis=1, keepdims=True)
    psigma = jnp.sqrt(jnp.mean(pc_ * pc_, axis=1, keepdims=True) + EPS)
    unit = pc_ / psigma
    projected = jnp.sum(dot_nn(two_rows(unit), proj[...]), axis=0, keepdims=True)
    numer = jnp.sum(projected * text, axis=1, keepdims=True)
    norm2 = jnp.sum(projected * projected, axis=1, keepdims=True) + 1e-06
    scale = 1.0 / jnp.sqrt(norm2 * text2)
    reward = numer * scale
    reward_ref[...] = reward
    dproj = -LOSS_SCALE * (text * scale - projected * (reward / norm2))
    dunit = jnp.sum(dot_nt(two_rows(dproj), proj[...]), axis=0, keepdims=True)

    def norm_back(dy, y, sg):
        m1 = jnp.mean(dy, axis=1, keepdims=True)
        m2 = jnp.mean(dy * y, axis=1, keepdims=True)
        return (dy - m1 - y * m2) / sg

    dpooled = norm_back(dunit, unit, psigma) * (1.0 / 256.0)
    demb = norm_back(dpooled, ybuf[...], sigma)
    dpat = dot_nt(jnp.concatenate(split2(demb), axis=0), pwp[...])
    dpat = dpat[0:32] + dpat[32:64]
    for n in range(7):
        d0 = dpat[0:16, n * 128:(n + 1) * 128]
        d1 = dpat[16:32, n * 128:(n + 1) * 128]
        pair = (
            jnp.where(lane16, d0, pltpu.roll(d1, 64, 1)),
            jnp.where(lane16, pltpu.roll(d0, 64, 1), d1),
        )
        for half in range(2):
            pc, pj = patch_column(2 * n + half)
            gt[pl.ds(pc * WL + pj, 16, stride=8), :] = pair[half]

    grows = jnp.concatenate(split2(gt[...] * inv_row), axis=1)
    image = dot_nt(back, grows).astype(BF16).astype(F32)
    even, odd = image[:, 0:WL], image[:, WL:2 * WL]
    left = iota((32, WL), 1) == 0
    right = iota((32, WL), 1) == WL - 1
    odd_before = jnp.where(left, 0.0, pltpu.roll(odd, 1, 1))
    even_after = jnp.where(right, 0.0, pltpu.roll(even, WL - 1, 1))
    igs[0] = jnp.concatenate([odd, even_after], axis=1)
    igs[1] = image
    igs[2] = jnp.concatenate([odd_before, even], axis=1)

    ims = []
    go = jnp.zeros((48, C), F32)
    for r in range(4):
        im = jnp.concatenate([igs[b, 4 * r:4 * r + 16, :] for b in range(3)], axis=0).astype(BF16)
        ims.append(im)
        go = go + dot_nn(im, hbuf[:, (r + 1) * C:(r + 2) * C])
    for half in range(2):
        go2[half, 27:32, :] = jnp.zeros((5, 128), F32)
        for t in range(9):
            at = (t % 3) * 16 + (2 - t // 3) * 4
            go2[half, 3 * t:3 * t + 3, :] = go[at:at + 3, half * 128:(half + 1) * 128]
    fc = y_hi * 2 + 1 - core
    outk = send(None, go2.at[1 - core], gocr, c_ss.at[3], c_rs.at[3], fc, s)

    wout = wo32[...].astype(BF16)
    cols_of = []
    for r in range(4):
        cg = dot_tn(ims[r], wout) * gate[:, r * C:(r + 1) * C]
        ev, od = cg[0:WL], cg[WL:2 * WL]
        od_before = jnp.where(first, 0.0, pltpu.roll(od, 1, 0))
        ev_after = jnp.where(last, 0.0, pltpu.roll(ev, WL - 1, 0))
        cols_of.append((od + ev_after, ev + od, od_before + ev))

    def put_grad(a, b, value):
        at = (3 * a + b) * C
        for half in range(2):
            part = value[:, half * 128:(half + 1) * 128]
            g32[half, at:at + C, :] = part
            gbf[half, at:at + C, :] = part.astype(BF16)

    outer = [
        jnp.concatenate([cols_of[0][b], cols_of[1][b] + cols_of[2][b], cols_of[3][b]], axis=0)
        .astype(BF16) for b in range(3)
    ]
    inner = [
        jnp.concatenate([cols_of[0][b] + cols_of[1][b], cols_of[2][b] + cols_of[3][b]], axis=0)
        .astype(BF16) for b in range(3)
    ]
    outk.wait_recv()
    gsum_z = go2[core] + gocr[...]
    goz[...] = gsum_z.astype(BF16)
    for d in range(1, 8):
        zd = (z + d) % 8
        send_part(None, goz, gozr.at[z], z_ss.at[0], z_rs.at[0], f, x * 16 + zd * 2 + y_lo)

    main = []
    for a, start, stop, terms in ((0, 0, 3, outer), (1, 1, 3, inner), (2, 1, 4, outer)):
        for b in range(3):
            put_grad(a, b, dot_nn(latt[:, start * WL:stop * WL], terms[b]))
        rows = pl.ds(a * 768, 768)
        main.append(
            send(None, gbf.at[1 - core, rows], gcr.at[rows], c_ss.at[a], c_rs.at[a], fc, s)
        )

    mine = jnp.where(core == 0, x, y)

    def quarter_device(n):
        fd = jnp.where(core == 0, f, (n // 2) * 2 + 1)
        sd = jnp.where(core == 0, n * 16 + z * 2 + y_lo, x * 16 + z * 2 + n % 2)
        return fd, sd

    def halves_sum(half, start, count):
        return g32[half, start:start + count, :] + gcr[start:start + count, :].astype(F32)

    for w in range(4):
        for part in range(2):
            if w == 0 and part == 0:
                main[0].wait_recv()
                main[1].wait_recv()
            elif w == 0:
                main[2].wait_recv()

            @pl.when(core == 0)
            def along_x():
                for n in (2 * part, 2 * part + 1):
                    total = jnp.concatenate(
                        [halves_sum(0, n * 576 + zd * 72, 72) for zd in (w, w + 4)], axis=0
                    )
                    x32[n, w] = total
                    xbf[n, w] = total.astype(BF16)

            @pl.when(core == 1)
            def along_y():
                units = [
                    halves_sum(1, (2 * part + h) * 576 + zd * 72, 72)
                    for zd in (w, w + 4) for h in range(2)
                ]
                for n in range(2):
                    total = jnp.concatenate([u[36 * n:36 * n + 36] for u in units], axis=0)
                    x32[2 * part + n, w] = total
                    xbf[2 * part + n, w] = total.astype(BF16)

            for n in (2 * part, 2 * part + 1):
                send_part(
                    mine != n, xbf.at[n, w], xr.at[w, mine], u_ss.at[w], u_rs.at[w],
                    *quarter_device(n),
                )

    for w in range(4):
        xr[w, mine] = jnp.zeros((144, 128), BF16)
    zr[z] = jnp.zeros((80, 128), BF16)
    for w in range(4):
        all_of(xr.at[w, pl.ds(0, 3)], u_ss.at[w], u_rs.at[w])
        for k in range(2):
            zd = w + 4 * k
            cut = slice(k * 72, (k + 1) * 72)
            total = x32[mine, w, cut, :]
            for n in range(4):
                total = total + xr[w, n, cut, :].astype(F32)
            z32[zd] = total
            zbf[zd] = jnp.concatenate([total, jnp.zeros((8, 128), F32)], axis=0).astype(BF16)
            send_part(
                z != zd, zbf.at[zd], zr.at[z], z_ss.at[1], z_rs.at[1], f, x * 16 + zd * 2 + y_lo
            )
        if w == 1:
            gozr[z] = jnp.zeros((32, 128), BF16)
            all_of(gozr.at[pl.ds(0, 7)], z_ss.at[0], z_rs.at[0])
            gsum_x = gsum_z + jnp.sum(gozr[...].astype(F32), axis=0)
            gox[...] = gsum_x
            for d in range(1, 4):
                xd = (x + d) % 4
                send_part(
                    None, gox, goxr.at[x], x_ss.at[0], x_rs.at[0], f, xd * 16 + z * 2 + y_lo
                )

    goxr[x] = gsum_x
    all_of(goxr.at[pl.ds(0, 3)], x_ss.at[0], x_rs.at[0])
    gsum_y = jnp.sum(goxr[...], axis=0)
    goy[...] = gsum_y
    for d in range(1, 8):
        yd = (yc + d) % 8
        send_part(None, goy, goyr.at[yc], y_ss.at[0], y_rs.at[0], *yc_device(yd))
    goyr[yc] = gsum_y

    all_of(zr.at[pl.ds(0, 7)], z_ss.at[1], z_rs.at[1])
    total = z32[z]
    for n in range(8):
        total = total + zr[n, 0:72, :].astype(F32)

    for n in range(2):
        yb[n, 0:36, :] = total[36 * n:36 * n + 36]
        yb[n, 36:40, :] = jnp.zeros((4, 128), F32)
    slot = jnp.where(core == 0, y, 4 + x)
    for n in range(2):
        sd = jnp.where(core == 0, x * 16 + z * 2 + n, (2 * y_hi + n) * 16 + z * 2 + y_lo)
        here = sd == s

        @pl.when(here)
        def keep():
            yr[slot] = yb[n]

        for j in range(4):
            send_part(
                jnp.logical_not(here & (f == j)), yb.at[n], yr.at[slot],
                y_ss.at[1], y_rs.at[1], j, sd,
            )

    all_of(goyr.at[pl.ds(0, 7)], y_ss.at[0], y_rs.at[0])
    for half in range(2):
        total = (goyr[half] + goyr[2 + half]) + (goyr[4 + half] + goyr[6 + half])
        for t in range(9):
            gout_ref[:, t * C + half * 128:t * C + (half + 1) * 128] = total[3 * t:3 * t + 3]
    seven = (core == 0) | (x // 2 == y_hi)
    all_of(yr.at[pl.ds(0, 7)], y_ss.at[1], y_rs.at[1], seven)
    all_of(yr, y_ss.at[1], y_rs.at[1], jnp.logical_not(seven))
    for half in range(2):
        total = (yr[4 * half] + yr[4 * half + 1]) + (yr[4 * half + 2] + yr[4 * half + 3])
        gconv_ref[:, half * 128:(half + 1) * 128] = total[0:36]

    for cond, copy in sends:
        guard(cond, copy.wait_send)


def per_device(latents, conv_weight, conv_bias, out_weight, row_table, patch_weight, pos_embed,
               proj_weight, text_embed):
    vmem = pl.BlockSpec(memory_space=pltpu.VMEM)
    hbm = pl.BlockSpec(memory_space=pltpu.HBM)
    V = pltpu.VMEM
    dma = pltpu.SemaphoreType.DMA
    reward, gconv, gout = pl.pallas_call(
        kernel,
        out_shape=(
            jax.ShapeDtypeStruct((1, 1), F32),
            jax.ShapeDtypeStruct((36, C), F32),
            jax.ShapeDtypeStruct((3, 9 * C), F32),
        ),
        in_specs=[hbm] * 9,
        out_specs=(vmem, vmem, vmem),
        scratch_shapes=[
            V((1, C), F32), V((3, 9 * C), BF16), V((1, IMG), jnp.int32), V((1, EMB), F32),
            V((4, WL, C), BF16),
            V((C, 9 * C), BF16),
            V((2 * WL, 9 * C), F32),
            V((2 * WL, 6 * C), BF16),
            V((2 * WL, 4 * C), F32),
            V((48, 6 * C), F32),
            V((48, C), F32),
            V((588, CW), BF16),
            V((KP, CW), BF16),
            V((32, CW), BF16),
            V((CW, EMB), BF16),
            V((16, 256), BF16),
            V((9, 16, 256), BF16),
            V((256, 128), F32),
            V((256, 128), F32),
            V((32, CW), F32),
            V((1, CW), F32),
            V((GROUPS, 1, CW), F32),
            V((3, 32, 256), F32),
            V((C, 4 * WL), BF16),
            V((2, 9 * C, 128), F32),
            V((2, 9 * C, 128), BF16),
            V((9 * C, 128), BF16),
            V((4, 4, 144, 128), BF16),
            V((4, 4, 144, 128), F32),
            V((4, 4, 144, 128), BF16),
            V((8, 80, 128), BF16),
            V((8, 72, 128), F32),
            V((8, 80, 128), BF16),
            V((2, 40, 128), F32),
            V((8, 40, 128), F32),
            V((2, 32, 128), F32),
            V((32, 128), F32),
            V((32, 128), BF16),
            V((8, 32, 128), BF16),
            V((32, 128), F32),
            V((4, 32, 128), F32),
            V((32, 128), F32),
            V((8, 32, 128), F32),
            dma((9,)), dma((2,)), dma((2,)), dma((9,)), dma((9,)), dma((1,)), dma((1,)),
            dma((4,)), dma((4,)), dma((4,)), dma((4,)), dma((1,)), dma((1,)),
            dma((2,)), dma((2,)), dma((2,)), dma((2,)), pltpu.SemaphoreType.REGULAR((5,)),
        ],
        compiler_params=pltpu.CompilerParams(
            collective_id=0, has_side_effects=True, vmem_limit_bytes=60 * 1024 * 1024
        ),
    )(
        latents, conv_weight, conv_bias.reshape(1, C), out_weight, row_table, patch_weight,
        pos_embed, proj_weight, text_embed.reshape(1, EMB),
    )
    return reward.reshape(1), gconv, gout


def solution(mesh):
    return jax.shard_map(
        per_device,
        mesh=mesh,
        in_specs=(
            P("frame", "slab", None, None), P(), P(), P(), P("frame", None), P(), P(), P(), P(),
        ),
        out_specs=(P("frame"), P("slab", None), P()),
        check_vma=False,
    )
```

```python
import jax
import jax.numpy as jnp
from jax import lax
from jax.experimental import pallas as pl
from jax.experimental.pallas import tpu as pltpu
from jax.sharding import PartitionSpec as P

MESH = pl.DeviceIdType.MESH
F32 = jnp.float32
BF16 = jnp.bfloat16

C = 256
CW = 1280
EMB = 1024
IMG = 224
PATCH = 14
WL = 128
N_SLAB = 64
GROUPS = 16
KP = 14 * 64
LOSS_SCALE = 256.0
EPS = 1e-05


def dot_nn(a, b):
    return lax.dot_general(a, b, (((1,), (0,)), ((), ())), preferred_element_type=F32)


def dot_nt(a, b):
    return lax.dot_general(a, b, (((1,), (1,)), ((), ())), preferred_element_type=F32)


def dot_tn(a, b):
    return lax.dot_general(a, b, (((0,), (0,)), ((), ())), preferred_element_type=F32)


def iota(shape, dim):
    return lax.broadcasted_iota(jnp.int32, shape, dim)


def split2(v):
    hi = v.astype(BF16)
    lo = (v - hi.astype(F32)).astype(BF16)
    return hi, lo


def lat_row(r6, a):
    return (r6 - 1 + a - 1) // 2 + 1


def patch_column(c14):
    c16 = c14 * 8 // 7
    return c16 % 2, c16 // 2


def kernel(
    lat_hbm, cw_hbm, bias_hbm, ow_hbm, table_hbm, pw_hbm, pos_hbm, proj_hbm, text_hbm,
    reward_ref, gconv_ref, gout_ref,
    bias_ref, ow_ref, table_ref, text_ref,
    lat4, wl, taps, hbuf, gate, wd32, wo32, pw, pwp, pos, proj,
    dec, dall, ct, ct2, gt, ybuf, psend, precv, igs, latt,
    g32, gbf, gcr, xbf, x32, xr, zbf, z32, zr, yb, yr,
    go2, gocr, goz, gozr, gox, goxr, goy, goyr,
    loc_sem, halo_ss, halo_rs, gat_ss, gat_rs, pool_ss, pool_rs,
    c_ss, c_rs, u_ss, u_rs, x_ss, x_rs, z_ss, z_rs, y_ss, y_rs, flood_sem,
):
    f = lax.axis_index("frame")
    s = lax.axis_index("slab")
    y_hi, core = f // 2, f % 2
    x, z, y_lo = s // 16, (s % 16) // 2, s % 2
    p, q = s // 4, s % 4
    low_half = q < 2
    base = jnp.where(low_half, 4 * p - 4, 4 * p)
    p2 = jnp.where(low_half, p - 1, p + 1)
    p2c = jnp.clip(p2, 0, GROUPS - 1)

    dall[...] = jnp.zeros_like(dall)
    lat4[0] = jnp.zeros((WL, C), BF16)
    lat4[3] = jnp.zeros((WL, C), BF16)

    barrier = pltpu.get_barrier_semaphore()

    def greet(cond, fd, sd):
        def go():
            pl.semaphore_signal(barrier, inc=1, device_id=(fd, sd), device_id_type=MESH)

        if cond is None:
            go()
        else:
            pl.when(cond)(go)

    greet(s > 0, f, s - 1)
    greet(s < N_SLAB - 1, f, s + 1)
    for d in range(1, 4):
        greet(None, f, 4 * p + (q + d) % 4)
    for v in range(4):
        greet((q == 0) & (p > 0), f, 4 * p - 4 + v)
        greet((q == 3) & (p < GROUPS - 1), f, 4 * p + 4 + v)
    greet((q < 3) & (p < GROUPS - 1), f, 4 * p + 4)
    for d in range(1, 4):
        greet(None, f, ((x + d) % 4) * 16 + z * 2 + y_lo)
    for d in (2, 6):
        greet(None, f, x * 16 + ((z + d) % 8) * 2 + y_lo)
    yc = y_hi * 4 + y_lo * 2 + core

    def yc_device(idx):
        return (idx // 4) * 2 + idx % 2, x * 16 + z * 2 + (idx // 2) % 2

    for d in range(1, 8):
        greet(None, *yc_device((yc + d) % 8))
    y = y_hi * 2 + y_lo

    def one(cond):
        return jnp.where(cond, 1, 0)

    expected = (
        one(s > 0) + one(s < N_SLAB - 1)
        + 3 + one(p < GROUPS - 1) + one(p > 0)
        + one((q == 0) & (p > 0)) * 3
        + 3 + 2 + 7
    )

    loads = []

    def load(src, dst):
        copy = pltpu.make_async_copy(src, dst, loc_sem.at[len(loads)])
        copy.start()
        loads.append(copy)
        return copy

    def load_parts(pairs, whole):
        sem = loc_sem.at[len(loads)]
        for src, dst in pairs:
            pltpu.make_async_copy(src, dst, sem).start()
        copy = pltpu.make_async_copy(whole, whole, sem)
        loads.append(copy)
        return copy

    lat_load = load(lat_hbm.at[0], lat4.at[pl.ds(1, 2)])
    w_load = load_parts(
        [
            (cw_hbm.at[pl.ds(t * C, C)], wl.at[:, pl.ds(t * C, C)])
            for t in range(9)
        ],
        wl,
    )

    pl.semaphore_wait(barrier, expected)

    def flood(stage):
        for n, d in enumerate((2, 6)):
            pl.semaphore_signal(
                flood_sem.at[2 * stage + n], inc=1,
                device_id=(f, x * 16 + ((z + d) % 8) * 2 + y_lo), device_id_type=MESH,
            )

    def flood_wait(stage):
        for n in range(2):
            pl.semaphore_wait(flood_sem.at[2 * stage + n], 1)

    flood(0)

    @pl.when((q == 0) & (p < GROUPS - 1))
    def tell():
        pl.semaphore_signal(
            flood_sem.at[4], inc=1, device_id=(f, s + 4), device_id_type=MESH
        )

    sends = []

    def remote(src, dst, ssem, rsem, fd, sd):
        return pltpu.make_async_remote_copy(
            src_ref=src, dst_ref=dst, send_sem=ssem, recv_sem=rsem,
            device_id=(fd, sd), device_id_type=MESH,
        )

    def guard(cond, action):
        if cond is None:
            action()
        else:
            pl.when(cond)(action)

    def send(cond, *what):
        copy = remote(*what)
        guard(cond, copy.start)
        sends.append((cond, copy))
        return copy

    def send_part(cond, *what):
        guard(cond, remote(*what).start)

    def all_of(whole, ssem, rsem, cond=None):
        copy = remote(whole, whole, ssem, rsem, y_hi * 2 + 1 - core, s)
        sends.append((cond, copy))
        guard(cond, copy.wait_recv)

    up = send(s > 0, lat_hbm.at[0, 0], lat4.at[3], halo_ss.at[0], halo_rs.at[1], f, s - 1)
    down = send(
        s < N_SLAB - 1, lat_hbm.at[0, 1], lat4.at[0], halo_ss.at[1], halo_rs.at[0], f, s + 1
    )

    ow_load = load(ow_hbm, ow_ref)
    bias_load = load(bias_hbm, bias_ref)
    table_load = load(table_hbm, table_ref)
    text_load = load(text_hbm, text_ref)
    pw_load = load(pw_hbm, pw)
    pos_load = load_parts(
        [
            (pos_hbm.at[pl.ds(pl.multiple_of(16 * p, 16), 16)], pos.at[pl.ds(0, 16)]),
            (pos_hbm.at[pl.ds(pl.multiple_of(16 * p2c, 16), 16)], pos.at[pl.ds(16, 16)]),
        ],
        pos,
    )
    proj_load = load(proj_hbm, proj)

    wd32[...] = jnp.zeros_like(wd32)
    wo32[...] = jnp.zeros_like(wo32)
    ow_load.wait()
    for a in range(3):
        for b in range(3):
            t = 3 * a + b
            tap = ow_ref[:, t * C:(t + 1) * C].astype(F32)
            wo32[b * 16 + (2 - a) * 4:b * 16 + (2 - a) * 4 + 3, :] = tap
            for r in range(4):
                wd32[b * 16 + r * 4:b * 16 + r * 4 + 3, (r + a) * C:(r + a + 1) * C] = tap

    bias_load.wait()
    bias = bias_ref[...]
    first = iota((WL, C), 0) == 0
    last = iota((WL, C), 0) == WL - 1

    def activate(r6, z0, z1, z2):
        before = jnp.where(first, 0.0, pltpu.roll(z0, 1, 0))
        after = jnp.where(last, 0.0, pltpu.roll(z2, WL - 1, 0))
        for pc, total in ((0, before + z1 + z2), (1, z0 + z1 + after)):
            total = total + bias
            hidden = total * (0.5 + 0.5 * jnp.tanh(0.5 * total))
            if r6 == 0:
                hidden = jnp.where(s > 0, hidden, 0.0)
            elif r6 == 5:
                hidden = jnp.where(s < N_SLAB - 1, hidden, 0.0)
            else:
                gate[pc * WL:(pc + 1) * WL, (r6 - 1) * C:r6 * C] = total
            hbuf[pc * WL:(pc + 1) * WL, r6 * C:(r6 + 1) * C] = hidden.astype(BF16)

    lat_load.wait()
    w_load.wait()

    taps[...] = dot_nn(lat4[1:3].reshape(2 * WL, C), wl[...])

    def part(row, a, b):
        t = 3 * a + b
        return taps[(row - 1) * WL:row * WL, t * C:(t + 1) * C]

    def own_terms(r6, b):
        rows = [(lat_row(r6, a), a) for a in range(3)]
        return sum(part(row, a, b) for row, a in rows if row in (1, 2))

    for r6 in (2, 3):
        activate(r6, *[own_terms(r6, b) for b in range(3)])

    guard(s < N_SLAB - 1, up.wait_recv)
    guard(s > 0, down.wait_recv)
    flood_wait(0)
    flood(1)
    for near, far, edge, start in ((1, 0, 0, 0), (4, 5, 3, 3)):
        halo_z = dot_nn(lat4[edge], wl[:, start * C:(start + 6) * C])
        inner = [halo_z[:, (b if near == 1 else b + 3) * C:][:, 0:C] for b in range(3)]
        outer = [halo_z[:, (b + 3 if near == 1 else b) * C:][:, 0:C] for b in range(3)]
        activate(near, *[own_terms(near, b) + inner[b] for b in range(3)])
        activate(far, *[own_terms(far, b) + (inner[b] + outer[b]) for b in range(3)])

    res = dot_nt(wd32[...].astype(BF16), hbuf[...])
    even, odd = res[:, 0:WL], res[:, WL:2 * WL]
    left = iota((16, WL), 1) == 0
    right = iota((16, WL), 1) == WL - 1
    dec_even = jnp.where(left, 0.0, pltpu.roll(odd[0:16], 1, 1)) + even[16:32] + odd[32:48]
    dec_odd = even[0:16] + odd[16:32] + jnp.where(right, 0.0, pltpu.roll(even[32:48], WL - 1, 1))
    decoded = jnp.concatenate([dec_even, dec_odd], axis=1).astype(BF16)
    dec[...] = decoded
    dall[jnp.where(low_half, q + 4, q)] = decoded

    @pl.when((q == 0) & (p > 0))
    def told():
        pl.semaphore_wait(flood_sem.at[4], 1)

    def gather_send(n, cond, target, slot):
        send(cond, dec, dall.at[slot], gat_ss.at[n], gat_rs.at[slot], f, target)

    for d in range(1, 4):
        qd = (q + d) % 4
        gather_send(d - 1, None, 4 * p + qd, jnp.where(qd < 2, q + 4, q))
    gather_send(3, p < GROUPS - 1, 4 * p + 4, q)
    gather_send(4, p > 0, 4 * p - 1, q + 4)
    gather_send(5, (q == 0) & (p > 0), 4 * p - 4, 8)
    gather_send(6, (q == 0) & (p > 0), 4 * p - 3, 8)
    gather_send(7, (q == 0) & (p > 0), 4 * p - 2, 4)
    gather_send(8, (q == 0) & (p > 1), 4 * p - 5, 8)

    rk = iota((128, 1), 0)
    g = rk & 63
    colour = one(g >= 14) + one(g >= 28)
    ig = jnp.where(rk < 64, p, p2) * PATCH + g - 14 * colour
    valid = (g < 42) & (ig >= 0) & (ig < IMG)
    table_load.wait()
    table = table_ref[...].astype(F32)
    cols = iota((128, IMG), 1)
    lo = jnp.sum(jnp.where(cols == ig, table, 0.0), axis=1, keepdims=True)
    nxt = jnp.sum(jnp.where(cols == ig + 1, table, 0.0), axis=1, keepdims=True)
    nxt = nxt + jnp.where(ig == IMG - 1, 256.0, 0.0)
    hi = jnp.maximum(nxt, lo + 1.0)
    inv = 1.0 / (hi - lo)
    lane = iota((128, 144), 1)
    row = (4 * jnp.where(rk < 64, 4 * p, base) + (lane >> 2)).astype(F32)
    inside = valid & ((lane & 3) == colour) & (row >= lo) & (row < hi)
    pick = jnp.where(inside, 1.0, 0.0).astype(BF16)
    lane = iota((128, 128), 1)
    row = (4 * s - 1 + (lane >> 2)).astype(F32)
    inside = valid & ((lane & 3) == colour) & (row >= lo) & (row < hi) & (lane < 24)
    both = jnp.where(lane == 32, inv, jnp.where(inside, 1.0, 0.0)).T
    back = both[0:32].astype(BF16)
    back = jnp.concatenate([back, back], axis=1)
    inv_row = both[32:33]

    pw_load.wait()
    prow = iota((KP, 588), 0)
    pg = prow & 63
    order = jnp.where(
        (pg < 42) & (iota((KP, 588), 1) == 14 * pg + 2 * (prow >> 7) + ((prow >> 6) & 1)), 1.0, 0.0
    ).astype(BF16)
    for n in range(CW // 256):
        cut = slice(n * 256, (n + 1) * 256)
        pwp[:, cut] = dot_nn(order, pw[:, cut]).astype(BF16)

    def gather_wait(slot, cond, source):
        copy = remote(dec, dall.at[slot], gat_ss.at[0], gat_rs.at[slot], f, source)
        pl.when(cond)(copy.wait_recv)

    more = p < GROUPS - 1
    for v in range(4):
        gather_wait(v, (q >= 2) & (q != v), 4 * p + v)
        gather_wait(v + 4, low_half & (q != v), 4 * p + v)
    gather_wait(4, (q >= 2) & more, 4 * p + 4)
    gather_wait(8, low_half & more, 4 * p + 4)
    lane16 = iota((16, 128), 1) < 64

    def patch_parts(crop, turned):
        turned[...] = jnp.concatenate([crop, jnp.zeros((64, 256), F32)], axis=0).T
        columns = []
        for c14 in range(14):
            pc, pj = patch_column(c14)
            columns.append(turned[pl.ds(pc * WL + pj, 16, stride=8), :])
        return [
            jnp.where(lane16, columns[2 * n], pltpu.roll(columns[2 * n + 1], 64, 1))
            for n in range(7)
        ]

    own_rows = dall[pl.ds(jnp.where(low_half, 4, 0), 5)].reshape(80, 256)
    own_parts = patch_parts(dot_nn(pick[0:64, 0:80], own_rows) * inv[0:64], ct)
    flood_wait(1)
    pos_load.wait()

    def embed(parts, rows):
        patches = jnp.concatenate(parts, axis=1)
        emb = dot_nn(jnp.concatenate(split2(patches), axis=0), pwp[...])
        emb = emb[0:16] + emb[16:32] + pos[rows, :].astype(F32)
        centred = emb - jnp.mean(emb, axis=1, keepdims=True)
        sigma = jnp.sqrt(jnp.mean(centred * centred, axis=1, keepdims=True) + EPS)
        normed = centred / sigma
        ybuf[rows, :] = normed
        return normed, sigma

    normed, sigma0 = embed(own_parts, slice(0, 16))
    gsum = jnp.sum(normed, axis=0, keepdims=True)
    psend[...] = gsum
    precv[p] = gsum

    for d in range(1, GROUPS):
        send_part(
            None, psend, precv.at[p], pool_ss.at[0], pool_rs.at[0], f, 4 * ((p + d) % GROUPS) + q
        )

    for v in range(4):
        gather_wait(v, (q == 0) & (p > 0), 4 * p - 4 + v)
        if v > 0:
            gather_wait(v + 4, (q == 3) & more, 4 * p + 4 + v)
    gather_wait(8, (q == 3) & (p < GROUPS - 2), 4 * p + 8)
    next_crop = dot_nn(pick[64:128], dall[...].reshape(144, 256)) * inv[64:128]
    sigma1 = embed(patch_parts(next_crop, ct2), slice(16, 32))[1]
    sigma = jnp.concatenate([sigma0, sigma1], axis=0)

    for n in range(4):
        cut = slice(n * C, (n + 1) * C)
        total = gate[:, cut]
        sig = 0.5 + 0.5 * jnp.tanh(0.5 * total)
        gate[:, cut] = sig * (1.0 + total * (1.0 - sig))
    for n in range(4):
        latt[:, n * WL:(n + 1) * WL] = lat4[n].astype(F32).T.astype(BF16)
    text_load.wait()
    text = text_ref[...]
    text2 = jnp.sum(text * text, axis=1, keepdims=True) + 1e-06
    gt[...] = jnp.zeros_like(gt)

    all_of(precv.at[pl.ds(0, GROUPS - 1)], pool_ss.at[0], pool_rs.at[0])
    pooled = precv[0]
    for n in range(1, GROUPS):
        pooled = pooled + precv[n]
    pooled = pooled * (1.0 / 256.0)

    proj_load.wait()

    def two_rows(v):
        top = iota((16, v.shape[1]), 0)
        hi_part = v.astype(BF16).astype(F32)
        return jnp.where(top == 0, hi_part, jnp.where(top == 1, v - hi_part, 0.0)).astype(BF16)

    pc_ = pooled - jnp.mean(pooled, axis=1, keepdims=True)
    psigma = jnp.sqrt(jnp.mean(pc_ * pc_, axis=1, keepdims=True) + EPS)
    unit = pc_ / psigma
    projected = jnp.sum(dot_nn(two_rows(unit), proj[...]), axis=0, keepdims=True)
    numer = jnp.sum(projected * text, axis=1, keepdims=True)
    norm2 = jnp.sum(projected * projected, axis=1, keepdims=True) + 1e-06
    scale = 1.0 / jnp.sqrt(norm2 * text2)
    reward = numer * scale
    reward_ref[...] = reward
    dproj = -LOSS_SCALE * (text * scale - projected * (reward / norm2))
    dunit = jnp.sum(dot_nt(two_rows(dproj), proj[...]), axis=0, keepdims=True)

    def norm_back(dy, y, sg):
        m1 = jnp.mean(dy, axis=1, keepdims=True)
        m2 = jnp.mean(dy * y, axis=1, keepdims=True)
        return (dy - m1 - y * m2) / sg

    dpooled = norm_back(dunit, unit, psigma) * (1.0 / 256.0)
    demb = norm_back(dpooled, ybuf[...], sigma)
    dpat = dot_nt(jnp.concatenate(split2(demb), axis=0), pwp[...])
    dpat = dpat[0:32] + dpat[32:64]
    for n in range(7):
        d0 = dpat[0:16, n * 128:(n + 1) * 128]
        d1 = dpat[16:32, n * 128:(n + 1) * 128]
        pair = (
            jnp.where(lane16, d0, pltpu.roll(d1, 64, 1)),
            jnp.where(lane16, pltpu.roll(d0, 64, 1), d1),
        )
        for half in range(2):
            pc, pj = patch_column(2 * n + half)
            gt[pl.ds(pc * WL + pj, 16, stride=8), :] = pair[half]

    grows = jnp.concatenate(split2(gt[...] * inv_row), axis=1)
    image = dot_nt(back, grows).astype(BF16).astype(F32)
    even, odd = image[:, 0:WL], image[:, WL:2 * WL]
    left = iota((32, WL), 1) == 0
    right = iota((32, WL), 1) == WL - 1
    odd_before = jnp.where(left, 0.0, pltpu.roll(odd, 1, 1))
    even_after = jnp.where(right, 0.0, pltpu.roll(even, WL - 1, 1))
    igs[0] = jnp.concatenate([odd, even_after], axis=1)
    igs[1] = image
    igs[2] = jnp.concatenate([odd_before, even], axis=1)

    ims = []
    go = jnp.zeros((48, C), F32)
    for r in range(4):
        im = jnp.concatenate([igs[b, 4 * r:4 * r + 16, :] for b in range(3)], axis=0).astype(BF16)
        ims.append(im)
        go = go + dot_nn(im, hbuf[:, (r + 1) * C:(r + 2) * C])
    for half in range(2):
        go2[half, 27:32, :] = jnp.zeros((5, 128), F32)
        for t in range(9):
            at = (t % 3) * 16 + (2 - t // 3) * 4
            go2[half, 3 * t:3 * t + 3, :] = go[at:at + 3, half * 128:(half + 1) * 128]
    fc = y_hi * 2 + 1 - core
    outk = send(None, go2.at[1 - core], gocr, c_ss.at[3], c_rs.at[3], fc, s)

    wout = wo32[...].astype(BF16)
    cols_of = []
    for r in range(4):
        cg = dot_tn(ims[r], wout) * gate[:, r * C:(r + 1) * C]
        ev, od = cg[0:WL], cg[WL:2 * WL]
        od_before = jnp.where(first, 0.0, pltpu.roll(od, 1, 0))
        ev_after = jnp.where(last, 0.0, pltpu.roll(ev, WL - 1, 0))
        cols_of.append((od + ev_after, ev + od, od_before + ev))

    def put_grad(a, b, value):
        at = (3 * a + b) * C
        for half in range(2):
            part = value[:, half * 128:(half + 1) * 128]
            g32[half, at:at + C, :] = part
            gbf[half, at:at + C, :] = part.astype(BF16)

    outer = [
        jnp.concatenate([cols_of[0][b], cols_of[1][b] + cols_of[2][b], cols_of[3][b]], axis=0)
        .astype(BF16) for b in range(3)
    ]
    inner = [
        jnp.concatenate([cols_of[0][b] + cols_of[1][b], cols_of[2][b] + cols_of[3][b]], axis=0)
        .astype(BF16) for b in range(3)
    ]
    outk.wait_recv()
    gsum_z = go2[core] + gocr[...]
    goz[...] = gsum_z.astype(BF16)
    for d in range(1, 8):
        zd = (z + d) % 8
        send_part(None, goz, gozr.at[z], z_ss.at[0], z_rs.at[0], f, x * 16 + zd * 2 + y_lo)

    main = []
    for a, start, stop, terms in ((0, 0, 3, outer), (1, 1, 3, inner), (2, 1, 4, outer)):
        for b in range(3):
            put_grad(a, b, dot_nn(latt[:, start * WL:stop * WL], terms[b]))
        rows = pl.ds(a * 768, 768)
        main.append(
            send(None, gbf.at[1 - core, rows], gcr.at[rows], c_ss.at[a], c_rs.at[a], fc, s)
        )

    mine = jnp.where(core == 0, x, y)

    def quarter_device(n):
        fd = jnp.where(core == 0, f, (n // 2) * 2 + 1)
        sd = jnp.where(core == 0, n * 16 + z * 2 + y_lo, x * 16 + z * 2 + n % 2)
        return fd, sd

    def halves_sum(half, start, count):
        return g32[half, start:start + count, :] + gcr[start:start + count, :].astype(F32)

    for w in range(4):
        for part in range(2):
            if w == 0 and part == 0:
                main[0].wait_recv()
                main[1].wait_recv()
            elif w == 0:
                main[2].wait_recv()

            @pl.when(core == 0)
            def along_x():
                for n in (2 * part, 2 * part + 1):
                    total = jnp.concatenate(
                        [halves_sum(0, n * 576 + zd * 72, 72) for zd in (w, w + 4)], axis=0
                    )
                    x32[n, w] = total
                    xbf[n, w] = total.astype(BF16)

            @pl.when(core == 1)
            def along_y():
                units = [
                    halves_sum(1, (2 * part + h) * 576 + zd * 72, 72)
                    for zd in (w, w + 4) for h in range(2)
                ]
                for n in range(2):
                    total = jnp.concatenate([u[36 * n:36 * n + 36] for u in units], axis=0)
                    x32[2 * part + n, w] = total
                    xbf[2 * part + n, w] = total.astype(BF16)

            for n in (2 * part, 2 * part + 1):
                send_part(
                    mine != n, xbf.at[n, w], xr.at[w, mine], u_ss.at[w], u_rs.at[w],
                    *quarter_device(n),
                )

    for w in range(4):
        xr[w, mine] = jnp.zeros((144, 128), BF16)
    zr[z] = jnp.zeros((80, 128), BF16)
    for w in range(4):
        all_of(xr.at[w, pl.ds(0, 3)], u_ss.at[w], u_rs.at[w])
        for k in range(2):
            zd = w + 4 * k
            cut = slice(k * 72, (k + 1) * 72)
            total = x32[mine, w, cut, :]
            for n in range(4):
                total = total + xr[w, n, cut, :].astype(F32)
            z32[zd] = total
            zbf[zd] = jnp.concatenate([total, jnp.zeros((8, 128), F32)], axis=0).astype(BF16)
            send_part(
                z != zd, zbf.at[zd], zr.at[z], z_ss.at[1], z_rs.at[1], f, x * 16 + zd * 2 + y_lo
            )
        if w == 1:
            gozr[z] = jnp.zeros((32, 128), BF16)
            all_of(gozr.at[pl.ds(0, 7)], z_ss.at[0], z_rs.at[0])
            gsum_x = gsum_z + jnp.sum(gozr[...].astype(F32), axis=0)
            gox[...] = gsum_x
            for d in range(1, 4):
                xd = (x + d) % 4
                send_part(
                    None, gox, goxr.at[x], x_ss.at[0], x_rs.at[0], f, xd * 16 + z * 2 + y_lo
                )

    goxr[x] = gsum_x
    all_of(goxr.at[pl.ds(0, 3)], x_ss.at[0], x_rs.at[0])
    gsum_y = jnp.sum(goxr[...], axis=0)
    goy[...] = gsum_y
    for d in range(1, 8):
        yd = (yc + d) % 8
        send_part(None, goy, goyr.at[yc], y_ss.at[0], y_rs.at[0], *yc_device(yd))
    goyr[yc] = gsum_y

    all_of(zr.at[pl.ds(0, 7)], z_ss.at[1], z_rs.at[1])
    total = z32[z]
    for n in range(8):
        total = total + zr[n, 0:72, :].astype(F32)

    for n in range(2):
        yb[n, 0:36, :] = total[36 * n:36 * n + 36]
        yb[n, 36:40, :] = jnp.zeros((4, 128), F32)
    slot = jnp.where(core == 0, y, 4 + x)
    for n in range(2):
        sd = jnp.where(core == 0, x * 16 + z * 2 + n, (2 * y_hi + n) * 16 + z * 2 + y_lo)
        here = sd == s

        @pl.when(here)
        def keep():
            yr[slot] = yb[n]

        for j in range(4):
            send_part(
                jnp.logical_not(here & (f == j)), yb.at[n], yr.at[slot],
                y_ss.at[1], y_rs.at[1], j, sd,
            )

    all_of(goyr.at[pl.ds(0, 7)], y_ss.at[0], y_rs.at[0])
    for half in range(2):
        total = (goyr[half] + goyr[2 + half]) + (goyr[4 + half] + goyr[6 + half])
        for t in range(9):
            gout_ref[:, t * C + half * 128:t * C + (half + 1) * 128] = total[3 * t:3 * t + 3]
    seven = (core == 0) | (x // 2 == y_hi)
    all_of(yr.at[pl.ds(0, 7)], y_ss.at[1], y_rs.at[1], seven)
    all_of(yr, y_ss.at[1], y_rs.at[1], jnp.logical_not(seven))
    for half in range(2):
        total = (yr[4 * half] + yr[4 * half + 1]) + (yr[4 * half + 2] + yr[4 * half + 3])
        gconv_ref[:, half * 128:(half + 1) * 128] = total[0:36]

    for cond, copy in sends:
        guard(cond, copy.wait_send)


def per_device(latents, conv_weight, conv_bias, out_weight, row_table, patch_weight, pos_embed,
               proj_weight, text_embed):
    vmem = pl.BlockSpec(memory_space=pltpu.VMEM)
    hbm = pl.BlockSpec(memory_space=pltpu.HBM)
    V = pltpu.VMEM
    dma = pltpu.SemaphoreType.DMA
    reward, gconv, gout = pl.pallas_call(
        kernel,
        out_shape=(
            jax.ShapeDtypeStruct((1, 1), F32),
            jax.ShapeDtypeStruct((36, C), F32),
            jax.ShapeDtypeStruct((3, 9 * C), F32),
        ),
        in_specs=[hbm] * 9,
        out_specs=(vmem, vmem, vmem),
        scratch_shapes=[
            V((1, C), F32), V((3, 9 * C), BF16), V((1, IMG), jnp.int32), V((1, EMB), F32),
            V((4, WL, C), BF16),
            V((C, 9 * C), BF16),
            V((2 * WL, 9 * C), F32),
            V((2 * WL, 6 * C), BF16),
            V((2 * WL, 4 * C), F32),
            V((48, 6 * C), F32),
            V((48, C), F32),
            V((588, CW), BF16),
            V((KP, CW), BF16),
            V((32, CW), BF16),
            V((CW, EMB), BF16),
            V((16, 256), BF16),
            V((9, 16, 256), BF16),
            V((256, 128), F32),
            V((256, 128), F32),
            V((256, 128), F32),
            V((32, CW), F32),
            V((1, CW), F32),
            V((GROUPS, 1, CW), F32),
            V((3, 32, 256), F32),
            V((C, 4 * WL), BF16),
            V((2, 9 * C, 128), F32),
            V((2, 9 * C, 128), BF16),
            V((9 * C, 128), BF16),
            V((4, 4, 144, 128), BF16),
            V((4, 4, 144, 128), F32),
            V((4, 4, 144, 128), BF16),
            V((8, 80, 128), BF16),
            V((8, 72, 128), F32),
            V((8, 80, 128), BF16),
            V((2, 40, 128), F32),
            V((8, 40, 128), F32),
            V((2, 32, 128), F32),
            V((32, 128), F32),
            V((32, 128), BF16),
            V((8, 32, 128), BF16),
            V((32, 128), F32),
            V((4, 32, 128), F32),
            V((32, 128), F32),
            V((8, 32, 128), F32),
            dma((9,)), dma((2,)), dma((2,)), dma((9,)), dma((9,)), dma((1,)), dma((1,)),
            dma((4,)), dma((4,)), dma((4,)), dma((4,)), dma((1,)), dma((1,)),
            dma((2,)), dma((2,)), dma((2,)), dma((2,)), pltpu.SemaphoreType.REGULAR((5,)),
        ],
        compiler_params=pltpu.CompilerParams(
            collective_id=0, has_side_effects=True, vmem_limit_bytes=48 * 1024 * 1024
        ),
    )(*[
        pltpu.with_memory_space_constraint(v, pltpu.HBM) for v in (
            latents, conv_weight, conv_bias.reshape(1, C), out_weight, row_table, patch_weight,
            pos_embed, proj_weight, text_embed.reshape(1, EMB),
        )
    ])
    return reward.reshape(1), gconv, gout


def solution(mesh):
    return jax.shard_map(
        per_device,
        mesh=mesh,
        in_specs=(
            P("frame", "slab", None, None), P(), P(), P(), P("frame", None), P(), P(), P(), P(),
        ),
        out_specs=(P("frame"), P("slab", None), P()),
        check_vma=False,
    )
```

```python
import jax
import jax.numpy as jnp
from jax import lax
from jax.experimental import pallas as pl
from jax.experimental.pallas import tpu as pltpu
from jax.sharding import PartitionSpec as P

MESH = pl.DeviceIdType.MESH
F32 = jnp.float32
BF16 = jnp.bfloat16

C = 256
CW = 1280
EMB = 1024
IMG = 224
PATCH = 14
WL = 128
N_SLAB = 64
GROUPS = 16
KP = 14 * 64
LOSS_SCALE = 256.0
EPS = 1e-05


def dot_nn(a, b):
    return lax.dot_general(a, b, (((1,), (0,)), ((), ())), preferred_element_type=F32)


def dot_nt(a, b):
    return lax.dot_general(a, b, (((1,), (1,)), ((), ())), preferred_element_type=F32)


def dot_tn(a, b):
    return lax.dot_general(a, b, (((0,), (0,)), ((), ())), preferred_element_type=F32)


def iota(shape, dim):
    return lax.broadcasted_iota(jnp.int32, shape, dim)


def split2(v):
    hi = v.astype(BF16)
    lo = (v - hi.astype(F32)).astype(BF16)
    return hi, lo


def lat_row(r6, a):
    return (r6 - 1 + a - 1) // 2 + 1


def patch_column(c14):
    c16 = c14 * 8 // 7
    return c16 % 2, c16 // 2


def kernel(
    lat_hbm, cw_hbm, bias_hbm, ow_hbm, table_hbm, pw_hbm, pos_hbm, proj_hbm, text_hbm,
    reward_ref, gconv_ref, gout_ref,
    bias_ref, ow_ref, table_ref, text_ref,
    lat4, wl, taps, hbuf, gate, wd32, wo32, pw, pwp, pwpt, pos, proj, projt,
    dec, dall, ct, ct2, gt, ybuf, psend, precv, igs, latt,
    g32, gbf, gcr, xbf, x32, xr, zbf, z32, zr, yb, yr,
    go2, gocr, goz, gozr, gox, goxr, goy, goyr,
    loc_sem, halo_ss, halo_rs, gat_ss, gat_rs, pool_ss, pool_rs,
    c_ss, c_rs, u_ss, u_rs, x_ss, x_rs, z_ss, z_rs, y_ss, y_rs, flood_sem,
):
    f = lax.axis_index("frame")
    s = lax.axis_index("slab")
    y_hi, core = f // 2, f % 2
    x, z, y_lo = s // 16, (s % 16) // 2, s % 2
    p, q = s // 4, s % 4
    low_half = q < 2
    base = jnp.where(low_half, 4 * p - 4, 4 * p)
    p2 = jnp.where(low_half, p - 1, p + 1)
    p2c = jnp.clip(p2, 0, GROUPS - 1)

    dall[...] = jnp.zeros_like(dall)
    lat4[0] = jnp.zeros((WL, C), BF16)
    lat4[3] = jnp.zeros((WL, C), BF16)

    barrier = pltpu.get_barrier_semaphore()

    def greet(cond, fd, sd):
        def go():
            pl.semaphore_signal(barrier, inc=1, device_id=(fd, sd), device_id_type=MESH)

        if cond is None:
            go()
        else:
            pl.when(cond)(go)

    greet(s > 0, f, s - 1)
    greet(s < N_SLAB - 1, f, s + 1)
    for d in range(1, 4):
        greet(None, f, 4 * p + (q + d) % 4)
    for v in range(4):
        greet((q == 0) & (p > 0), f, 4 * p - 4 + v)
        greet((q == 3) & (p < GROUPS - 1), f, 4 * p + 4 + v)
    greet((q < 3) & (p < GROUPS - 1), f, 4 * p + 4)
    for d in range(1, 4):
        greet(None, f, ((x + d) % 4) * 16 + z * 2 + y_lo)
    for d in (2, 6):
        greet(None, f, x * 16 + ((z + d) % 8) * 2 + y_lo)
    yc = y_hi * 4 + y_lo * 2 + core

    def yc_device(idx):
        return (idx // 4) * 2 + idx % 2, x * 16 + z * 2 + (idx // 2) % 2

    for d in range(1, 8):
        greet(None, *yc_device((yc + d) % 8))
    y = y_hi * 2 + y_lo

    def one(cond):
        return jnp.where(cond, 1, 0)

    expected = (
        one(s > 0) + one(s < N_SLAB - 1)
        + 3 + one(p < GROUPS - 1) + one(p > 0)
        + one((q == 0) & (p > 0)) * 3
        + 3 + 2 + 7
    )

    loads = []

    def load(src, dst):
        copy = pltpu.make_async_copy(src, dst, loc_sem.at[len(loads)])
        copy.start()
        loads.append(copy)
        return copy

    def load_parts(pairs, whole):
        sem = loc_sem.at[len(loads)]
        for src, dst in pairs:
            pltpu.make_async_copy(src, dst, sem).start()
        copy = pltpu.make_async_copy(whole, whole, sem)
        loads.append(copy)
        return copy

    lat_load = load(lat_hbm.at[0], lat4.at[pl.ds(1, 2)])
    w_load = load_parts(
        [
            (cw_hbm.at[pl.ds(t * C, C)], wl.at[:, pl.ds(t * C, C)])
            for t in range(9)
        ],
        wl,
    )

    pl.semaphore_wait(barrier, expected)

    def flood(stage):
        for n, d in enumerate((2, 6)):
            pl.semaphore_signal(
                flood_sem.at[2 * stage + n], inc=1,
                device_id=(f, x * 16 + ((z + d) % 8) * 2 + y_lo), device_id_type=MESH,
            )

    def flood_wait(stage):
        for n in range(2):
            pl.semaphore_wait(flood_sem.at[2 * stage + n], 1)

    flood(0)

    @pl.when((q == 0) & (p < GROUPS - 1))
    def tell():
        pl.semaphore_signal(
            flood_sem.at[4], inc=1, device_id=(f, s + 4), device_id_type=MESH
        )

    sends = []

    def remote(src, dst, ssem, rsem, fd, sd):
        return pltpu.make_async_remote_copy(
            src_ref=src, dst_ref=dst, send_sem=ssem, recv_sem=rsem,
            device_id=(fd, sd), device_id_type=MESH,
        )

    def guard(cond, action):
        if cond is None:
            action()
        else:
            pl.when(cond)(action)

    def send(cond, *what):
        copy = remote(*what)
        guard(cond, copy.start)
        sends.append((cond, copy))
        return copy

    def send_part(cond, *what):
        guard(cond, remote(*what).start)

    def all_of(whole, ssem, rsem, cond=None):
        copy = remote(whole, whole, ssem, rsem, y_hi * 2 + 1 - core, s)
        sends.append((cond, copy))
        guard(cond, copy.wait_recv)

    up = send(s > 0, lat_hbm.at[0, 0], lat4.at[3], halo_ss.at[0], halo_rs.at[1], f, s - 1)
    down = send(
        s < N_SLAB - 1, lat_hbm.at[0, 1], lat4.at[0], halo_ss.at[1], halo_rs.at[0], f, s + 1
    )

    ow_load = load(ow_hbm, ow_ref)
    bias_load = load(bias_hbm, bias_ref)
    table_load = load(table_hbm, table_ref)
    text_load = load(text_hbm, text_ref)
    pw_load = load(pw_hbm, pw)
    pos_load = load_parts(
        [
            (pos_hbm.at[pl.ds(pl.multiple_of(16 * p, 16), 16)], pos.at[pl.ds(0, 16)]),
            (pos_hbm.at[pl.ds(pl.multiple_of(16 * p2c, 16), 16)], pos.at[pl.ds(16, 16)]),
        ],
        pos,
    )
    proj_load = load(proj_hbm, proj)

    wd32[...] = jnp.zeros_like(wd32)
    wo32[...] = jnp.zeros_like(wo32)
    ow_load.wait()
    for a in range(3):
        for b in range(3):
            t = 3 * a + b
            tap = ow_ref[:, t * C:(t + 1) * C].astype(F32)
            wo32[b * 16 + (2 - a) * 4:b * 16 + (2 - a) * 4 + 3, :] = tap
            for r in range(4):
                wd32[b * 16 + r * 4:b * 16 + r * 4 + 3, (r + a) * C:(r + a + 1) * C] = tap

    bias_load.wait()
    bias = bias_ref[...]
    first = iota((WL, C), 0) == 0
    last = iota((WL, C), 0) == WL - 1

    def activate(r6, z0, z1, z2):
        before = jnp.where(first, 0.0, pltpu.roll(z0, 1, 0))
        after = jnp.where(last, 0.0, pltpu.roll(z2, WL - 1, 0))
        for pc, total in ((0, before + z1 + z2), (1, z0 + z1 + after)):
            total = total + bias
            hidden = total * (0.5 + 0.5 * jnp.tanh(0.5 * total))
            if r6 == 0:
                hidden = jnp.where(s > 0, hidden, 0.0)
            elif r6 == 5:
                hidden = jnp.where(s < N_SLAB - 1, hidden, 0.0)
            else:
                gate[pc * WL:(pc + 1) * WL, (r6 - 1) * C:r6 * C] = total
            hbuf[pc * WL:(pc + 1) * WL, r6 * C:(r6 + 1) * C] = hidden.astype(BF16)

    lat_load.wait()
    w_load.wait()

    taps[...] = dot_nn(lat4[1:3].reshape(2 * WL, C), wl[...])

    def part(row, a, b):
        t = 3 * a + b
        return taps[(row - 1) * WL:row * WL, t * C:(t + 1) * C]

    def own_terms(r6, b):
        rows = [(lat_row(r6, a), a) for a in range(3)]
        return sum(part(row, a, b) for row, a in rows if row in (1, 2))

    for r6 in (2, 3):
        activate(r6, *[own_terms(r6, b) for b in range(3)])

    guard(s < N_SLAB - 1, up.wait_recv)
    guard(s > 0, down.wait_recv)
    flood_wait(0)
    flood(1)
    for near, far, edge, start in ((1, 0, 0, 0), (4, 5, 3, 3)):
        halo_z = dot_nn(lat4[edge], wl[:, start * C:(start + 6) * C])
        inner = [halo_z[:, (b if near == 1 else b + 3) * C:][:, 0:C] for b in range(3)]
        outer = [halo_z[:, (b + 3 if near == 1 else b) * C:][:, 0:C] for b in range(3)]
        activate(near, *[own_terms(near, b) + inner[b] for b in range(3)])
        activate(far, *[own_terms(far, b) + (inner[b] + outer[b]) for b in range(3)])

    res = dot_nt(wd32[...].astype(BF16), hbuf[...])
    even, odd = res[:, 0:WL], res[:, WL:2 * WL]
    left = iota((16, WL), 1) == 0
    right = iota((16, WL), 1) == WL - 1
    dec_even = jnp.where(left, 0.0, pltpu.roll(odd[0:16], 1, 1)) + even[16:32] + odd[32:48]
    dec_odd = even[0:16] + odd[16:32] + jnp.where(right, 0.0, pltpu.roll(even[32:48], WL - 1, 1))
    decoded = jnp.concatenate([dec_even, dec_odd], axis=1).astype(BF16)
    dec[...] = decoded
    dall[jnp.where(low_half, q + 4, q)] = decoded

    @pl.when((q == 0) & (p > 0))
    def told():
        pl.semaphore_wait(flood_sem.at[4], 1)

    def gather_send(n, cond, target, slot):
        send(cond, dec, dall.at[slot], gat_ss.at[n], gat_rs.at[slot], f, target)

    for d in range(1, 4):
        qd = (q + d) % 4
        gather_send(d - 1, None, 4 * p + qd, jnp.where(qd < 2, q + 4, q))
    gather_send(3, p < GROUPS - 1, 4 * p + 4, q)
    gather_send(4, p > 0, 4 * p - 1, q + 4)
    gather_send(5, (q == 0) & (p > 0), 4 * p - 4, 8)
    gather_send(6, (q == 0) & (p > 0), 4 * p - 3, 8)
    gather_send(7, (q == 0) & (p > 0), 4 * p - 2, 4)
    gather_send(8, (q == 0) & (p > 1), 4 * p - 5, 8)

    rk = iota((128, 1), 0)
    g = rk & 63
    colour = one(g >= 14) + one(g >= 28)
    ig = jnp.where(rk < 64, p, p2) * PATCH + g - 14 * colour
    valid = (g < 42) & (ig >= 0) & (ig < IMG)
    table_load.wait()
    table = table_ref[...].astype(F32)
    cols = iota((128, IMG), 1)
    lo = jnp.sum(jnp.where(cols == ig, table, 0.0), axis=1, keepdims=True)
    nxt = jnp.sum(jnp.where(cols == ig + 1, table, 0.0), axis=1, keepdims=True)
    nxt = nxt + jnp.where(ig == IMG - 1, 256.0, 0.0)
    hi = jnp.maximum(nxt, lo + 1.0)
    inv = 1.0 / (hi - lo)
    lane = iota((128, 144), 1)
    row = (4 * jnp.where(rk < 64, 4 * p, base) + (lane >> 2)).astype(F32)
    inside = valid & ((lane & 3) == colour) & (row >= lo) & (row < hi)
    pick = jnp.where(inside, 1.0, 0.0).astype(BF16)
    lane = iota((128, 128), 1)
    row = (4 * s - 1 + (lane >> 2)).astype(F32)
    inside = valid & ((lane & 3) == colour) & (row >= lo) & (row < hi) & (lane < 24)
    both = jnp.where(lane == 32, inv, jnp.where(inside, 1.0, 0.0)).T
    back = both[0:32].astype(BF16)
    back = jnp.concatenate([back, back], axis=1)
    inv_row = both[32:33]

    pw_load.wait()
    prow = iota((KP, 588), 0)
    pg = prow & 63
    order = jnp.where(
        (pg < 42) & (iota((KP, 588), 1) == 14 * pg + 2 * (prow >> 7) + ((prow >> 6) & 1)), 1.0, 0.0
    ).astype(BF16)
    for n in range(CW // 256):
        cut = slice(n * 256, (n + 1) * 256)
        pwp[:, cut] = dot_nn(order, pw[:, cut]).astype(BF16)

    def gather_wait(slot, cond, source):
        copy = remote(dec, dall.at[slot], gat_ss.at[0], gat_rs.at[slot], f, source)
        pl.when(cond)(copy.wait_recv)

    more = p < GROUPS - 1
    for v in range(4):
        gather_wait(v, (q >= 2) & (q != v), 4 * p + v)
        gather_wait(v + 4, low_half & (q != v), 4 * p + v)
    gather_wait(4, (q >= 2) & more, 4 * p + 4)
    gather_wait(8, low_half & more, 4 * p + 4)
    lane16 = iota((16, 128), 1) < 64

    def patch_parts(crop, turned):
        turned[...] = jnp.concatenate([crop, jnp.zeros((64, 256), F32)], axis=0).T
        columns = []
        for c14 in range(14):
            pc, pj = patch_column(c14)
            columns.append(turned[pl.ds(pc * WL + pj, 16, stride=8), :])
        return [
            jnp.where(lane16, columns[2 * n], pltpu.roll(columns[2 * n + 1], 64, 1))
            for n in range(7)
        ]

    own_rows = dall[pl.ds(jnp.where(low_half, 4, 0), 5)].reshape(80, 256)
    own_parts = patch_parts(dot_nn(pick[0:64, 0:80], own_rows) * inv[0:64], ct)
    pos_load.wait()

    def embed(parts, rows):
        patches = jnp.concatenate(parts, axis=1)
        emb = dot_nn(jnp.concatenate(split2(patches), axis=0), pwp[...])
        emb = emb[0:16] + emb[16:32] + pos[rows, :].astype(F32)
        centred = emb - jnp.mean(emb, axis=1, keepdims=True)
        sigma = jnp.sqrt(jnp.mean(centred * centred, axis=1, keepdims=True) + EPS)
        normed = centred / sigma
        ybuf[rows, :] = normed
        return normed, sigma

    normed, sigma0 = embed(own_parts, slice(0, 16))
    gsum = jnp.sum(normed, axis=0, keepdims=True)
    psend[...] = gsum
    precv[p] = gsum

    flood_wait(1)
    for d in range(1, GROUPS):
        send_part(
            None, psend, precv.at[p], pool_ss.at[0], pool_rs.at[0], f, 4 * ((p + d) % GROUPS) + q
        )

    for v in range(4):
        gather_wait(v, (q == 0) & (p > 0), 4 * p - 4 + v)
        if v > 0:
            gather_wait(v + 4, (q == 3) & more, 4 * p + 4 + v)
    gather_wait(8, (q == 3) & (p < GROUPS - 2), 4 * p + 8)
    next_crop = dot_nn(pick[64:128], dall[...].reshape(144, 256)) * inv[64:128]
    sigma1 = embed(patch_parts(next_crop, ct2), slice(16, 32))[1]
    sigma = jnp.concatenate([sigma0, sigma1], axis=0)

    for n in range(4):
        cut = slice(n * C, (n + 1) * C)
        total = gate[:, cut]
        sig = 0.5 + 0.5 * jnp.tanh(0.5 * total)
        gate[:, cut] = sig * (1.0 + total * (1.0 - sig))
    for n in range(4):
        latt[:, n * WL:(n + 1) * WL] = lat4[n].astype(F32).T.astype(BF16)
    proj_load.wait()
    for n in range(CW // 256):
        cut = slice(n * 256, (n + 1) * 256)
        projt[:, cut] = proj[cut, :].astype(F32).T.astype(BF16)
    for n in range(KP // 128):
        cut = slice(n * 128, (n + 1) * 128)
        pwpt[:, cut] = pwp[cut, :].astype(F32).T.astype(BF16)
    text_load.wait()
    text = text_ref[...]
    text2 = jnp.sum(text * text, axis=1, keepdims=True) + 1e-06
    gt[...] = jnp.zeros_like(gt)

    all_of(precv.at[pl.ds(0, GROUPS - 1)], pool_ss.at[0], pool_rs.at[0])
    pooled = precv[0]
    for n in range(1, GROUPS):
        pooled = pooled + precv[n]
    pooled = pooled * (1.0 / 256.0)


    def two_rows(v):
        top = iota((16, v.shape[1]), 0)
        hi_part = v.astype(BF16).astype(F32)
        return jnp.where(top == 0, hi_part, jnp.where(top == 1, v - hi_part, 0.0)).astype(BF16)

    pc_ = pooled - jnp.mean(pooled, axis=1, keepdims=True)
    psigma = jnp.sqrt(jnp.mean(pc_ * pc_, axis=1, keepdims=True) + EPS)
    unit = pc_ / psigma
    projected = jnp.sum(dot_nn(two_rows(unit), proj[...]), axis=0, keepdims=True)
    numer = jnp.sum(projected * text, axis=1, keepdims=True)
    norm2 = jnp.sum(projected * projected, axis=1, keepdims=True) + 1e-06
    scale = 1.0 / jnp.sqrt(norm2 * text2)
    reward = numer * scale
    reward_ref[...] = reward
    dproj = -LOSS_SCALE * (text * scale - projected * (reward / norm2))
    dunit = jnp.sum(dot_nn(two_rows(dproj), projt[...]), axis=0, keepdims=True)

    def norm_back(dy, y, sg):
        m1 = jnp.mean(dy, axis=1, keepdims=True)
        m2 = jnp.mean(dy * y, axis=1, keepdims=True)
        return (dy - m1 - y * m2) / sg

    dpooled = norm_back(dunit, unit, psigma) * (1.0 / 256.0)
    demb = norm_back(dpooled, ybuf[...], sigma)
    dpat = dot_nn(jnp.concatenate(split2(demb), axis=0), pwpt[...])
    dpat = dpat[0:32] + dpat[32:64]
    for n in range(7):
        d0 = dpat[0:16, n * 128:(n + 1) * 128]
        d1 = dpat[16:32, n * 128:(n + 1) * 128]
        pair = (
            jnp.where(lane16, d0, pltpu.roll(d1, 64, 1)),
            jnp.where(lane16, pltpu.roll(d0, 64, 1), d1),
        )
        for half in range(2):
            pc, pj = patch_column(2 * n + half)
            gt[pl.ds(pc * WL + pj, 16, stride=8), :] = pair[half]

    grows = jnp.concatenate(split2(gt[...] * inv_row), axis=1)
    image = dot_nt(back, grows).astype(BF16).astype(F32)
    even, odd = image[:, 0:WL], image[:, WL:2 * WL]
    left = iota((32, WL), 1) == 0
    right = iota((32, WL), 1) == WL - 1
    odd_before = jnp.where(left, 0.0, pltpu.roll(odd, 1, 1))
    even_after = jnp.where(right, 0.0, pltpu.roll(even, WL - 1, 1))
    igs[0] = jnp.concatenate([odd, even_after], axis=1)
    igs[1] = image
    igs[2] = jnp.concatenate([odd_before, even], axis=1)

    ims = []
    go = jnp.zeros((48, C), F32)
    for r in range(4):
        im = jnp.concatenate([igs[b, 4 * r:4 * r + 16, :] for b in range(3)], axis=0).astype(BF16)
        ims.append(im)
        go = go + dot_nn(im, hbuf[:, (r + 1) * C:(r + 2) * C])
    for half in range(2):
        go2[half, 27:32, :] = jnp.zeros((5, 128), F32)
        for t in range(9):
            at = (t % 3) * 16 + (2 - t // 3) * 4
            go2[half, 3 * t:3 * t + 3, :] = go[at:at + 3, half * 128:(half + 1) * 128]
    fc = y_hi * 2 + 1 - core
    outk = send(None, go2.at[1 - core], gocr, c_ss.at[3], c_rs.at[3], fc, s)

    wout = wo32[...].astype(BF16)
    cols_of = []
    for r in range(4):
        cg = dot_tn(ims[r], wout) * gate[:, r * C:(r + 1) * C]
        ev, od = cg[0:WL], cg[WL:2 * WL]
        od_before = jnp.where(first, 0.0, pltpu.roll(od, 1, 0))
        ev_after = jnp.where(last, 0.0, pltpu.roll(ev, WL - 1, 0))
        cols_of.append((od + ev_after, ev + od, od_before + ev))

    def put_grad(a, b, value):
        at = (3 * a + b) * C
        left, right = value[:, 0:128], value[:, 128:256]
        g32[at:at + C, :] = jnp.where(core == 0, left, right)
        gbf[at:at + C, :] = jnp.where(core == 0, right, left).astype(BF16)

    outer = [
        jnp.concatenate([cols_of[0][b], cols_of[1][b] + cols_of[2][b], cols_of[3][b]], axis=0)
        .astype(BF16) for b in range(3)
    ]
    inner = [
        jnp.concatenate([cols_of[0][b] + cols_of[1][b], cols_of[2][b] + cols_of[3][b]], axis=0)
        .astype(BF16) for b in range(3)
    ]
    outk.wait_recv()
    gsum_z = go2[core] + gocr[...]
    goz[...] = gsum_z.astype(BF16)
    for d in range(1, 8):
        zd = (z + d) % 8
        send_part(None, goz, gozr.at[z], z_ss.at[0], z_rs.at[0], f, x * 16 + zd * 2 + y_lo)

    main = []
    outer = jnp.concatenate(outer, axis=1)
    inner = jnp.concatenate(inner, axis=1)
    for a, start, stop, terms in ((0, 0, 3, outer), (1, 1, 3, inner), (2, 1, 4, outer)):
        value = dot_nn(latt[:, start * WL:stop * WL], terms)
        for b in range(3):
            put_grad(a, b, value[:, b * C:(b + 1) * C])
        rows = pl.ds(a * 768, 768)
        main.append(
            send(None, gbf.at[rows], gcr.at[rows], c_ss.at[a], c_rs.at[a], fc, s)
        )

    mine = jnp.where(core == 0, x, y)

    def quarter_device(n):
        fd = jnp.where(core == 0, f, (n // 2) * 2 + 1)
        sd = jnp.where(core == 0, n * 16 + z * 2 + y_lo, x * 16 + z * 2 + n % 2)
        return fd, sd

    def halves_sum(start, count):
        return g32[start:start + count, :] + gcr[start:start + count, :].astype(F32)

    for w in range(4):
        for part in range(2):
            if w == 0 and part == 0:
                main[0].wait_recv()
                main[1].wait_recv()
            elif w == 0:
                main[2].wait_recv()

            @pl.when(core == 0)
            def along_x():
                for n in (2 * part, 2 * part + 1):
                    total = jnp.concatenate(
                        [halves_sum(n * 576 + zd * 72, 72) for zd in (w, w + 4)], axis=0
                    )
                    x32[n, w] = total
                    xbf[n, w] = total.astype(BF16)

            @pl.when(core == 1)
            def along_y():
                units = [
                    halves_sum((2 * part + h) * 576 + zd * 72, 72)
                    for zd in (w, w + 4) for h in range(2)
                ]
                for n in range(2):
                    total = jnp.concatenate([u[36 * n:36 * n + 36] for u in units], axis=0)
                    x32[2 * part + n, w] = total
                    xbf[2 * part + n, w] = total.astype(BF16)

            for n in (2 * part, 2 * part + 1):
                send_part(
                    mine != n, xbf.at[n, w], xr.at[w, mine], u_ss.at[w], u_rs.at[w],
                    *quarter_device(n),
                )

    for w in range(4):
        xr[w, mine] = jnp.zeros((144, 128), BF16)
    zr[z] = jnp.zeros((80, 128), BF16)
    for w in range(4):
        all_of(xr.at[w, pl.ds(0, 3)], u_ss.at[w], u_rs.at[w])
        for k in range(2):
            zd = w + 4 * k
            cut = slice(k * 72, (k + 1) * 72)
            total = x32[mine, w, cut, :]
            for n in range(4):
                total = total + xr[w, n, cut, :].astype(F32)
            z32[zd] = total
            zbf[zd] = jnp.concatenate([total, jnp.zeros((8, 128), F32)], axis=0).astype(BF16)
            send_part(
                z != zd, zbf.at[zd], zr.at[z], z_ss.at[1], z_rs.at[1], f, x * 16 + zd * 2 + y_lo
            )
        if w == 1:
            gozr[z] = jnp.zeros((32, 128), BF16)
            all_of(gozr.at[pl.ds(0, 7)], z_ss.at[0], z_rs.at[0])
            gsum_x = gsum_z + jnp.sum(gozr[...].astype(F32), axis=0)
            gox[...] = gsum_x
            for d in range(1, 4):
                xd = (x + d) % 4
                send_part(
                    None, gox, goxr.at[x], x_ss.at[0], x_rs.at[0], f, xd * 16 + z * 2 + y_lo
                )

    goxr[x] = gsum_x
    all_of(goxr.at[pl.ds(0, 3)], x_ss.at[0], x_rs.at[0])
    gsum_y = jnp.sum(goxr[...], axis=0)
    goy[...] = gsum_y
    for d in range(1, 8):
        yd = (yc + d) % 8
        send_part(None, goy, goyr.at[yc], y_ss.at[0], y_rs.at[0], *yc_device(yd))
    goyr[yc] = gsum_y

    all_of(zr.at[pl.ds(0, 7)], z_ss.at[1], z_rs.at[1])
    total = z32[z]
    for n in range(8):
        total = total + zr[n, 0:72, :].astype(F32)

    for n in range(2):
        yb[n, 0:36, :] = total[36 * n:36 * n + 36]
        yb[n, 36:40, :] = jnp.zeros((4, 128), F32)
    slot = jnp.where(core == 0, y, 4 + x)
    for n in range(2):
        sd = jnp.where(core == 0, x * 16 + z * 2 + n, (2 * y_hi + n) * 16 + z * 2 + y_lo)
        here = sd == s

        @pl.when(here)
        def keep():
            yr[slot] = yb[n]

        for j in range(4):
            send_part(
                jnp.logical_not(here & (f == j)), yb.at[n], yr.at[slot],
                y_ss.at[1], y_rs.at[1], j, sd,
            )

    all_of(goyr.at[pl.ds(0, 7)], y_ss.at[0], y_rs.at[0])
    for half in range(2):
        total = (goyr[half] + goyr[2 + half]) + (goyr[4 + half] + goyr[6 + half])
        for t in range(9):
            gout_ref[:, t * C + half * 128:t * C + (half + 1) * 128] = total[3 * t:3 * t + 3]
    seven = (core == 0) | (x // 2 == y_hi)
    all_of(yr.at[pl.ds(0, 7)], y_ss.at[1], y_rs.at[1], seven)
    all_of(yr, y_ss.at[1], y_rs.at[1], jnp.logical_not(seven))
    for half in range(2):
        total = (yr[4 * half] + yr[4 * half + 1]) + (yr[4 * half + 2] + yr[4 * half + 3])
        gconv_ref[:, half * 128:(half + 1) * 128] = total[0:36]

    for cond, copy in sends:
        guard(cond, copy.wait_send)


def per_device(latents, conv_weight, conv_bias, out_weight, row_table, patch_weight, pos_embed,
               proj_weight, text_embed):
    vmem = pl.BlockSpec(memory_space=pltpu.VMEM)
    hbm = pl.BlockSpec(memory_space=pltpu.HBM)
    V = pltpu.VMEM
    dma = pltpu.SemaphoreType.DMA
    reward, gconv, gout = pl.pallas_call(
        kernel,
        out_shape=(
            jax.ShapeDtypeStruct((1, 1), F32),
            jax.ShapeDtypeStruct((36, C), F32),
            jax.ShapeDtypeStruct((3, 9 * C), F32),
        ),
        in_specs=[hbm] * 9,
        out_specs=(vmem, vmem, vmem),
        scratch_shapes=[
            V((1, C), F32), V((3, 9 * C), BF16), V((1, IMG), jnp.int32), V((1, EMB), F32),
            V((4, WL, C), BF16),
            V((C, 9 * C), BF16),
            V((2 * WL, 9 * C), F32),
            V((2 * WL, 6 * C), BF16),
            V((2 * WL, 4 * C), F32),
            V((48, 6 * C), F32),
            V((48, C), F32),
            V((588, CW), BF16),
            V((KP, CW), BF16),
            V((CW, KP), BF16),
            V((32, CW), BF16),
            V((CW, EMB), BF16),
            V((EMB, CW), BF16),
            V((16, 256), BF16),
            V((9, 16, 256), BF16),
            V((256, 128), F32),
            V((256, 128), F32),
            V((256, 128), F32),
            V((32, CW), F32),
            V((1, CW), F32),
            V((GROUPS, 1, CW), F32),
            V((3, 32, 256), F32),
            V((C, 4 * WL), BF16),
            V((9 * C, 128), F32),
            V((9 * C, 128), BF16),
            V((9 * C, 128), BF16),
            V((4, 4, 144, 128), BF16),
            V((4, 4, 144, 128), F32),
            V((4, 4, 144, 128), BF16),
            V((8, 80, 128), BF16),
            V((8, 72, 128), F32),
            V((8, 80, 128), BF16),
            V((2, 40, 128), F32),
            V((8, 40, 128), F32),
            V((2, 32, 128), F32),
            V((32, 128), F32),
            V((32, 128), BF16),
            V((8, 32, 128), BF16),
            V((32, 128), F32),
            V((4, 32, 128), F32),
            V((32, 128), F32),
            V((8, 32, 128), F32),
            dma((9,)), dma((2,)), dma((2,)), dma((9,)), dma((9,)), dma((1,)), dma((1,)),
            dma((4,)), dma((4,)), dma((4,)), dma((4,)), dma((1,)), dma((1,)),
            dma((2,)), dma((2,)), dma((2,)), dma((2,)), pltpu.SemaphoreType.REGULAR((5,)),
        ],
        compiler_params=pltpu.CompilerParams(
            collective_id=0, has_side_effects=True, vmem_limit_bytes=48 * 1024 * 1024
        ),
    )(*[
        pltpu.with_memory_space_constraint(v, pltpu.HBM) for v in (
            latents, conv_weight, conv_bias.reshape(1, C), out_weight, row_table, patch_weight,
            pos_embed, proj_weight, text_embed.reshape(1, EMB),
        )
    ])
    return reward.reshape(1), gconv, gout


def solution(mesh):
    return jax.shard_map(
        per_device,
        mesh=mesh,
        in_specs=(
            P("frame", "slab", None, None), P(), P(), P(), P("frame", None), P(), P(), P(), P(),
        ),
        out_specs=(P("frame"), P("slab", None), P()),
        check_vma=False,
    )
```

```python
import jax
import jax.numpy as jnp
from jax import lax
from jax.experimental import pallas as pl
from jax.experimental.pallas import tpu as pltpu
from jax.sharding import PartitionSpec as P

MESH = pl.DeviceIdType.MESH
F32 = jnp.float32
BF16 = jnp.bfloat16

C = 256
CW = 1280
EMB = 1024
IMG = 224
PATCH = 14
WL = 128
N_SLAB = 64
GROUPS = 16
KP = 14 * 64
LOSS_SCALE = 256.0
EPS = 1e-05


def dot_nn(a, b):
    return lax.dot_general(a, b, (((1,), (0,)), ((), ())), preferred_element_type=F32)


def dot_nt(a, b):
    return lax.dot_general(a, b, (((1,), (1,)), ((), ())), preferred_element_type=F32)


def dot_tn(a, b):
    return lax.dot_general(a, b, (((0,), (0,)), ((), ())), preferred_element_type=F32)


def iota(shape, dim):
    return lax.broadcasted_iota(jnp.int32, shape, dim)


def split2(v):
    hi = v.astype(BF16)
    lo = (v - hi.astype(F32)).astype(BF16)
    return hi, lo


def lat_row(r6, a):
    return (r6 - 1 + a - 1) // 2 + 1


def patch_column(c14):
    c16 = c14 * 8 // 7
    return c16 % 2, c16 // 2


def kernel(
    lat_hbm, cw_hbm, bias_hbm, ow_hbm, table_hbm, pw_hbm, pos_hbm, proj_hbm, text_hbm,
    reward_ref, gconv_ref, gout_ref,
    bias_ref, ow_ref, table_ref, text_ref,
    lat4, wl, taps, hbuf, gate, wd32, wo32, pw, pwp, pwpt, pos, proj, projt,
    dec, dall, ct, ct2, gt, ybuf, psend, precv, igs, latt,
    g32, gbf, gcr, xbf, x32, xr, zbf, z32, zr, yb, yr,
    go2, gocr, goz, gozr, gox, goxr, goy, goyr,
    loc_sem, halo_ss, halo_rs, gat_ss, gat_rs, pool_ss, pool_rs,
    c_ss, c_rs, u_ss, u_rs, x_ss, x_rs, z_ss, z_rs, y_ss, y_rs, flood_sem,
):
    f = lax.axis_index("frame")
    s = lax.axis_index("slab")
    y_hi, core = f // 2, f % 2
    x, z, y_lo = s // 16, (s % 16) // 2, s % 2
    p, q = s // 4, s % 4
    low_half = q < 2
    base = jnp.where(low_half, 4 * p - 4, 4 * p)
    p2 = jnp.where(low_half, p - 1, p + 1)
    p2c = jnp.clip(p2, 0, GROUPS - 1)

    dall[...] = jnp.zeros_like(dall)
    lat4[0] = jnp.zeros((WL, C), BF16)
    lat4[3] = jnp.zeros((WL, C), BF16)

    barrier = pltpu.get_barrier_semaphore()

    def greet(cond, fd, sd):
        def go():
            pl.semaphore_signal(barrier, inc=1, device_id=(fd, sd), device_id_type=MESH)

        if cond is None:
            go()
        else:
            pl.when(cond)(go)

    greet(s > 0, f, s - 1)
    greet(s < N_SLAB - 1, f, s + 1)
    for d in range(1, 4):
        greet(None, f, 4 * p + (q + d) % 4)
    for v in range(4):
        greet((q == 0) & (p > 0), f, 4 * p - 4 + v)
        greet((q == 3) & (p < GROUPS - 1), f, 4 * p + 4 + v)
    greet((q < 3) & (p < GROUPS - 1), f, 4 * p + 4)
    for d in range(1, 4):
        greet(None, f, ((x + d) % 4) * 16 + z * 2 + y_lo)
    for d in (2, 6):
        greet(None, f, x * 16 + ((z + d) % 8) * 2 + y_lo)
    yc = y_hi * 4 + y_lo * 2 + core

    def yc_device(idx):
        return (idx // 4) * 2 + idx % 2, x * 16 + z * 2 + (idx // 2) % 2

    for d in range(1, 8):
        greet(None, *yc_device((yc + d) % 8))
    y = y_hi * 2 + y_lo

    def one(cond):
        return jnp.where(cond, 1, 0)

    expected = (
        one(s > 0) + one(s < N_SLAB - 1)
        + 3 + one(p < GROUPS - 1) + one(p > 0)
        + one((q == 0) & (p > 0)) * 3
        + 3 + 2 + 7
    )

    loads = []

    def load(src, dst):
        copy = pltpu.make_async_copy(src, dst, loc_sem.at[len(loads)])
        copy.start()
        loads.append(copy)
        return copy

    def load_parts(pairs, whole):
        sem = loc_sem.at[len(loads)]
        for src, dst in pairs:
            pltpu.make_async_copy(src, dst, sem).start()
        copy = pltpu.make_async_copy(whole, whole, sem)
        loads.append(copy)
        return copy

    lat_load = load(lat_hbm.at[0], lat4.at[pl.ds(1, 2)])
    w_load = load_parts(
        [
            (cw_hbm.at[pl.ds(t * C, C)], wl.at[:, pl.ds(t * C, C)])
            for t in range(9)
        ],
        wl,
    )

    pl.semaphore_wait(barrier, expected)

    def flood(stage):
        for n, d in enumerate((2, 6)):
            pl.semaphore_signal(
                flood_sem.at[2 * stage + n], inc=1,
                device_id=(f, x * 16 + ((z + d) % 8) * 2 + y_lo), device_id_type=MESH,
            )

    def flood_wait(stage):
        for n in range(2):
            pl.semaphore_wait(flood_sem.at[2 * stage + n], 1)

    flood(0)

    @pl.when((q == 0) & (p < GROUPS - 1))
    def tell():
        pl.semaphore_signal(
            flood_sem.at[4], inc=1, device_id=(f, s + 4), device_id_type=MESH
        )

    sends = []

    def remote(src, dst, ssem, rsem, fd, sd):
        return pltpu.make_async_remote_copy(
            src_ref=src, dst_ref=dst, send_sem=ssem, recv_sem=rsem,
            device_id=(fd, sd), device_id_type=MESH,
        )

    def guard(cond, action):
        if cond is None:
            action()
        else:
            pl.when(cond)(action)

    def send(cond, *what):
        copy = remote(*what)
        guard(cond, copy.start)
        sends.append((cond, copy))
        return copy

    def send_part(cond, *what):
        guard(cond, remote(*what).start)

    def all_of(whole, ssem, rsem, cond=None):
        copy = remote(whole, whole, ssem, rsem, y_hi * 2 + 1 - core, s)
        sends.append((cond, copy))
        guard(cond, copy.wait_recv)

    up = send(s > 0, lat_hbm.at[0, 0], lat4.at[3], halo_ss.at[0], halo_rs.at[1], f, s - 1)
    down = send(
        s < N_SLAB - 1, lat_hbm.at[0, 1], lat4.at[0], halo_ss.at[1], halo_rs.at[0], f, s + 1
    )

    ow_load = load(ow_hbm, ow_ref)
    bias_load = load(bias_hbm, bias_ref)
    table_load = load(table_hbm, table_ref)
    text_load = load(text_hbm, text_ref)
    pw_load = load(pw_hbm, pw)
    pos_load = load_parts(
        [
            (pos_hbm.at[pl.ds(pl.multiple_of(16 * p, 16), 16)], pos.at[pl.ds(0, 16)]),
            (pos_hbm.at[pl.ds(pl.multiple_of(16 * p2c, 16), 16)], pos.at[pl.ds(16, 16)]),
        ],
        pos,
    )
    proj_load = load(proj_hbm, proj)

    wd32[...] = jnp.zeros_like(wd32)
    wo32[...] = jnp.zeros_like(wo32)
    ow_load.wait()
    for a in range(3):
        for b in range(3):
            t = 3 * a + b
            tap = ow_ref[:, t * C:(t + 1) * C].astype(F32)
            wo32[b * 16 + (2 - a) * 4:b * 16 + (2 - a) * 4 + 3, :] = tap
            for r in range(4):
                wd32[b * 16 + r * 4:b * 16 + r * 4 + 3, (r + a) * C:(r + a + 1) * C] = tap

    bias_load.wait()
    bias = bias_ref[...]
    first = iota((WL, C), 0) == 0
    last = iota((WL, C), 0) == WL - 1

    def activate(r6, z0, z1, z2):
        before = jnp.where(first, 0.0, pltpu.roll(z0, 1, 0))
        after = jnp.where(last, 0.0, pltpu.roll(z2, WL - 1, 0))
        for pc, total in ((0, before + z1 + z2), (1, z0 + z1 + after)):
            total = total + bias
            hidden = total * (0.5 + 0.5 * jnp.tanh(0.5 * total))
            if r6 == 0:
                hidden = jnp.where(s > 0, hidden, 0.0)
            elif r6 == 5:
                hidden = jnp.where(s < N_SLAB - 1, hidden, 0.0)
            else:
                gate[pc * WL:(pc + 1) * WL, (r6 - 1) * C:r6 * C] = total
            hbuf[pc * WL:(pc + 1) * WL, r6 * C:(r6 + 1) * C] = hidden.astype(BF16)

    lat_load.wait()
    w_load.wait()

    taps[...] = dot_nn(lat4[1:3].reshape(2 * WL, C), wl[...])

    def part(row, a, b):
        t = 3 * a + b
        return taps[(row - 1) * WL:row * WL, t * C:(t + 1) * C]

    def own_terms(r6, b):
        rows = [(lat_row(r6, a), a) for a in range(3)]
        return sum(part(row, a, b) for row, a in rows if row in (1, 2))

    for r6 in (2, 3):
        activate(r6, *[own_terms(r6, b) for b in range(3)])

    guard(s < N_SLAB - 1, up.wait_recv)
    guard(s > 0, down.wait_recv)
    flood_wait(0)
    flood(1)
    for near, far, edge, start in ((1, 0, 0, 0), (4, 5, 3, 3)):
        halo_z = dot_nn(lat4[edge], wl[:, start * C:(start + 6) * C])
        inner = [halo_z[:, (b if near == 1 else b + 3) * C:][:, 0:C] for b in range(3)]
        outer = [halo_z[:, (b + 3 if near == 1 else b) * C:][:, 0:C] for b in range(3)]
        activate(near, *[own_terms(near, b) + inner[b] for b in range(3)])
        activate(far, *[own_terms(far, b) + (inner[b] + outer[b]) for b in range(3)])

    res = dot_nt(wd32[...].astype(BF16), hbuf[...])
    even, odd = res[:, 0:WL], res[:, WL:2 * WL]
    left = iota((16, WL), 1) == 0
    right = iota((16, WL), 1) == WL - 1
    dec_even = jnp.where(left, 0.0, pltpu.roll(odd[0:16], 1, 1)) + even[16:32] + odd[32:48]
    dec_odd = even[0:16] + odd[16:32] + jnp.where(right, 0.0, pltpu.roll(even[32:48], WL - 1, 1))
    decoded = jnp.concatenate([dec_even, dec_odd], axis=1).astype(BF16)
    dec[...] = decoded
    dall[jnp.where(low_half, q + 4, q)] = decoded

    @pl.when((q == 0) & (p > 0))
    def told():
        pl.semaphore_wait(flood_sem.at[4], 1)

    def gather_send(n, cond, target, slot):
        send(cond, dec, dall.at[slot], gat_ss.at[n], gat_rs.at[slot], f, target)

    gather_send(5, (q == 0) & (p > 0), 4 * p - 4, 8)
    gather_send(6, (q == 0) & (p > 0), 4 * p - 3, 8)
    gather_send(7, (q == 0) & (p > 0), 4 * p - 2, 4)
    for d in range(1, 4):
        qd = (q + d) % 4
        gather_send(d - 1, None, 4 * p + qd, jnp.where(qd < 2, q + 4, q))
    gather_send(3, p < GROUPS - 1, 4 * p + 4, q)
    gather_send(4, p > 0, 4 * p - 1, q + 4)
    gather_send(8, (q == 0) & (p > 1), 4 * p - 5, 8)

    rk = iota((128, 1), 0)
    g = rk & 63
    colour = one(g >= 14) + one(g >= 28)
    ig = jnp.where(rk < 64, p, p2) * PATCH + g - 14 * colour
    valid = (g < 42) & (ig >= 0) & (ig < IMG)
    table_load.wait()
    table = table_ref[...].astype(F32)
    cols = iota((128, IMG), 1)
    lo = jnp.sum(jnp.where(cols == ig, table, 0.0), axis=1, keepdims=True)
    nxt = jnp.sum(jnp.where(cols == ig + 1, table, 0.0), axis=1, keepdims=True)
    nxt = nxt + jnp.where(ig == IMG - 1, 256.0, 0.0)
    hi = jnp.maximum(nxt, lo + 1.0)
    inv = 1.0 / (hi - lo)
    lane = iota((128, 144), 1)
    row = (4 * jnp.where(rk < 64, 4 * p, base) + (lane >> 2)).astype(F32)
    inside = valid & ((lane & 3) == colour) & (row >= lo) & (row < hi)
    pick = jnp.where(inside, 1.0, 0.0).astype(BF16)
    lane = iota((128, 128), 1)
    row = (4 * s - 1 + (lane >> 2)).astype(F32)
    inside = valid & ((lane & 3) == colour) & (row >= lo) & (row < hi) & (lane < 24)
    both = jnp.where(lane == 32, inv, jnp.where(inside, 1.0, 0.0)).T
    back = both[0:32].astype(BF16)
    back = jnp.concatenate([back, back], axis=1)
    inv_row = both[32:33]

    pw_load.wait()
    prow = iota((KP, 588), 0)
    pg = prow & 63
    order = jnp.where(
        (pg < 42) & (iota((KP, 588), 1) == 14 * pg + 2 * (prow >> 7) + ((prow >> 6) & 1)), 1.0, 0.0
    ).astype(BF16)
    for n in range(CW // 256):
        cut = slice(n * 256, (n + 1) * 256)
        pwp[:, cut] = dot_nn(order, pw[:, cut]).astype(BF16)

    def gather_wait(slot, cond, source):
        copy = remote(dec, dall.at[slot], gat_ss.at[0], gat_rs.at[slot], f, source)
        pl.when(cond)(copy.wait_recv)

    more = p < GROUPS - 1
    for v in range(4):
        gather_wait(v, (q >= 2) & (q != v), 4 * p + v)
        gather_wait(v + 4, low_half & (q != v), 4 * p + v)
    gather_wait(4, (q >= 2) & more, 4 * p + 4)
    gather_wait(8, low_half & more, 4 * p + 4)
    lane16 = iota((16, 128), 1) < 64

    def patch_parts(crop, turned):
        turned[...] = jnp.concatenate([crop, jnp.zeros((64, 256), F32)], axis=0).T
        columns = []
        for c14 in range(14):
            pc, pj = patch_column(c14)
            columns.append(turned[pl.ds(pc * WL + pj, 16, stride=8), :])
        return [
            jnp.where(lane16, columns[2 * n], pltpu.roll(columns[2 * n + 1], 64, 1))
            for n in range(7)
        ]

    own_rows = dall[pl.ds(jnp.where(low_half, 4, 0), 5)].reshape(80, 256)
    own_parts = patch_parts(dot_nn(pick[0:64, 0:80], own_rows) * inv[0:64], ct)
    pos_load.wait()

    def embed(parts, rows):
        patches = jnp.concatenate(parts, axis=1)
        emb = dot_nn(jnp.concatenate(split2(patches), axis=0), pwp[...])
        emb = emb[0:16] + emb[16:32] + pos[rows, :].astype(F32)
        centred = emb - jnp.mean(emb, axis=1, keepdims=True)
        sigma = jnp.sqrt(jnp.mean(centred * centred, axis=1, keepdims=True) + EPS)
        normed = centred / sigma
        ybuf[rows, :] = normed
        return normed, sigma

    normed, sigma0 = embed(own_parts, slice(0, 16))
    gsum = jnp.sum(normed, axis=0, keepdims=True)
    psend[...] = gsum
    precv[p] = gsum

    flood_wait(1)
    steps = [(dx, dz) for dx in range(4) for dz in range(4) if dx or dz]
    steps.sort(key=lambda d: -min(d[0], 4 - d[0]) - 2 * min(d[1], 4 - d[1]))
    for dx, dz in steps:
        other = ((x + dx) % 4) * 4 + (z // 2 + dz) % 4
        send_part(None, psend, precv.at[p], pool_ss.at[0], pool_rs.at[0], f, 4 * other + q)

    for v in range(4):
        gather_wait(v, (q == 0) & (p > 0), 4 * p - 4 + v)
        if v > 0:
            gather_wait(v + 4, (q == 3) & more, 4 * p + 4 + v)
    gather_wait(8, (q == 3) & (p < GROUPS - 2), 4 * p + 8)
    next_crop = dot_nn(pick[64:128], dall[...].reshape(144, 256)) * inv[64:128]
    sigma1 = embed(patch_parts(next_crop, ct2), slice(16, 32))[1]
    sigma = jnp.concatenate([sigma0, sigma1], axis=0)

    for n in range(4):
        cut = slice(n * C, (n + 1) * C)
        total = gate[:, cut]
        sig = 0.5 + 0.5 * jnp.tanh(0.5 * total)
        gate[:, cut] = sig * (1.0 + total * (1.0 - sig))
    for n in range(4):
        latt[:, n * WL:(n + 1) * WL] = lat4[n].astype(F32).T.astype(BF16)
    proj_load.wait()
    for n in range(CW // 256):
        cut = slice(n * 256, (n + 1) * 256)
        projt[:, cut] = proj[cut, :].astype(F32).T.astype(BF16)
    for n in range(KP // 128):
        cut = slice(n * 128, (n + 1) * 128)
        pwpt[:, cut] = pwp[cut, :].astype(F32).T.astype(BF16)
    text_load.wait()
    text = text_ref[...]
    text2 = jnp.sum(text * text, axis=1, keepdims=True) + 1e-06
    gt[...] = jnp.zeros_like(gt)

    all_of(precv.at[pl.ds(0, GROUPS - 1)], pool_ss.at[0], pool_rs.at[0])
    pooled = precv[0]
    for n in range(1, GROUPS):
        pooled = pooled + precv[n]
    pooled = pooled * (1.0 / 256.0)


    def two_rows(v):
        top = iota((16, v.shape[1]), 0)
        hi_part = v.astype(BF16).astype(F32)
        return jnp.where(top == 0, hi_part, jnp.where(top == 1, v - hi_part, 0.0)).astype(BF16)

    pc_ = pooled - jnp.mean(pooled, axis=1, keepdims=True)
    psigma = jnp.sqrt(jnp.mean(pc_ * pc_, axis=1, keepdims=True) + EPS)
    unit = pc_ / psigma
    projected = jnp.sum(dot_nn(two_rows(unit), proj[...]), axis=0, keepdims=True)
    numer = jnp.sum(projected * text, axis=1, keepdims=True)
    norm2 = jnp.sum(projected * projected, axis=1, keepdims=True) + 1e-06
    scale = 1.0 / jnp.sqrt(norm2 * text2)
    reward = numer * scale
    reward_ref[...] = reward
    dproj = -LOSS_SCALE * (text * scale - projected * (reward / norm2))
    dunit = jnp.sum(dot_nn(two_rows(dproj), projt[...]), axis=0, keepdims=True)

    def norm_back(dy, y, sg):
        m1 = jnp.mean(dy, axis=1, keepdims=True)
        m2 = jnp.mean(dy * y, axis=1, keepdims=True)
        return (dy - m1 - y * m2) / sg

    dpooled = norm_back(dunit, unit, psigma) * (1.0 / 256.0)
    demb = norm_back(dpooled, ybuf[...], sigma)
    dpat = dot_nn(jnp.concatenate(split2(demb), axis=0), pwpt[...])
    dpat = dpat[0:32] + dpat[32:64]
    for n in range(7):
        d0 = dpat[0:16, n * 128:(n + 1) * 128]
        d1 = dpat[16:32, n * 128:(n + 1) * 128]
        pair = (
            jnp.where(lane16, d0, pltpu.roll(d1, 64, 1)),
            jnp.where(lane16, pltpu.roll(d0, 64, 1), d1),
        )
        for half in range(2):
            pc, pj = patch_column(2 * n + half)
            gt[pl.ds(pc * WL + pj, 16, stride=8), :] = pair[half]

    grows = jnp.concatenate(split2(gt[...] * inv_row), axis=1)
    image = dot_nt(back, grows).astype(BF16).astype(F32)
    even, odd = image[:, 0:WL], image[:, WL:2 * WL]
    left = iota((32, WL), 1) == 0
    right = iota((32, WL), 1) == WL - 1
    odd_before = jnp.where(left, 0.0, pltpu.roll(odd, 1, 1))
    even_after = jnp.where(right, 0.0, pltpu.roll(even, WL - 1, 1))
    igs[0] = jnp.concatenate([odd, even_after], axis=1)
    igs[1] = image
    igs[2] = jnp.concatenate([odd_before, even], axis=1)

    ims = []
    go = jnp.zeros((48, C), F32)
    for r in range(4):
        im = jnp.concatenate([igs[b, 4 * r:4 * r + 16, :] for b in range(3)], axis=0).astype(BF16)
        ims.append(im)
        go = go + dot_nn(im, hbuf[:, (r + 1) * C:(r + 2) * C])
    for half in range(2):
        go2[half, 27:32, :] = jnp.zeros((5, 128), F32)
        for t in range(9):
            at = (t % 3) * 16 + (2 - t // 3) * 4
            go2[half, 3 * t:3 * t + 3, :] = go[at:at + 3, half * 128:(half + 1) * 128]
    fc = y_hi * 2 + 1 - core
    outk = send(None, go2.at[1 - core], gocr, c_ss.at[3], c_rs.at[3], fc, s)

    wout = wo32[...].astype(BF16)
    cols_of = []
    for r in range(4):
        cg = dot_tn(ims[r], wout) * gate[:, r * C:(r + 1) * C]
        ev, od = cg[0:WL], cg[WL:2 * WL]
        od_before = jnp.where(first, 0.0, pltpu.roll(od, 1, 0))
        ev_after = jnp.where(last, 0.0, pltpu.roll(ev, WL - 1, 0))
        cols_of.append((od + ev_after, ev + od, od_before + ev))

    def put_grad(a, b, value):
        at = (3 * a + b) * C
        left, right = value[:, 0:128], value[:, 128:256]
        g32[at:at + C, :] = jnp.where(core == 0, left, right)
        gbf[at:at + C, :] = jnp.where(core == 0, right, left).astype(BF16)

    outer = [
        jnp.concatenate([cols_of[0][b], cols_of[1][b] + cols_of[2][b], cols_of[3][b]], axis=0)
        .astype(BF16) for b in range(3)
    ]
    inner = [
        jnp.concatenate([cols_of[0][b] + cols_of[1][b], cols_of[2][b] + cols_of[3][b]], axis=0)
        .astype(BF16) for b in range(3)
    ]
    outk.wait_recv()
    gsum_z = go2[core] + gocr[...]
    goz[...] = gsum_z.astype(BF16)
    for d in range(1, 8):
        zd = (z + d) % 8
        send_part(None, goz, gozr.at[z], z_ss.at[0], z_rs.at[0], f, x * 16 + zd * 2 + y_lo)

    main = []
    outer = jnp.concatenate(outer, axis=1)
    inner = jnp.concatenate(inner, axis=1)
    for a, start, stop, terms in ((0, 0, 3, outer), (1, 1, 3, inner), (2, 1, 4, outer)):
        value = dot_nn(latt[:, start * WL:stop * WL], terms)
        for b in range(3):
            put_grad(a, b, value[:, b * C:(b + 1) * C])
        rows = pl.ds(a * 768, 768)
        main.append(
            send(None, gbf.at[rows], gcr.at[rows], c_ss.at[a], c_rs.at[a], fc, s)
        )

    mine = jnp.where(core == 0, x, y)

    def quarter_device(n):
        fd = jnp.where(core == 0, f, (n // 2) * 2 + 1)
        sd = jnp.where(core == 0, n * 16 + z * 2 + y_lo, x * 16 + z * 2 + n % 2)
        return fd, sd

    def halves_sum(start, count):
        return g32[start:start + count, :] + gcr[start:start + count, :].astype(F32)

    for w in range(4):
        for part in range(2):
            if w == 0 and part == 0:
                main[0].wait_recv()
                main[1].wait_recv()
            elif w == 0:
                main[2].wait_recv()

            @pl.when(core == 0)
            def along_x():
                for n in (2 * part, 2 * part + 1):
                    total = jnp.concatenate(
                        [halves_sum(n * 576 + zd * 72, 72) for zd in (w, w + 4)], axis=0
                    )
                    x32[n, w] = total
                    xbf[n, w] = total.astype(BF16)

            @pl.when(core == 1)
            def along_y():
                units = [
                    halves_sum((2 * part + h) * 576 + zd * 72, 72)
                    for zd in (w, w + 4) for h in range(2)
                ]
                for n in range(2):
                    total = jnp.concatenate([u[36 * n:36 * n + 36] for u in units], axis=0)
                    x32[2 * part + n, w] = total
                    xbf[2 * part + n, w] = total.astype(BF16)

            for n in (2 * part, 2 * part + 1):
                send_part(
                    mine != n, xbf.at[n, w], xr.at[w, mine], u_ss.at[w], u_rs.at[w],
                    *quarter_device(n),
                )

    for w in range(4):
        xr[w, mine] = jnp.zeros((144, 128), BF16)
    zr[z] = jnp.zeros((80, 128), BF16)
    for w in range(4):
        all_of(xr.at[w, pl.ds(0, 3)], u_ss.at[w], u_rs.at[w])
        for k in range(2):
            zd = w + 4 * k
            cut = slice(k * 72, (k + 1) * 72)
            total = x32[mine, w, cut, :]
            for n in range(4):
                total = total + xr[w, n, cut, :].astype(F32)
            z32[zd] = total
            zbf[zd] = jnp.concatenate([total, jnp.zeros((8, 128), F32)], axis=0).astype(BF16)
            send_part(
                z != zd, zbf.at[zd], zr.at[z], z_ss.at[1], z_rs.at[1], f, x * 16 + zd * 2 + y_lo
            )
        if w == 1:
            gozr[z] = jnp.zeros((32, 128), BF16)
            all_of(gozr.at[pl.ds(0, 7)], z_ss.at[0], z_rs.at[0])
            gsum_x = gsum_z + jnp.sum(gozr[...].astype(F32), axis=0)
            gox[...] = gsum_x
            for d in range(1, 4):
                xd = (x + d) % 4
                send_part(
                    None, gox, goxr.at[x], x_ss.at[0], x_rs.at[0], f, xd * 16 + z * 2 + y_lo
                )

    goxr[x] = gsum_x
    all_of(goxr.at[pl.ds(0, 3)], x_ss.at[0], x_rs.at[0])
    gsum_y = jnp.sum(goxr[...], axis=0)
    goy[...] = gsum_y
    for d in range(1, 8):
        yd = (yc + d) % 8
        send_part(None, goy, goyr.at[yc], y_ss.at[0], y_rs.at[0], *yc_device(yd))
    goyr[yc] = gsum_y

    all_of(zr.at[pl.ds(0, 7)], z_ss.at[1], z_rs.at[1])
    total = z32[z]
    for n in range(8):
        total = total + zr[n, 0:72, :].astype(F32)

    for n in range(2):
        yb[n, 0:36, :] = total[36 * n:36 * n + 36]
        yb[n, 36:40, :] = jnp.zeros((4, 128), F32)
    slot = jnp.where(core == 0, y, 4 + x)
    for n in range(2):
        sd = jnp.where(core == 0, x * 16 + z * 2 + n, (2 * y_hi + n) * 16 + z * 2 + y_lo)
        here = sd == s

        @pl.when(here)
        def keep():
            yr[slot] = yb[n]

        for j in range(4):
            send_part(
                jnp.logical_not(here & (f == j)), yb.at[n], yr.at[slot],
                y_ss.at[1], y_rs.at[1], j, sd,
            )

    all_of(goyr.at[pl.ds(0, 7)], y_ss.at[0], y_rs.at[0])
    for half in range(2):
        total = (goyr[half] + goyr[2 + half]) + (goyr[4 + half] + goyr[6 + half])
        for t in range(9):
            gout_ref[:, t * C + half * 128:t * C + (half + 1) * 128] = total[3 * t:3 * t + 3]
    seven = (core == 0) | (x // 2 == y_hi)
    all_of(yr.at[pl.ds(0, 7)], y_ss.at[1], y_rs.at[1], seven)
    all_of(yr, y_ss.at[1], y_rs.at[1], jnp.logical_not(seven))
    for half in range(2):
        total = (yr[4 * half] + yr[4 * half + 1]) + (yr[4 * half + 2] + yr[4 * half + 3])
        gconv_ref[:, half * 128:(half + 1) * 128] = total[0:36]

    for cond, copy in sends:
        guard(cond, copy.wait_send)


def per_device(latents, conv_weight, conv_bias, out_weight, row_table, patch_weight, pos_embed,
               proj_weight, text_embed):
    vmem = pl.BlockSpec(memory_space=pltpu.VMEM)
    hbm = pl.BlockSpec(memory_space=pltpu.HBM)
    V = pltpu.VMEM
    dma = pltpu.SemaphoreType.DMA
    reward, gconv, gout = pl.pallas_call(
        kernel,
        out_shape=(
            jax.ShapeDtypeStruct((1, 1), F32),
            jax.ShapeDtypeStruct((36, C), F32),
            jax.ShapeDtypeStruct((3, 9 * C), F32),
        ),
        in_specs=[hbm] * 9,
        out_specs=(vmem, vmem, vmem),
        scratch_shapes=[
            V((1, C), F32), V((3, 9 * C), BF16), V((1, IMG), jnp.int32), V((1, EMB), F32),
            V((4, WL, C), BF16),
            V((C, 9 * C), BF16),
            V((2 * WL, 9 * C), F32),
            V((2 * WL, 6 * C), BF16),
            V((2 * WL, 4 * C), F32),
            V((48, 6 * C), F32),
            V((48, C), F32),
            V((588, CW), BF16),
            V((KP, CW), BF16),
            V((CW, KP), BF16),
            V((32, CW), BF16),
            V((CW, EMB), BF16),
            V((EMB, CW), BF16),
            V((16, 256), BF16),
            V((9, 16, 256), BF16),
            V((256, 128), F32),
            V((256, 128), F32),
            V((256, 128), F32),
            V((32, CW), F32),
            V((1, CW), F32),
            V((GROUPS, 1, CW), F32),
            V((3, 32, 256), F32),
            V((C, 4 * WL), BF16),
            V((9 * C, 128), F32),
            V((9 * C, 128), BF16),
            V((9 * C, 128), BF16),
            V((4, 4, 144, 128), BF16),
            V((4, 4, 144, 128), F32),
            V((4, 4, 144, 128), BF16),
            V((8, 80, 128), BF16),
            V((8, 72, 128), F32),
            V((8, 80, 128), BF16),
            V((2, 40, 128), F32),
            V((8, 40, 128), F32),
            V((2, 32, 128), F32),
            V((32, 128), F32),
            V((32, 128), BF16),
            V((8, 32, 128), BF16),
            V((32, 128), F32),
            V((4, 32, 128), F32),
            V((32, 128), F32),
            V((8, 32, 128), F32),
            dma((9,)), dma((2,)), dma((2,)), dma((9,)), dma((9,)), dma((1,)), dma((1,)),
            dma((4,)), dma((4,)), dma((4,)), dma((4,)), dma((1,)), dma((1,)),
            dma((2,)), dma((2,)), dma((2,)), dma((2,)), pltpu.SemaphoreType.REGULAR((5,)),
        ],
        compiler_params=pltpu.CompilerParams(
            collective_id=0, has_side_effects=True, vmem_limit_bytes=48 * 1024 * 1024
        ),
    )(*[
        pltpu.with_memory_space_constraint(v, pltpu.HBM) for v in (
            latents, conv_weight, conv_bias.reshape(1, C), out_weight, row_table, patch_weight,
            pos_embed, proj_weight, text_embed.reshape(1, EMB),
        )
    ])
    return reward.reshape(1), gconv, gout


def solution(mesh):
    return jax.shard_map(
        per_device,
        mesh=mesh,
        in_specs=(
            P("frame", "slab", None, None), P(), P(), P(), P("frame", None), P(), P(), P(), P(),
        ),
        out_specs=(P("frame"), P("slab", None), P()),
        check_vma=False,
    )
```

```python
import jax
import jax.numpy as jnp
from jax import lax
from jax.experimental import pallas as pl
from jax.experimental.pallas import tpu as pltpu
from jax.sharding import PartitionSpec as P

MESH = pl.DeviceIdType.MESH
F32 = jnp.float32
BF16 = jnp.bfloat16

C = 256
CW = 1280
EMB = 1024
IMG = 224
PATCH = 14
WL = 128
N_SLAB = 64
GROUPS = 16
KP = 14 * 64
LOSS_SCALE = 256.0
EPS = 1e-05


def dot_nn(a, b):
    return lax.dot_general(a, b, (((1,), (0,)), ((), ())), preferred_element_type=F32)


def dot_nt(a, b):
    return lax.dot_general(a, b, (((1,), (1,)), ((), ())), preferred_element_type=F32)


def dot_tn(a, b):
    return lax.dot_general(a, b, (((0,), (0,)), ((), ())), preferred_element_type=F32)


def iota(shape, dim):
    return lax.broadcasted_iota(jnp.int32, shape, dim)


def split2(v):
    hi = v.astype(BF16)
    lo = (v - hi.astype(F32)).astype(BF16)
    return hi, lo


def lat_row(r6, a):
    return (r6 - 1 + a - 1) // 2 + 1


def patch_column(c14):
    c16 = c14 * 8 // 7
    return c16 % 2, c16 // 2


def kernel(
    lat_hbm, cw_hbm, bias_hbm, ow_hbm, table_hbm, pw_hbm, pos_hbm, proj_hbm, text_hbm,
    reward_ref, gconv_ref, gout_ref,
    bias_ref, ow_ref, table_ref, text_ref,
    lat4, wl, taps, hbuf, gate, wd32, wo32, pw, pwp, pwpt, pos, proj, projt,
    dec, dall, ct, ct2, gt, ybuf, psend, precv, igs, latt,
    g32, gbf, gcr, xbf, x32, xr, zbf, z32, zr, yb, yr,
    go2, gocr, goz, gozr, gox, goxr, goy, goyr,
    loc_sem, halo_ss, halo_rs, gat_ss, gat_rs, pool_ss, pool_rs,
    c_ss, c_rs, u_ss, u_rs, x_ss, x_rs, z_ss, z_rs, y_ss, y_rs, flood_sem,
):
    f = lax.axis_index("frame")
    s = lax.axis_index("slab")
    y_hi, core = f // 2, f % 2
    x, z, y_lo = s // 16, (s % 16) // 2, s % 2
    p, q = s // 4, s % 4
    low_half = q < 2
    base = jnp.where(low_half, 4 * p - 4, 4 * p)
    p2 = jnp.where(low_half, p - 1, p + 1)
    p2c = jnp.clip(p2, 0, GROUPS - 1)

    dall[...] = jnp.zeros_like(dall)
    lat4[0] = jnp.zeros((WL, C), BF16)
    lat4[3] = jnp.zeros((WL, C), BF16)

    barrier = pltpu.get_barrier_semaphore()

    def greet(cond, fd, sd):
        def go():
            pl.semaphore_signal(barrier, inc=1, device_id=(fd, sd), device_id_type=MESH)

        if cond is None:
            go()
        else:
            pl.when(cond)(go)

    greet(s > 0, f, s - 1)
    greet(s < N_SLAB - 1, f, s + 1)
    for d in range(1, 4):
        greet(None, f, 4 * p + (q + d) % 4)
    for v in range(4):
        greet((q == 0) & (p > 0), f, 4 * p - 4 + v)
        greet((q == 3) & (p < GROUPS - 1), f, 4 * p + 4 + v)
    greet((q < 3) & (p < GROUPS - 1), f, 4 * p + 4)
    for d in range(1, 4):
        greet(None, f, ((x + d) % 4) * 16 + z * 2 + y_lo)
    for d in (2, 6):
        greet(None, f, x * 16 + ((z + d) % 8) * 2 + y_lo)
    yc = y_hi * 4 + y_lo * 2 + core

    def yc_device(idx):
        return (idx // 4) * 2 + idx % 2, x * 16 + z * 2 + (idx // 2) % 2

    greet(None, y_hi * 2 + 1 - core, s)
    greet(None, (1 - y_hi) * 2 + core, s)
    y = y_hi * 2 + y_lo

    def one(cond):
        return jnp.where(cond, 1, 0)

    expected = (
        one(s > 0) + one(s < N_SLAB - 1)
        + 3 + one(p < GROUPS - 1) + one(p > 0)
        + one((q == 0) & (p > 0)) * 3
        + 3 + 2 + 2
    )

    loads = []

    def load(src, dst):
        copy = pltpu.make_async_copy(src, dst, loc_sem.at[len(loads)])
        copy.start()
        loads.append(copy)
        return copy

    def load_parts(pairs, whole):
        sem = loc_sem.at[len(loads)]
        for src, dst in pairs:
            pltpu.make_async_copy(src, dst, sem).start()
        copy = pltpu.make_async_copy(whole, whole, sem)
        loads.append(copy)
        return copy

    lat_load = load(lat_hbm.at[0], lat4.at[pl.ds(1, 2)])
    w_load = load_parts(
        [
            (cw_hbm.at[pl.ds(t * C, C)], wl.at[:, pl.ds(t * C, C)])
            for t in range(9)
        ],
        wl,
    )

    pl.semaphore_wait(barrier, expected)

    def flood(stage):
        for n, d in enumerate((2, 6)):
            pl.semaphore_signal(
                flood_sem.at[2 * stage + n], inc=1,
                device_id=(f, x * 16 + ((z + d) % 8) * 2 + y_lo), device_id_type=MESH,
            )

    def flood_wait(stage):
        for n in range(2):
            pl.semaphore_wait(flood_sem.at[2 * stage + n], 1)

    flood(0)

    @pl.when((q == 0) & (p < GROUPS - 1))
    def tell():
        pl.semaphore_signal(
            flood_sem.at[4], inc=1, device_id=(f, s + 4), device_id_type=MESH
        )

    sends = []

    def remote(src, dst, ssem, rsem, fd, sd):
        return pltpu.make_async_remote_copy(
            src_ref=src, dst_ref=dst, send_sem=ssem, recv_sem=rsem,
            device_id=(fd, sd), device_id_type=MESH,
        )

    def guard(cond, action):
        if cond is None:
            action()
        else:
            pl.when(cond)(action)

    def send(cond, *what):
        copy = remote(*what)
        guard(cond, copy.start)
        sends.append((cond, copy))
        return copy

    def send_part(cond, *what):
        guard(cond, remote(*what).start)

    def all_of(whole, ssem, rsem, cond=None):
        copy = remote(whole, whole, ssem, rsem, y_hi * 2 + 1 - core, s)
        sends.append((cond, copy))
        guard(cond, copy.wait_recv)

    up = send(s > 0, lat_hbm.at[0, 0], lat4.at[3], halo_ss.at[0], halo_rs.at[1], f, s - 1)
    down = send(
        s < N_SLAB - 1, lat_hbm.at[0, 1], lat4.at[0], halo_ss.at[1], halo_rs.at[0], f, s + 1
    )

    ow_load = load(ow_hbm, ow_ref)
    bias_load = load(bias_hbm, bias_ref)
    table_load = load(table_hbm, table_ref)
    text_load = load(text_hbm, text_ref)
    pw_load = load(pw_hbm, pw)
    pos_load = load_parts(
        [
            (pos_hbm.at[pl.ds(pl.multiple_of(16 * p, 16), 16)], pos.at[pl.ds(0, 16)]),
            (pos_hbm.at[pl.ds(pl.multiple_of(16 * p2c, 16), 16)], pos.at[pl.ds(16, 16)]),
        ],
        pos,
    )
    proj_load = load(proj_hbm, proj)

    wd32[...] = jnp.zeros_like(wd32)
    wo32[...] = jnp.zeros_like(wo32)
    ow_load.wait()
    for a in range(3):
        for b in range(3):
            t = 3 * a + b
            tap = ow_ref[:, t * C:(t + 1) * C].astype(F32)
            wo32[b * 16 + (2 - a) * 4:b * 16 + (2 - a) * 4 + 3, :] = tap
            for r in range(4):
                wd32[b * 16 + r * 4:b * 16 + r * 4 + 3, (r + a) * C:(r + a + 1) * C] = tap

    bias_load.wait()
    bias = bias_ref[...]
    first = iota((WL, C), 0) == 0
    last = iota((WL, C), 0) == WL - 1

    def activate(r6, z0, z1, z2):
        before = jnp.where(first, 0.0, pltpu.roll(z0, 1, 0))
        after = jnp.where(last, 0.0, pltpu.roll(z2, WL - 1, 0))
        for pc, total in ((0, before + z1 + z2), (1, z0 + z1 + after)):
            total = total + bias
            hidden = total * (0.5 + 0.5 * jnp.tanh(0.5 * total))
            if r6 == 0:
                hidden = jnp.where(s > 0, hidden, 0.0)
            elif r6 == 5:
                hidden = jnp.where(s < N_SLAB - 1, hidden, 0.0)
            else:
                gate[pc * WL:(pc + 1) * WL, (r6 - 1) * C:r6 * C] = total
            hbuf[pc * WL:(pc + 1) * WL, r6 * C:(r6 + 1) * C] = hidden.astype(BF16)

    lat_load.wait()
    w_load.wait()

    taps[...] = dot_nn(lat4[1:3].reshape(2 * WL, C), wl[...])

    def part(row, a, b):
        t = 3 * a + b
        return taps[(row - 1) * WL:row * WL, t * C:(t + 1) * C]

    def own_terms(r6, b):
        rows = [(lat_row(r6, a), a) for a in range(3)]
        return sum(part(row, a, b) for row, a in rows if row in (1, 2))

    for r6 in (2, 3):
        activate(r6, *[own_terms(r6, b) for b in range(3)])

    guard(s < N_SLAB - 1, up.wait_recv)
    guard(s > 0, down.wait_recv)
    flood_wait(0)
    flood(1)
    for near, far, edge, start in ((1, 0, 0, 0), (4, 5, 3, 3)):
        halo_z = dot_nn(lat4[edge], wl[:, start * C:(start + 6) * C])
        inner = [halo_z[:, (b if near == 1 else b + 3) * C:][:, 0:C] for b in range(3)]
        outer = [halo_z[:, (b + 3 if near == 1 else b) * C:][:, 0:C] for b in range(3)]
        activate(near, *[own_terms(near, b) + inner[b] for b in range(3)])
        activate(far, *[own_terms(far, b) + (inner[b] + outer[b]) for b in range(3)])

    res = dot_nt(wd32[...].astype(BF16), hbuf[...])
    even, odd = res[:, 0:WL], res[:, WL:2 * WL]
    left = iota((16, WL), 1) == 0
    right = iota((16, WL), 1) == WL - 1
    dec_even = jnp.where(left, 0.0, pltpu.roll(odd[0:16], 1, 1)) + even[16:32] + odd[32:48]
    dec_odd = even[0:16] + odd[16:32] + jnp.where(right, 0.0, pltpu.roll(even[32:48], WL - 1, 1))
    decoded = jnp.concatenate([dec_even, dec_odd], axis=1).astype(BF16)
    dec[...] = decoded
    dall[jnp.where(low_half, q + 4, q)] = decoded

    @pl.when((q == 0) & (p > 0))
    def told():
        pl.semaphore_wait(flood_sem.at[4], 1)

    def gather_send(n, cond, target, slot):
        send(cond, dec, dall.at[slot], gat_ss.at[n], gat_rs.at[slot], f, target)

    gather_send(5, (q == 0) & (p > 0), 4 * p - 4, 8)
    gather_send(6, (q == 0) & (p > 0), 4 * p - 3, 8)
    gather_send(7, (q == 0) & (p > 0), 4 * p - 2, 4)
    for d in range(1, 4):
        qd = (q + d) % 4
        gather_send(d - 1, None, 4 * p + qd, jnp.where(qd < 2, q + 4, q))
    gather_send(3, p < GROUPS - 1, 4 * p + 4, q)
    gather_send(4, p > 0, 4 * p - 1, q + 4)
    gather_send(8, (q == 0) & (p > 1), 4 * p - 5, 8)

    rk = iota((128, 1), 0)
    g = rk & 63
    colour = one(g >= 14) + one(g >= 28)
    ig = jnp.where(rk < 64, p, p2) * PATCH + g - 14 * colour
    valid = (g < 42) & (ig >= 0) & (ig < IMG)
    table_load.wait()
    table = table_ref[...].astype(F32)
    cols = iota((128, IMG), 1)
    lo = jnp.sum(jnp.where(cols == ig, table, 0.0), axis=1, keepdims=True)
    nxt = jnp.sum(jnp.where(cols == ig + 1, table, 0.0), axis=1, keepdims=True)
    nxt = nxt + jnp.where(ig == IMG - 1, 256.0, 0.0)
    hi = jnp.maximum(nxt, lo + 1.0)
    inv = 1.0 / (hi - lo)
    lane = iota((128, 144), 1)
    row = (4 * jnp.where(rk < 64, 4 * p, base) + (lane >> 2)).astype(F32)
    inside = valid & ((lane & 3) == colour) & (row >= lo) & (row < hi)
    pick = jnp.where(inside, 1.0, 0.0).astype(BF16)
    lane = iota((128, 128), 1)
    row = (4 * s - 1 + (lane >> 2)).astype(F32)
    inside = valid & ((lane & 3) == colour) & (row >= lo) & (row < hi) & (lane < 24)
    both = jnp.where(lane == 32, inv, jnp.where(inside, 1.0, 0.0)).T
    back = both[0:32].astype(BF16)
    back = jnp.concatenate([back, back], axis=1)
    inv_row = both[32:33]

    pw_load.wait()
    prow = iota((KP, 588), 0)
    pg = prow & 63
    order = jnp.where(
        (pg < 42) & (iota((KP, 588), 1) == 14 * pg + 2 * (prow >> 7) + ((prow >> 6) & 1)), 1.0, 0.0
    ).astype(BF16)
    for n in range(CW // 256):
        cut = slice(n * 256, (n + 1) * 256)
        pwp[:, cut] = dot_nn(order, pw[:, cut]).astype(BF16)

    def gather_wait(slot, cond, source):
        copy = remote(dec, dall.at[slot], gat_ss.at[0], gat_rs.at[slot], f, source)
        pl.when(cond)(copy.wait_recv)

    more = p < GROUPS - 1
    for v in range(4):
        gather_wait(v, (q >= 2) & (q != v), 4 * p + v)
        gather_wait(v + 4, low_half & (q != v), 4 * p + v)
    gather_wait(4, (q >= 2) & more, 4 * p + 4)
    gather_wait(8, low_half & more, 4 * p + 4)
    lane16 = iota((16, 128), 1) < 64

    def patch_parts(crop, turned):
        turned[...] = jnp.concatenate([crop, jnp.zeros((64, 256), F32)], axis=0).T
        columns = []
        for c14 in range(14):
            pc, pj = patch_column(c14)
            columns.append(turned[pl.ds(pc * WL + pj, 16, stride=8), :])
        return [
            jnp.where(lane16, columns[2 * n], pltpu.roll(columns[2 * n + 1], 64, 1))
            for n in range(7)
        ]

    own_rows = dall[pl.ds(jnp.where(low_half, 4, 0), 5)].reshape(80, 256)
    own_parts = patch_parts(dot_nn(pick[0:64, 0:80], own_rows) * inv[0:64], ct)
    pos_load.wait()

    def embed(parts, rows):
        patches = jnp.concatenate(parts, axis=1)
        emb = dot_nn(jnp.concatenate(split2(patches), axis=0), pwp[...])
        emb = emb[0:16] + emb[16:32] + pos[rows, :].astype(F32)
        centred = emb - jnp.mean(emb, axis=1, keepdims=True)
        sigma = jnp.sqrt(jnp.mean(centred * centred, axis=1, keepdims=True) + EPS)
        normed = centred / sigma
        ybuf[rows, :] = normed
        return normed, sigma

    normed, sigma0 = embed(own_parts, slice(0, 16))
    gsum = jnp.sum(normed, axis=0, keepdims=True)
    psend[...] = gsum
    precv[p] = gsum

    flood_wait(1)
    steps = [(dx, dz) for dx in range(4) for dz in range(4) if dx or dz]
    steps.sort(key=lambda d: -min(d[0], 4 - d[0]) - 2 * min(d[1], 4 - d[1]))
    for dx, dz in steps:
        other = ((x + dx) % 4) * 4 + (z // 2 + dz) % 4
        send_part(None, psend, precv.at[p], pool_ss.at[0], pool_rs.at[0], f, 4 * other + q)

    for v in range(4):
        gather_wait(v, (q == 0) & (p > 0), 4 * p - 4 + v)
        if v > 0:
            gather_wait(v + 4, (q == 3) & more, 4 * p + 4 + v)
    gather_wait(8, (q == 3) & (p < GROUPS - 2), 4 * p + 8)
    next_crop = dot_nn(pick[64:128], dall[...].reshape(144, 256)) * inv[64:128]
    sigma1 = embed(patch_parts(next_crop, ct2), slice(16, 32))[1]
    sigma = jnp.concatenate([sigma0, sigma1], axis=0)

    for n in range(4):
        cut = slice(n * C, (n + 1) * C)
        total = gate[:, cut]
        sig = 0.5 + 0.5 * jnp.tanh(0.5 * total)
        gate[:, cut] = sig * (1.0 + total * (1.0 - sig))
    for n in range(4):
        latt[:, n * WL:(n + 1) * WL] = lat4[n].astype(F32).T.astype(BF16)
    proj_load.wait()
    for n in range(CW // 256):
        cut = slice(n * 256, (n + 1) * 256)
        projt[:, cut] = proj[cut, :].astype(F32).T.astype(BF16)
    for n in range(KP // 128):
        cut = slice(n * 128, (n + 1) * 128)
        pwpt[:, cut] = pwp[cut, :].astype(F32).T.astype(BF16)
    text_load.wait()
    text = text_ref[...]
    text2 = jnp.sum(text * text, axis=1, keepdims=True) + 1e-06
    gt[...] = jnp.zeros_like(gt)

    all_of(precv.at[pl.ds(0, GROUPS - 1)], pool_ss.at[0], pool_rs.at[0])
    pooled = precv[0]
    for n in range(1, GROUPS):
        pooled = pooled + precv[n]
    pooled = pooled * (1.0 / 256.0)


    def two_rows(v):
        top = iota((16, v.shape[1]), 0)
        hi_part = v.astype(BF16).astype(F32)
        return jnp.where(top == 0, hi_part, jnp.where(top == 1, v - hi_part, 0.0)).astype(BF16)

    pc_ = pooled - jnp.mean(pooled, axis=1, keepdims=True)
    psigma = jnp.sqrt(jnp.mean(pc_ * pc_, axis=1, keepdims=True) + EPS)
    unit = pc_ / psigma
    projected = jnp.sum(dot_nn(two_rows(unit), proj[...]), axis=0, keepdims=True)
    numer = jnp.sum(projected * text, axis=1, keepdims=True)
    norm2 = jnp.sum(projected * projected, axis=1, keepdims=True) + 1e-06
    scale = 1.0 / jnp.sqrt(norm2 * text2)
    reward = numer * scale
    reward_ref[...] = reward
    dproj = -LOSS_SCALE * (text * scale - projected * (reward / norm2))
    dunit = jnp.sum(dot_nn(two_rows(dproj), projt[...]), axis=0, keepdims=True)

    def norm_back(dy, y, sg):
        m1 = jnp.mean(dy, axis=1, keepdims=True)
        m2 = jnp.mean(dy * y, axis=1, keepdims=True)
        return (dy - m1 - y * m2) / sg

    dpooled = norm_back(dunit, unit, psigma) * (1.0 / 256.0)
    demb = norm_back(dpooled, ybuf[...], sigma)
    dpat = dot_nn(jnp.concatenate(split2(demb), axis=0), pwpt[...])
    dpat = dpat[0:32] + dpat[32:64]
    for n in range(7):
        d0 = dpat[0:16, n * 128:(n + 1) * 128]
        d1 = dpat[16:32, n * 128:(n + 1) * 128]
        pair = (
            jnp.where(lane16, d0, pltpu.roll(d1, 64, 1)),
            jnp.where(lane16, pltpu.roll(d0, 64, 1), d1),
        )
        for half in range(2):
            pc, pj = patch_column(2 * n + half)
            gt[pl.ds(pc * WL + pj, 16, stride=8), :] = pair[half]

    grows = jnp.concatenate(split2(gt[...] * inv_row), axis=1)
    image = dot_nt(back, grows).astype(BF16).astype(F32)
    even, odd = image[:, 0:WL], image[:, WL:2 * WL]
    left = iota((32, WL), 1) == 0
    right = iota((32, WL), 1) == WL - 1
    odd_before = jnp.where(left, 0.0, pltpu.roll(odd, 1, 1))
    even_after = jnp.where(right, 0.0, pltpu.roll(even, WL - 1, 1))
    igs[0] = jnp.concatenate([odd, even_after], axis=1)
    igs[1] = image
    igs[2] = jnp.concatenate([odd_before, even], axis=1)

    ims = []
    go = jnp.zeros((48, C), F32)
    for r in range(4):
        im = jnp.concatenate([igs[b, 4 * r:4 * r + 16, :] for b in range(3)], axis=0).astype(BF16)
        ims.append(im)
        go = go + dot_nn(im, hbuf[:, (r + 1) * C:(r + 2) * C])
    for half in range(2):
        go2[half, 27:32, :] = jnp.zeros((5, 128), F32)
        for t in range(9):
            at = (t % 3) * 16 + (2 - t // 3) * 4
            go2[half, 3 * t:3 * t + 3, :] = go[at:at + 3, half * 128:(half + 1) * 128]
    fc = y_hi * 2 + 1 - core
    outk = send(None, go2.at[1 - core], gocr, c_ss.at[3], c_rs.at[3], fc, s)

    wout = wo32[...].astype(BF16)
    cols_of = []
    for r in range(4):
        cg = dot_tn(ims[r], wout) * gate[:, r * C:(r + 1) * C]
        ev, od = cg[0:WL], cg[WL:2 * WL]
        od_before = jnp.where(first, 0.0, pltpu.roll(od, 1, 0))
        ev_after = jnp.where(last, 0.0, pltpu.roll(ev, WL - 1, 0))
        cols_of.append((od + ev_after, ev + od, od_before + ev))

    def put_grad(a, b, value):
        at = (3 * a + b) * C
        left, right = value[:, 0:128], value[:, 128:256]
        g32[at:at + C, :] = jnp.where(core == 0, left, right)
        gbf[at:at + C, :] = jnp.where(core == 0, right, left).astype(BF16)

    outer = [
        jnp.concatenate([cols_of[0][b], cols_of[1][b] + cols_of[2][b], cols_of[3][b]], axis=0)
        .astype(BF16) for b in range(3)
    ]
    inner = [
        jnp.concatenate([cols_of[0][b] + cols_of[1][b], cols_of[2][b] + cols_of[3][b]], axis=0)
        .astype(BF16) for b in range(3)
    ]
    outk.wait_recv()
    gsum_z = go2[core] + gocr[...]
    goz[...] = gsum_z.astype(BF16)
    for d in range(1, 8):
        zd = (z + d) % 8
        send_part(None, goz, gozr.at[z], z_ss.at[0], z_rs.at[0], f, x * 16 + zd * 2 + y_lo)

    main = []
    outer = jnp.concatenate(outer, axis=1)
    inner = jnp.concatenate(inner, axis=1)
    for a, start, stop, terms in ((0, 0, 3, outer), (1, 1, 3, inner), (2, 1, 4, outer)):
        value = dot_nn(latt[:, start * WL:stop * WL], terms)
        for b in range(3):
            put_grad(a, b, value[:, b * C:(b + 1) * C])
        rows = pl.ds(a * 768, 768)
        main.append(
            send(None, gbf.at[rows], gcr.at[rows], c_ss.at[a], c_rs.at[a], fc, s)
        )

    mine = jnp.where(core == 0, x, y)

    def quarter_device(n):
        fd = jnp.where(core == 0, f, (n // 2) * 2 + 1)
        sd = jnp.where(core == 0, n * 16 + z * 2 + y_lo, x * 16 + z * 2 + n % 2)
        return fd, sd

    def halves_sum(start, count):
        return g32[start:start + count, :] + gcr[start:start + count, :].astype(F32)

    for w in range(4):
        for part in range(2):
            if w == 0 and part == 0:
                main[0].wait_recv()
                main[1].wait_recv()
            elif w == 0:
                main[2].wait_recv()

            @pl.when(core == 0)
            def along_x():
                for n in (2 * part, 2 * part + 1):
                    total = jnp.concatenate(
                        [halves_sum(n * 576 + zd * 72, 72) for zd in (w, w + 4)], axis=0
                    )
                    x32[n, w] = total
                    xbf[n, w] = total.astype(BF16)

            @pl.when(core == 1)
            def along_y():
                units = [
                    halves_sum((2 * part + h) * 576 + zd * 72, 72)
                    for zd in (w, w + 4) for h in range(2)
                ]
                for n in range(2):
                    total = jnp.concatenate([u[36 * n:36 * n + 36] for u in units], axis=0)
                    x32[2 * part + n, w] = total
                    xbf[2 * part + n, w] = total.astype(BF16)

            for n in (2 * part, 2 * part + 1):
                send_part(
                    mine != n, xbf.at[n, w], xr.at[w, mine], u_ss.at[w], u_rs.at[w],
                    *quarter_device(n),
                )

    for w in range(4):
        xr[w, mine] = jnp.zeros((144, 128), BF16)
    zr[z] = jnp.zeros((80, 128), BF16)
    for w in range(4):
        all_of(xr.at[w, pl.ds(0, 3)], u_ss.at[w], u_rs.at[w])
        for k in range(2):
            zd = w + 4 * k
            cut = slice(k * 72, (k + 1) * 72)
            total = x32[mine, w, cut, :]
            for n in range(4):
                total = total + xr[w, n, cut, :].astype(F32)
            z32[zd] = total
            zbf[zd] = jnp.concatenate([total, jnp.zeros((8, 128), F32)], axis=0).astype(BF16)
            send_part(
                z != zd, zbf.at[zd], zr.at[z], z_ss.at[1], z_rs.at[1], f, x * 16 + zd * 2 + y_lo
            )
        if w == 1:
            gozr[z] = jnp.zeros((32, 128), BF16)
            all_of(gozr.at[pl.ds(0, 7)], z_ss.at[0], z_rs.at[0])
            gsum_x = gsum_z + jnp.sum(gozr[...].astype(F32), axis=0)
            gox[...] = gsum_x
            for d in range(1, 4):
                xd = (x + d) % 4
                send_part(
                    None, gox, goxr.at[x], x_ss.at[0], x_rs.at[0], f, xd * 16 + z * 2 + y_lo
                )

    goxr[x] = gsum_x
    all_of(goxr.at[pl.ds(0, 3)], x_ss.at[0], x_rs.at[0])
    gsum_y = jnp.sum(goxr[...], axis=0)
    goy[...] = gsum_y
    for d in range(1, 8):
        yd = (yc + d) % 8
        send_part(None, goy, goyr.at[yc], y_ss.at[0], y_rs.at[0], *yc_device(yd))
    goyr[yc] = gsum_y

    all_of(zr.at[pl.ds(0, 7)], z_ss.at[1], z_rs.at[1])
    total = z32[z]
    for n in range(8):
        total = total + zr[n, 0:72, :].astype(F32)

    for n in range(2):
        yb[n, 0:36, :] = total[36 * n:36 * n + 36]
        yb[n, 36:40, :] = jnp.zeros((4, 128), F32)
    slot = jnp.where(core == 0, y, 4 + x)
    for n in range(2):
        sd = jnp.where(core == 0, x * 16 + z * 2 + n, (2 * y_hi + n) * 16 + z * 2 + y_lo)
        here = sd == s

        @pl.when(here)
        def keep():
            yr[slot] = yb[n]

        for j in range(4):
            send_part(
                jnp.logical_not(here & (f == j)), yb.at[n], yr.at[slot],
                y_ss.at[1], y_rs.at[1], j, sd,
            )

    all_of(goyr.at[pl.ds(0, 7)], y_ss.at[0], y_rs.at[0])
    for half in range(2):
        total = (goyr[half] + goyr[2 + half]) + (goyr[4 + half] + goyr[6 + half])
        for t in range(9):
            gout_ref[:, t * C + half * 128:t * C + (half + 1) * 128] = total[3 * t:3 * t + 3]
    seven = (core == 0) | (x // 2 == y_hi)
    all_of(yr.at[pl.ds(0, 7)], y_ss.at[1], y_rs.at[1], seven)
    all_of(yr, y_ss.at[1], y_rs.at[1], jnp.logical_not(seven))
    for half in range(2):
        total = (yr[4 * half] + yr[4 * half + 1]) + (yr[4 * half + 2] + yr[4 * half + 3])
        gconv_ref[:, half * 128:(half + 1) * 128] = total[0:36]

    for cond, copy in sends:
        guard(cond, copy.wait_send)


def per_device(latents, conv_weight, conv_bias, out_weight, row_table, patch_weight, pos_embed,
               proj_weight, text_embed):
    vmem = pl.BlockSpec(memory_space=pltpu.VMEM)
    hbm = pl.BlockSpec(memory_space=pltpu.HBM)
    V = pltpu.VMEM
    dma = pltpu.SemaphoreType.DMA
    reward, gconv, gout = pl.pallas_call(
        kernel,
        out_shape=(
            jax.ShapeDtypeStruct((1, 1), F32),
            jax.ShapeDtypeStruct((36, C), F32),
            jax.ShapeDtypeStruct((3, 9 * C), F32),
        ),
        in_specs=[hbm] * 9,
        out_specs=(vmem, vmem, vmem),
        scratch_shapes=[
            V((1, C), F32), V((3, 9 * C), BF16), V((1, IMG), jnp.int32), V((1, EMB), F32),
            V((4, WL, C), BF16),
            V((C, 9 * C), BF16),
            V((2 * WL, 9 * C), F32),
            V((2 * WL, 6 * C), BF16),
            V((2 * WL, 4 * C), F32),
            V((48, 6 * C), F32),
            V((48, C), F32),
            V((588, CW), BF16),
            V((KP, CW), BF16),
            V((CW, KP), BF16),
            V((32, CW), BF16),
            V((CW, EMB), BF16),
            V((EMB, CW), BF16),
            V((16, 256), BF16),
            V((9, 16, 256), BF16),
            V((256, 128), F32),
            V((256, 128), F32),
            V((256, 128), F32),
            V((32, CW), F32),
            V((1, CW), F32),
            V((GROUPS, 1, CW), F32),
            V((3, 32, 256), F32),
            V((C, 4 * WL), BF16),
            V((9 * C, 128), F32),
            V((9 * C, 128), BF16),
            V((9 * C, 128), BF16),
            V((4, 4, 144, 128), BF16),
            V((4, 4, 144, 128), F32),
            V((4, 4, 144, 128), BF16),
            V((8, 80, 128), BF16),
            V((8, 72, 128), F32),
            V((8, 80, 128), BF16),
            V((2, 40, 128), F32),
            V((8, 40, 128), F32),
            V((2, 32, 128), F32),
            V((32, 128), F32),
            V((32, 128), BF16),
            V((8, 32, 128), BF16),
            V((32, 128), F32),
            V((4, 32, 128), F32),
            V((32, 128), F32),
            V((8, 32, 128), F32),
            dma((9,)), dma((2,)), dma((2,)), dma((9,)), dma((9,)), dma((1,)), dma((1,)),
            dma((4,)), dma((4,)), dma((4,)), dma((4,)), dma((1,)), dma((1,)),
            dma((2,)), dma((2,)), dma((2,)), dma((2,)), pltpu.SemaphoreType.REGULAR((5,)),
        ],
        compiler_params=pltpu.CompilerParams(
            collective_id=0, has_side_effects=True, vmem_limit_bytes=48 * 1024 * 1024
        ),
    )(*[
        pltpu.with_memory_space_constraint(v, pltpu.HBM) for v in (
            latents, conv_weight, conv_bias.reshape(1, C), out_weight, row_table, patch_weight,
            pos_embed, proj_weight, text_embed.reshape(1, EMB),
        )
    ])
    return reward.reshape(1), gconv, gout


def solution(mesh):
    return jax.shard_map(
        per_device,
        mesh=mesh,
        in_specs=(
            P("frame", "slab", None, None), P(), P(), P(), P("frame", None), P(), P(), P(), P(),
        ),
        out_specs=(P("frame"), P("slab", None), P()),
        check_vma=False,
    )
```
